128 devices in a mesh: ang: 16 (over x, y), sp: 8 (over z, core).
Axes of the slice: x: 4, y: 4, z: 4, core: 2. Of those that a mesh axis runs over, the one named last changes fastest.
Arguments:
- inputs: bfloat16 [16, 16, 4, 64, 192], P('ang', None, None, 'sp'), may hold values from -6 to 6
- cotangent: bfloat16 [16, 16, 4, 64, 192], P('ang', None, None, 'sp'), may hold values from -6 to 6
- kernel: bfloat16 [3, 3, 3, 3, 192, 192], replicated, may hold values from -0.046875 to 0.046875
- moment_one: float32 [2985984], P(('ang', 'sp')), may hold values from -3 to 3
- moment_two: float32 [2985984], P(('ang', 'sp')), may hold values from 0.05 to 1
Outputs:
- grad_input: bfloat16 [16, 16, 4, 64, 192], P('ang', None, None, 'sp')
- moment_next: float32 [2985984], P(('ang', 'sp'))
- square_next: float32 [2985984], P(('ang', 'sp'))
- direction: float32 [2985984], P(('ang', 'sp'))
The draws below stay inside these ranges and needn't reach their ends.
All inputs are finite; a program needn't handle non-finite values.
Results may differ from the reference program's by a relative error of at most 0.0049.
Values may be sent and summed in bfloat16 or wider, within the bound.
A program may use at most 128 MiB of HBM per device.

```python
import math
import jax
import jax.numpy as jnp
from jax import lax

C = 192
V = 16
S = 4
U = 16
TW = 64
KSIZE = 2985984


def steps_of(rng, extent, cuts, least, largest):
    loudness, own = 1.0, jax.random.fold_in(rng, 6)
    for dim, shards_of in cuts:
        heights = jnp.exp(jax.random.uniform(jax.random.fold_in(own, dim), (shards_of,), jnp.float32, least / len(cuts), largest / len(cuts)))
        loudness = loudness * jnp.repeat(heights, extent[dim] // shards_of).reshape([-1 if axis == dim else 1 for axis in range(len(extent))])
    return loudness


def normal_values(own_key, extent, spread, most, split=(), held_as=jnp.bfloat16):
    values = jax.random.normal(own_key, extent, jnp.float32) * spread
    if len(split) > 0:
        values = steps_of(own_key, extent, split, -0.22, 0.18) * values
    return jnp.clip(values, min=-most, max=most).astype(held_as)


def setup_inputs(seed: int = 0) -> dict:
    key_of = jax.random.split(jax.random.key(seed), 6)
    return {
        "inputs": normal_values(key_of[0], (U, V, S, TW, C), 1.0, 6.0, ((0, 16), (3, 8))),
        "cotangent": normal_values(key_of[1], (U, V, S, TW, C), 1.0, 6.0, ((0, 16), (3, 8))),
        "kernel": normal_values(key_of[2], (3, 3, 3, 3, C, C), (81 * C) ** -0.5, 0.046875),
        "moment_one": normal_values(key_of[3], (KSIZE,), 0.5, 3.0, ((0, 128),), jnp.float32),
        "moment_two": jnp.clip(jnp.exp(math.log(1.0) - 2.9957323 * jax.random.uniform(key_of[4], (KSIZE,), jnp.float32) ** steps_of(key_of[4], (KSIZE,), ((0, 128),), -0.2, 0.2)), 0.05, 1.0),
    }


beta_one = 0.9
beta_two = 0.999
adam_step = 100
epsilon = 1e-08

def tap_columns(block, tap_shift):
    row_count = block.shape[0] - 2
    view_count = block.shape[1] - 2
    line_count = block.shape[2] - 2
    col_count = block.shape[3] - 2
    pieces = []
    for off_view in range(3):
        for off_row in range(3):
            for off_col in range(3):
                pieces.append(block[tap_shift:tap_shift + row_count, off_view:off_view + view_count, off_row:off_row + line_count, off_col:off_col + col_count])
    stacked = jnp.concatenate(pieces, axis=-1)
    return stacked.reshape(-1, stacked.shape[-1])

def correlate(block, kernel_taps):
    running = jnp.zeros((1, 1), jnp.float32)
    for tap_shift in range(3):
        running = running + jnp.dot(tap_columns(block, tap_shift), kernel_taps[tap_shift], preferred_element_type=jnp.float32)
    return running

def pad_field(field):
    return jnp.pad(field, ((1, 1), (1, 1), (1, 1), (1, 1), (0, 0)))

def reference(inputs, cotangent, kernel, moment_one, moment_two):
    channels = inputs.shape[-1]
    kernel_taps = kernel.reshape(3, 27 * channels, channels)
    flipped_taps = jnp.swapaxes(kernel[::-1, ::-1, ::-1, ::-1], 4, 5).reshape(3, 27 * channels, channels)
    padded_input = pad_field(inputs)
    row_total = inputs.shape[0]

    def forward_row(row_index):
        block = lax.dynamic_slice_in_dim(padded_input, row_index, 3, 0)
        preact = correlate(block, kernel_taps)
        upstream = lax.dynamic_index_in_dim(cotangent, row_index, 0, keepdims=False).reshape(-1, channels).astype(jnp.float32)
        sigmoid_pre = jax.nn.sigmoid(preact)
        return (upstream * sigmoid_pre * (1.0 + preact * (1.0 - sigmoid_pre))).astype(jnp.bfloat16)
    row_ids = jnp.arange(row_total, dtype=jnp.int32)
    grad_rows = lax.map(forward_row, row_ids)
    grad_pre = grad_rows.reshape(inputs.shape)
    padded_grad = pad_field(grad_pre)

    def backward_row(row_index):
        block = lax.dynamic_slice_in_dim(padded_grad, row_index, 3, 0)
        return correlate(block, flipped_taps).astype(jnp.bfloat16)
    grad_input = lax.map(backward_row, row_ids).reshape(inputs.shape)

    def kernel_row(running, packed):
        row_index, grad_row = packed
        block = lax.dynamic_slice_in_dim(padded_input, row_index, 3, 0)
        parts = []
        for tap_shift in range(3):
            parts.append(lax.dot_general(tap_columns(block, tap_shift), grad_row, (((0,), (0,)), ((), ())), preferred_element_type=jnp.float32))
        return (running + jnp.stack(parts), None)
    start = jnp.zeros((3, 27 * channels, channels), jnp.float32)
    summed, _ = lax.scan(kernel_row, start, (row_ids, grad_rows))
    pixels = inputs.size // channels
    grad_kernel = summed.reshape(-1) * jnp.float32(1.0 / math.sqrt(pixels))
    moment_next = beta_one * moment_one + (1.0 - beta_one) * grad_kernel
    square_next = beta_two * moment_two + (1.0 - beta_two) * grad_kernel * grad_kernel
    first_fix = 1.0 - beta_one ** adam_step
    second_fix = 1.0 - beta_two ** adam_step
    direction = moment_next / first_fix / (jnp.sqrt(square_next / second_fix) + epsilon)
    return (grad_input, moment_next, square_next, direction)
```

```python
import functools
import math

import jax
import jax.numpy as jnp
from jax import lax
from jax.experimental import pallas as pl
from jax.experimental.pallas import tpu as pltpu
from jax.sharding import PartitionSpec as P

beta_one = 0.9
beta_two = 0.999
adam_step = 100
epsilon = 1e-08

MESH = pl.DeviceIdType.MESH
F32 = jnp.float32
BF16 = jnp.bfloat16

V, S, T, C = 16, 4, 8, 192
CELLS = V * S * T
GROUP = 9 * C
WIDE = GROUP + 64
ROWS = 9 * GROUP
LANES = 256
SIDES = ((0, 1), (0, -1), (1, 0), (-1, 0), (1, 1), (1, -1), (-1, 1), (-1, -1))


def start_halo(field, send, recv):
    rows, cols = lax.axis_size("ang"), lax.axis_size("sp")
    row, col = lax.axis_index("ang"), lax.axis_index("sp")
    jobs = []
    for side, (da, ds) in enumerate(SIDES):
        if ds == 0:
            src, dst = pl.ds(1, T), pl.ds(1, T)
        elif ds == 1:
            src, dst = pl.ds(T, 1), pl.ds(0, 1)
        else:
            src, dst = pl.ds(1, 1), pl.ds(T + 1, 1)
        sent = (row + da >= 0) & (row + da < rows) & (col + ds >= 0) & (col + ds < cols)
        got = (row - da >= 0) & (row - da < rows) & (col - ds >= 0) & (col - ds < cols)
        copy = pltpu.make_async_remote_copy(
            src_ref=field.at[1, pl.ds(1, S), src],
            dst_ref=field.at[1 - da, pl.ds(1, S), dst],
            send_sem=send.at[side],
            recv_sem=recv.at[side],
            device_id=(row + da, col + ds),
            device_id_type=MESH,
        )
        pl.when(sent)(copy.start)
        jobs.append((copy, sent, got))
    return jobs


def enter_halo():
    rows, cols = lax.axis_size("ang"), lax.axis_size("sp")
    row, col = lax.axis_index("ang"), lax.axis_index("sp")
    barrier = pltpu.get_barrier_semaphore()
    for da, ds in SIDES:
        there = (row + da >= 0) & (row + da < rows) & (col + ds >= 0) & (col + ds < cols)

        @pl.when(there)
        def _():
            pl.semaphore_signal(
                barrier, inc=1, device_id=(row + da, col + ds), device_id_type=MESH
            )

    tall = 1 + (row > 0).astype(jnp.int32) + (row < rows - 1).astype(jnp.int32)
    broad = 1 + (col > 0).astype(jnp.int32) + (col < cols - 1).astype(jnp.int32)
    pl.semaphore_wait(barrier, tall * broad - 1)


def unfold(field, taps, view_row):
    @pl.loop(0, S)
    def _(s):
        def low(k):
            block = field[view_row, s + k // 3, pl.ds(k % 3, T)]
            return block.reshape(T * V, LANES)

        out = pl.ds(pl.multiple_of(s * T * V, T * V), T * V)
        for pair in range(4):
            first = low(2 * pair)
            second = pltpu.roll(low(2 * pair + 1), 64, 1)
            at = 384 * pair
            taps[out, at : at + 128] = first[:, :128]
            taps[out, at + 128 : at + 256] = first[:, 128:] + second[:, :128]
            taps[out, at + 256 : at + 384] = second[:, 128:]
        taps[out, 1536:1792] = low(8)


def shifted(values, by):
    rows = values.shape[0]
    view = lax.broadcasted_iota(jnp.int32, values.shape, 0) % V
    keep = (view >= by) if by > 0 else (view < V + by)
    return jnp.where(keep, pltpu.roll(values, by % rows, 0), jnp.zeros_like(values))


def correlate(taps, weights, acc, view_row, first):
    @pl.loop(0, 3)
    def _(b):
        at = pl.multiple_of((view_row * 3 + b) * GROUP, 64)
        term = jnp.dot(taps[...], weights[pl.ds(at, WIDE), :], preferred_element_type=F32)
        if first:
            acc[b] = term
        else:
            acc[b] += term


def forward_kernel(x_ref, cot_ref, w_ref, dw_ref, gp_ref, xp, xc, wv, acc, gall, send, recv, wsem):
    rest = pl.ds(ROWS, WIDE - GROUP)
    wcopy = pltpu.make_async_copy(w_ref, wv.at[pl.ds(0, ROWS)], wsem)
    wcopy.start()
    wv[rest, :] = jnp.zeros((WIDE - GROUP, C), BF16)
    xp[...] = jnp.zeros_like(xp)
    gp_ref[...] = jnp.zeros_like(gp_ref)
    for s in range(S):
        block = jnp.swapaxes(x_ref[0, :, s].astype(F32), 0, 1).astype(BF16)
        xp[1, 1 + s, 1 : 1 + T, :, 0:C] = block
    enter_halo()
    jobs = start_halo(xp, send.at[0], recv.at[0])
    for copy, _, got in jobs:
        pl.when(got)(copy.wait_recv)
    wcopy.wait()
    for view_row in range(3):
        unfold(xp, xc.at[view_row], view_row)
    for view_row in (1, 0, 2):
        correlate(xc.at[view_row], wv, acc, view_row, view_row == 1)
    for copy, sent, _ in jobs:
        pl.when(sent)(copy.wait_send)

    preact = shifted(acc[0], 1) + acc[1] + shifted(acc[2], -1)
    for s in range(S):
        upstream = jnp.swapaxes(cot_ref[0, :, s].astype(F32), 0, 1).reshape(T * V, C)
        pre = preact[s * T * V : (s + 1) * T * V]
        sigmoid = jax.nn.sigmoid(pre)
        grad = upstream * sigmoid * (1.0 + pre * (1.0 - sigmoid))
        gp_ref[1, 1 + s, 1 : 1 + T, :, 0:C] = grad.astype(BF16).reshape(T, V, C)
    jobs = start_halo(gp_ref, send.at[1], recv.at[1])
    grad = gp_ref[1, 1 : 1 + S, 1 : 1 + T].reshape(CELLS, LANES)
    wide = grad.astype(F32)
    gall[:, 0:256] = shifted(wide, -1).astype(BF16)
    gall[:, 256:512] = grad
    gall[:, 512:768] = shifted(wide, 1).astype(BF16)

    for a in range(3):
        for part in range(5):
            at, size = 384 * part, (384 if part < 4 else 192)
            term = lax.dot_general(
                xc[a, :, at : at + (size if part < 4 else 256)],
                gall[...],
                (((0,), (0,)), ((), ())),
                preferred_element_type=F32,
            )
            for b in range(3):
                row = (3 * a + b) * GROUP + at
                dw_ref[row : row + size, :] = term[0:size, 256 * b : 256 * b + C].astype(BF16)

    for copy, sent, got in jobs:
        pl.when(sent)(copy.wait_send)
        pl.when(got)(copy.wait_recv)


def input_kernel(gp_ref, w_ref, out_ref, wv, wt, gc, acc, wsem):
    wcopy = pltpu.make_async_copy(w_ref, wv, wsem)
    wcopy.start()
    wt[pl.ds(ROWS, WIDE - GROUP), :] = jnp.zeros((WIDE - GROUP, C), BF16)
    wcopy.wait()

    @pl.loop(0, 81)
    def _(tap):
        src = pl.ds(pl.multiple_of((80 - tap) * C, 64), C)
        dst = pl.ds(pl.multiple_of(tap * C, 64), C)
        wt[dst, :] = wv[src, :].T

    for view_row in range(3):
        unfold(gp_ref, gc.at[view_row], view_row)
    for view_row in (1, 0, 2):
        correlate(gc.at[view_row], wt, acc, view_row, view_row == 1)
    total = shifted(acc[0], 1) + acc[1] + shifted(acc[2], -1)
    for s in range(S):
        block = total[s * T * V : (s + 1) * T * V].reshape(T, V, C)
        out_ref[0, :, s] = jnp.swapaxes(block, 0, 1).astype(BF16)


def local(inputs, cotangent, kernel, moment_one, moment_two):
    flat = kernel.reshape(ROWS, C)
    vmem = pl.BlockSpec(memory_space=pltpu.VMEM)
    anywhere = pl.BlockSpec(memory_space=pl.ANY)
    padded = (3, S + 2, T + 2, V, LANES)
    params = functools.partial(pltpu.CompilerParams, vmem_limit_bytes=56 * 1024 * 1024)
    terms, grads = pl.pallas_call(
        forward_kernel,
        out_shape=(
            jax.ShapeDtypeStruct((ROWS, C), BF16),
            jax.ShapeDtypeStruct(padded, BF16),
        ),
        in_specs=[vmem, vmem, anywhere],
        out_specs=(vmem, vmem),
        scratch_shapes=[
            pltpu.VMEM(padded, BF16),
            pltpu.VMEM((3, CELLS, WIDE), BF16),
            pltpu.VMEM((ROWS + WIDE - GROUP, C), BF16),
            pltpu.VMEM((3, CELLS, C), F32),
            pltpu.VMEM((CELLS, 768), BF16),
            pltpu.SemaphoreType.DMA((2, 8)),
            pltpu.SemaphoreType.DMA((2, 8)),
            pltpu.SemaphoreType.DMA,
        ],
        compiler_params=params(collective_id=0, has_side_effects=True),
        cost_estimate=pl.CostEstimate(flops=6 * 10**9, bytes_accessed=16 * 10**6, transcendentals=10**5),
    )(inputs, cotangent, flat)
    grad_input = pl.pallas_call(
        input_kernel,
        out_shape=jax.ShapeDtypeStruct(inputs.shape, BF16),
        in_specs=[vmem, anywhere],
        out_specs=vmem,
        scratch_shapes=[
            pltpu.VMEM((ROWS, C), BF16),
            pltpu.VMEM((ROWS + WIDE - GROUP, C), BF16),
            pltpu.VMEM((3, CELLS, WIDE), BF16),
            pltpu.VMEM((3, CELLS, C), F32),
            pltpu.SemaphoreType.DMA,
        ],
        compiler_params=params(),
        cost_estimate=pl.CostEstimate(flops=3 * 10**9, bytes_accessed=10**7, transcendentals=0),
    )(grads, flat)
    share = lax.psum_scatter(terms.reshape(-1), ("ang", "sp"), scatter_dimension=0, tiled=True)
    pixels = CELLS * lax.axis_size("ang") * lax.axis_size("sp")
    grad_share = share.astype(F32) * F32(1.0 / math.sqrt(pixels))
    moment_next = beta_one * moment_one + (1.0 - beta_one) * grad_share
    square_next = beta_two * moment_two + (1.0 - beta_two) * grad_share * grad_share
    first_fix = 1.0 - beta_one**adam_step
    second_fix = 1.0 - beta_two**adam_step
    direction = moment_next / first_fix / (jnp.sqrt(square_next / second_fix) + epsilon)
    return (grad_input, moment_next, square_next, direction)


def solution(mesh):
    field = P("ang", None, None, "sp", None)
    share = P(("ang", "sp"))
    return jax.shard_map(
        local,
        mesh=mesh,
        in_specs=(field, field, P(), share, share),
        out_specs=(field, share, share, share),
        check_vma=False,
    )
```

```python
import functools
import math

import jax
import jax.numpy as jnp
from jax import lax
from jax.experimental import pallas as pl
from jax.experimental.pallas import tpu as pltpu
from jax.sharding import PartitionSpec as P

beta_one = 0.9
beta_two = 0.999
adam_step = 100
epsilon = 1e-08

MESH = pl.DeviceIdType.MESH
F32 = jnp.float32
BF16 = jnp.bfloat16

V, S, T, C = 16, 4, 8, 192
CELLS = V * S * T
GROUP = 9 * C
WIDE = GROUP + 64
ROWS = 9 * GROUP
LANES = 256
SIDES = ((0, 1), (0, -1), (1, 0), (-1, 0), (1, 1), (1, -1), (-1, 1), (-1, -1))


def start_halo(field, send, recv):
    rows, cols = lax.axis_size("ang"), lax.axis_size("sp")
    row, col = lax.axis_index("ang"), lax.axis_index("sp")
    jobs = []
    for side, (da, ds) in enumerate(SIDES):
        if ds == 0:
            src, dst = pl.ds(1, T), pl.ds(1, T)
        elif ds == 1:
            src, dst = pl.ds(T, 1), pl.ds(0, 1)
        else:
            src, dst = pl.ds(1, 1), pl.ds(T + 1, 1)
        sent = (row + da >= 0) & (row + da < rows) & (col + ds >= 0) & (col + ds < cols)
        got = (row - da >= 0) & (row - da < rows) & (col - ds >= 0) & (col - ds < cols)
        copy = pltpu.make_async_remote_copy(
            src_ref=field.at[1, pl.ds(1, S), src],
            dst_ref=field.at[1 - da, pl.ds(1, S), dst],
            send_sem=send.at[side],
            recv_sem=recv.at[side],
            device_id=(row + da, col + ds),
            device_id_type=MESH,
        )
        pl.when(sent)(copy.start)
        jobs.append((copy, sent, got))
    return jobs


def enter():
    rows, cols = lax.axis_size("ang"), lax.axis_size("sp")
    row, col = lax.axis_index("ang"), lax.axis_index("sp")
    barrier = pltpu.get_barrier_semaphore()

    def greet(peer):
        pl.semaphore_signal(barrier, inc=1, device_id=peer, device_id_type=MESH)

    for da, ds in SIDES:
        there = (row + da >= 0) & (row + da < rows) & (col + ds >= 0) & (col + ds < cols)
        pl.when(there)(functools.partial(greet, (row + da, col + ds)))
    for axis in range(3):
        for step in range(1, 4):
            greet(peer_along(axis, step))
    greet(sibling())
    tall = 1 + (row > 0).astype(jnp.int32) + (row < rows - 1).astype(jnp.int32)
    broad = 1 + (col > 0).astype(jnp.int32) + (col < cols - 1).astype(jnp.int32)
    pl.semaphore_wait(barrier, tall * broad + 9)


def place():
    row, col = lax.axis_index("ang"), lax.axis_index("sp")
    return lax.div(row, 4), lax.rem(row, 4), lax.div(col, 2), lax.rem(col, 2)


def peer_along(axis, step):
    at = list(place())
    at[axis] = lax.rem(at[axis] + step, 4)
    return (at[0] * 4 + at[1], at[2] * 2 + at[3])


def sibling():
    x, y, z, core = place()
    return (x * 4 + y, z * 2 + 1 - core)


def unfold(field, taps, view_row):
    @pl.loop(0, S)
    def _(s):
        def low(k):
            block = field[view_row, s + k // 3, pl.ds(k % 3, T)]
            return block.reshape(T * V, LANES)

        out = pl.ds(pl.multiple_of(s * T * V, T * V), T * V)
        for pair in range(4):
            first = low(2 * pair)
            second = pltpu.roll(low(2 * pair + 1), 64, 1)
            at = 384 * pair
            taps[out, at : at + 128] = first[:, :128]
            taps[out, at + 128 : at + 256] = first[:, 128:] + second[:, :128]
            taps[out, at + 256 : at + 384] = second[:, 128:]
        taps[out, 1536:1792] = low(8)


def shifted(values, by):
    rows = values.shape[0]
    view = lax.broadcasted_iota(jnp.int32, values.shape, 0) % V
    keep = (view >= by) if by > 0 else (view < V + by)
    return jnp.where(keep, pltpu.roll(values, by % rows, 0), jnp.zeros_like(values))


def correlate(taps, weights, acc, view_row, first):
    @pl.loop(0, 3)
    def _(b):
        at = pl.multiple_of((view_row * 3 + b) * GROUP, 64)
        term = jnp.dot(taps[...], weights[pl.ds(at, WIDE), :], preferred_element_type=F32)
        if first:
            acc[b] = term
        else:
            acc[b] += term


UNITS = 243
TILE = (16, 128)
HALVES = (32, 36, 40)
HALVES_NEXT = (9, 10, 10)


def window(chips, index, count):
    start = (index * (chips * 243)) // 64
    if isinstance(index, int):
        return min(start, UNITS - count)
    return jnp.minimum(start, UNITS - count)


def kernel_terms(taps, grads, dw, a):
    for part in range(5):
        at, size = 384 * part, (384 if part < 4 else 192)
        term = lax.dot_general(
            taps[a, :, at : at + (size if part < 4 else 256)],
            grads[...],
            (((0,), (0,)), ((), ())),
            preferred_element_type=F32,
        )
        for b in range(3):
            count = size // 64
            block = term[0:size, 256 * b : 256 * b + 256].reshape(count, 2, 2, 16, 256)
            dst = pl.ds((3 * a + b) * 27 + 6 * part, count)
            for core in range(2):
                low, high = block[:, core, 0], block[:, core, 1]
                dw[core, 0, dst] = low[:, :, :128].astype(BF16)
                dw[core, 1, dst] = high[:, :, :128].astype(BF16)
                tail = pltpu.roll(high[:, :, 128:].reshape(count * 16, 128), 64, 1)
                dw[core, 2, dst] = (low[:, :, 128:] + tail.reshape(count, 16, 128)).astype(BF16)


def send_to(peer, src, dst, sems, index):
    copy = pltpu.make_async_remote_copy(
        src_ref=src,
        dst_ref=dst,
        send_sem=sems.at[0, index],
        recv_sem=sems.at[1, index],
        device_id=peer,
        device_id_type=MESH,
    )
    copy.start()
    return copy


class Ring:
    def __init__(self, axis, src, got, relay, sems):
        self.axis, self.src, self.got, self.relay, self.sems = axis, src, got, relay, sems
        self.me = place()[axis]
        self.up, self.across, self.down = (lax.rem(self.me + k, 4) for k in (1, 2, 3))

    def send(self, src, slot):
        peer = peer_along(self.axis, 1 if slot % 2 == 0 else 3)
        return send_to(peer, src, self.got.at[slot], self.sems, slot)

    def open(self):
        src = self.src
        self.jobs = [self.send(src.at[self.across, 1 - k], k) for k in range(2)]
        self.jobs.append(self.send(src.at[self.up, 0], 2))
        self.jobs.append(self.send(src.at[self.down, 1], 3))

    def pass_on(self):
        self.jobs[0].wait_recv()
        self.relay[0] = self.got[0] + self.src[self.up, 1]
        self.jobs.append(self.send(self.relay.at[0], 4))
        self.jobs[1].wait_recv()
        self.relay[1] = self.got[1] + self.src[self.down, 0]
        self.jobs.append(self.send(self.relay.at[1], 5))

    def close(self):
        for job in self.jobs[2:]:
            job.wait_recv()
        for job in self.jobs:
            job.wait_send()
        wide = lambda tile: tile.astype(F32)
        first = wide(self.src[self.me, 0]) + wide(self.got[2]) + wide(self.got[5])
        second = wide(self.src[self.me, 1]) + wide(self.got[3]) + wide(self.got[4])
        return first.astype(BF16), second.astype(BF16)


def step_kernel(
    x_ref, cot_ref, w_ref, gi_ref, gk_ref,
    xp, gp, xc, wv, wt, acc, gall, dw, pair,
    first_a, first_b, first_c, got_a, got_b, got_c, relay_a, relay_b, relay_c,
    sum_a, sum_b, sum_c,
    second_a, second_b, second_c, next_a, next_b, next_c, pass_a, pass_b, pass_c,
    last_a, last_b, last_c, ends, both,
    halo_send, halo_recv, wsem, pair_sems, ring_sems, next_sems, last_sems, core_sems,
):
    chip_x, chip_y, chip_z, core = place()
    wcopy = pltpu.make_async_copy(w_ref, wv.at[pl.ds(0, ROWS)], wsem)
    wcopy.start()
    xp[...] = jnp.zeros_like(xp)
    gp[...] = jnp.zeros_like(gp)
    for s in range(S):
        block = jnp.swapaxes(x_ref[0, :, s].astype(F32), 0, 1).astype(BF16)
        xp[1, 1 + s, 1 : 1 + T, :, 0:C] = block
    enter()
    jobs = start_halo(xp, halo_send.at[0], halo_recv.at[0])

    rest = pl.ds(ROWS, WIDE - GROUP)
    wv[rest, :] = jnp.zeros((WIDE - GROUP, C), BF16)
    wt[rest, :] = jnp.zeros((WIDE - GROUP, C), BF16)
    wcopy.wait()

    @pl.loop(0, 81)
    def _(tap):
        src = pl.ds(pl.multiple_of((80 - tap) * C, 64), C)
        dst = pl.ds(pl.multiple_of(tap * C, 64), C)
        wt[dst, :] = wv[src, :].T

    for copy, _, got in jobs:
        pl.when(got)(copy.wait_recv)
    for copy, sent, _ in jobs:
        pl.when(sent)(copy.wait_send)
    for view_row in range(3):
        unfold(xp, xc.at[view_row], view_row)
    for view_row in (1, 0, 2):
        correlate(xc.at[view_row], wv, acc, view_row, view_row == 1)

    preact = shifted(acc[0], 1) + acc[1] + shifted(acc[2], -1)
    for s in range(S):
        upstream = jnp.swapaxes(cot_ref[0, :, s].astype(F32), 0, 1).reshape(T * V, C)
        pre = preact[s * T * V : (s + 1) * T * V]
        sigmoid = jax.nn.sigmoid(pre)
        grad = upstream * sigmoid * (1.0 + pre * (1.0 - sigmoid))
        gp[1, 1 + s, 1 : 1 + T, :, 0:C] = grad.astype(BF16).reshape(T, V, C)
    jobs = start_halo(gp, halo_send.at[1], halo_recv.at[1])
    grad = gp[1, 1 : 1 + S, 1 : 1 + T].reshape(CELLS, LANES)
    wide = grad.astype(F32)
    gall[:, 0:256] = shifted(wide, -1).astype(BF16)
    gall[:, 256:512] = grad
    gall[:, 512:768] = shifted(wide, 1).astype(BF16)

    pairs = []
    for a in range(3):
        kernel_terms(xc, gall, dw, a)
        units = pl.ds(81 * a, 81)
        src, dst = dw.at[1 - core, :, units], pair.at[:, units]
        pairs.append(send_to(sibling(), src, dst, pair_sems, a))

    for copy, sent, got in jobs:
        pl.when(got)(copy.wait_recv)
    for copy, sent, got in jobs:
        pl.when(sent)(copy.wait_send)
    for view_row in range(3):
        unfold(gp, xc.at[view_row], view_row)
    for copy in pairs:
        copy.wait()

    def both_cores(plane, start, count):
        units = pl.ds(start, count)
        return dw[core, plane, units] + pair[plane, units]

    for x in range(4):
        for half in range(2):
            first_a[x, half] = both_cores(0, window(16, x, 64) + 32 * half, 32)

    @pl.loop(0, 16)
    def _(xy):
        x, y = xy // 4, xy % 4
        first_b[y, x // 2, pl.ds((x % 2) * 18, 18)] = both_cores(1, window(4, xy, 18), 18)

    @pl.loop(0, 64)
    def _(q):
        x, y, z = q // 16, (q // 4) % 4, q % 4
        to = ((x % 2) * 4 + y) * 5
        first_c[z, x // 2, pl.ds(to, 5)] = both_cores(2, window(1, q, 5), 5)

    rings = [
        Ring(0, first_a, got_a, relay_a, ring_sems.at[0]),
        Ring(1, first_b, got_b, relay_b, ring_sems.at[1]),
        Ring(2, first_c, got_c, relay_c, ring_sems.at[2]),
    ]
    for ring in rings:
        ring.open()
    correlate(xc.at[1], wt, acc, 1, True)
    correlate(xc.at[0], wt, acc, 0, False)
    for ring in rings:
        ring.pass_on()
    correlate(xc.at[2], wt, acc, 2, False)

    column = chip_x * 4 + chip_y
    chip = column * 4 + chip_z
    low, high = rings[0].close()
    sum_a[0:32] = low
    sum_a[32:64] = high
    for y in range(4):
        start = window(4, chip_x * 4 + y, 18) - window(16, chip_x, 64)
        for half in range(2):
            second_a[y, half] = sum_a[pl.ds(start + 9 * half, 9)]
    low, high = rings[1].close()
    sum_b[0:2] = low.reshape(2, 18, *TILE)
    sum_b[2:4] = high.reshape(2, 18, *TILE)
    for x in range(4):
        for z in range(4):
            start = window(1, x * 16 + chip_y * 4 + z, 5) - window(4, x * 4 + chip_y, 18)
            second_b[z, x // 2, 5 * (x % 2) : 5 * (x % 2) + 5] = sum_b[x, pl.ds(start, 5)]
    low, high = rings[2].close()
    second_c[0:2] = low.reshape(2, 2, 10, *TILE)
    second_c[2:4] = high.reshape(2, 2, 10, *TILE)

    rings = [
        Ring(1, second_a, next_a, pass_a, next_sems.at[0]),
        Ring(2, second_b, next_b, pass_b, next_sems.at[1]),
        Ring(0, second_c, next_c, pass_c, next_sems.at[2]),
    ]
    for ring in rings:
        ring.open()
    total = shifted(acc[0], 1) + acc[1] + shifted(acc[2], -1)
    for s in range(S):
        block = total[s * T * V : (s + 1) * T * V].reshape(T, V, C)
        gi_ref[0, :, s] = jnp.swapaxes(block, 0, 1).astype(BF16)
    for ring in rings:
        ring.pass_on()
    low, high = rings[0].close()
    last = []
    sum_a[0:9] = low
    sum_a[9:18] = high
    for z in range(4):
        start = window(1, column * 4 + z, 5) - window(4, column, 18)
        last_a[z] = sum_a[pl.ds(start, 5)]
    low, high = rings[1].close()
    last_b[0:2] = low.reshape(2, 5, *TILE)
    last_b[2:4] = high.reshape(2, 5, *TILE)
    low, high = rings[2].close()
    last_c[0:2] = low.reshape(2, 5, *TILE)
    last_c[2:4] = high.reshape(2, 5, *TILE)

    jobs = []
    for plane, (axis, src) in enumerate(((2, last_a), (0, last_b), (1, last_c))):
        for step in range(1, 4):
            target = lax.rem(place()[axis] + step, 4)
            slot = 3 * plane + step - 1
            jobs.append(send_to(peer_along(axis, step), src.at[target], ends.at[slot], last_sems, slot))
    for job in jobs:
        job.wait()
    for plane, (me, src) in enumerate(((chip_z, last_a), (chip_x, last_b), (chip_y, last_c))):
        total = src[me].astype(F32)
        for step in range(3):
            total += ends[3 * plane + step].astype(F32)
        both[core, plane] = total
    send_to(sibling(), both.at[core], both.at[core], core_sems, 0).wait()
    for k in range(2):
        gk_ref[:, k, 0, :, 0:128] = both[k, 0]
        gk_ref[:, k, 1, :, 0:128] = both[k, 1]
        tail = both[k, 2]
        gk_ref[:, k, 0, :, 128:192] = tail[:, :, 0:64]
        turned = pltpu.roll(tail.reshape(80, 128), 64, 1).reshape(5, 16, 128)
        gk_ref[:, k, 1, :, 128:192] = turned[:, :, 0:64]


def local(inputs, cotangent, kernel, moment_one, moment_two):
    vmem = pl.BlockSpec(memory_space=pltpu.VMEM)
    anywhere = pl.BlockSpec(memory_space=pl.ANY)
    padded = (3, S + 2, T + 2, V, LANES)
    tiles = lambda *lead: pltpu.VMEM((*lead, *TILE), BF16)
    dma = lambda *shape: pltpu.SemaphoreType.DMA(shape)
    long_kernel = pltpu.VMEM((ROWS + WIDE - GROUP, C), BF16)
    grad_input, window_grad = pl.pallas_call(
        step_kernel,
        out_shape=(
            jax.ShapeDtypeStruct(inputs.shape, BF16),
            jax.ShapeDtypeStruct((5, 2, 2, 16, C), F32),
        ),
        in_specs=[vmem, vmem, anywhere],
        out_specs=(vmem, vmem),
        scratch_shapes=[
            pltpu.VMEM(padded, BF16),
            pltpu.VMEM(padded, BF16),
            pltpu.VMEM((3, CELLS, WIDE), BF16),
            long_kernel,
            long_kernel,
            pltpu.VMEM((3, CELLS, C), F32),
            pltpu.VMEM((CELLS, 768), BF16),
            tiles(2, 3, UNITS),
            tiles(3, UNITS),
            *(tiles(4, 2, n) for n in HALVES),
            *(tiles(6, n) for n in HALVES),
            *(tiles(2, n) for n in HALVES),
            tiles(64),
            tiles(4, 18),
            tiles(4, 2, 10),
            *(tiles(4, 2, n) for n in HALVES_NEXT),
            *(tiles(6, n) for n in HALVES_NEXT),
            *(tiles(2, n) for n in HALVES_NEXT),
            *(tiles(4, 5) for _ in range(3)),
            tiles(9, 5),
            pltpu.VMEM((2, 3, 5, *TILE), F32),
            dma(2, 8),
            dma(2, 8),
            pltpu.SemaphoreType.DMA,
            dma(2, 3),
            dma(3, 2, 6),
            dma(3, 2, 6),
            dma(2, 9),
            dma(2, 1),
        ],
        compiler_params=pltpu.CompilerParams(
            vmem_limit_bytes=56 * 1024 * 1024, collective_id=0, has_side_effects=True
        ),
        cost_estimate=pl.CostEstimate(flops=9 * 10**9, bytes_accessed=10**7, transcendentals=10**5),
    )(inputs, cotangent, kernel.reshape(ROWS, C))
    share_len = moment_one.shape[0]
    chip = lax.axis_index("ang") * 4 + lax.axis_index("sp") // 2
    device = lax.axis_index(("ang", "sp"))
    begin = device * share_len - window(1, chip, 5) * (64 * C)
    share = lax.dynamic_slice_in_dim(window_grad.reshape(-1), begin, share_len, 0)
    pixels = CELLS * lax.axis_size("ang") * lax.axis_size("sp")
    grad_share = share * F32(1.0 / math.sqrt(pixels))
    moment_next = beta_one * moment_one + (1.0 - beta_one) * grad_share
    square_next = beta_two * moment_two + (1.0 - beta_two) * grad_share * grad_share
    first_fix = 1.0 - beta_one**adam_step
    second_fix = 1.0 - beta_two**adam_step
    direction = moment_next / first_fix / (jnp.sqrt(square_next / second_fix) + epsilon)
    return (grad_input, moment_next, square_next, direction)


def solution(mesh):
    field = P("ang", None, None, "sp", None)
    share = P(("ang", "sp"))
    return jax.shard_map(
        local,
        mesh=mesh,
        in_specs=(field, field, P(), share, share),
        out_specs=(field, share, share, share),
        check_vma=False,
    )
```

```python
import functools
import math

import jax
import jax.numpy as jnp
from jax import lax
from jax.experimental import pallas as pl
from jax.experimental.pallas import tpu as pltpu
from jax.sharding import PartitionSpec as P

beta_one = 0.9
beta_two = 0.999
adam_step = 100
epsilon = 1e-08

MESH = pl.DeviceIdType.MESH
F32 = jnp.float32
BF16 = jnp.bfloat16

V, S, T, C = 16, 4, 8, 192
CELLS = V * S * T
GROUP = 9 * C
WIDE = GROUP + 64
ROWS = 9 * GROUP
LANES = 256
SIDES = ((0, 1), (0, -1), (1, 0), (-1, 0), (1, 1), (1, -1), (-1, 1), (-1, -1))


def start_halo(field, send, recv):
    rows, cols = lax.axis_size("ang"), lax.axis_size("sp")
    row, col = lax.axis_index("ang"), lax.axis_index("sp")
    jobs = []
    for side, (da, ds) in enumerate(SIDES):
        if ds == 0:
            src, dst = pl.ds(1, T), pl.ds(1, T)
        elif ds == 1:
            src, dst = pl.ds(T, 1), pl.ds(0, 1)
        else:
            src, dst = pl.ds(1, 1), pl.ds(T + 1, 1)
        sent = (row + da >= 0) & (row + da < rows) & (col + ds >= 0) & (col + ds < cols)
        got = (row - da >= 0) & (row - da < rows) & (col - ds >= 0) & (col - ds < cols)
        copy = pltpu.make_async_remote_copy(
            src_ref=field.at[1, pl.ds(1, S), src],
            dst_ref=field.at[1 - da, pl.ds(1, S), dst],
            send_sem=send.at[side],
            recv_sem=recv.at[side],
            device_id=(row + da, col + ds),
            device_id_type=MESH,
        )
        pl.when(sent)(copy.start)
        jobs.append((copy, sent, got))
    return jobs


def greet():
    rows, cols = lax.axis_size("ang"), lax.axis_size("sp")
    row, col = lax.axis_index("ang"), lax.axis_index("sp")
    barrier = pltpu.get_barrier_semaphore()

    def signal(peer):
        pl.semaphore_signal(barrier, inc=1, device_id=peer, device_id_type=MESH)

    for da, ds in SIDES:
        there = (row + da >= 0) & (row + da < rows) & (col + ds >= 0) & (col + ds < cols)
        pl.when(there)(functools.partial(signal, (row + da, col + ds)))
    for axis in range(3):
        for step in range(1, 4):
            signal(peer_along(axis, step))
    signal(sibling())
    tall = 1 + (row > 0).astype(jnp.int32) + (row < rows - 1).astype(jnp.int32)
    broad = 1 + (col > 0).astype(jnp.int32) + (col < cols - 1).astype(jnp.int32)
    return tall * broad + 9


def place():
    row, col = lax.axis_index("ang"), lax.axis_index("sp")
    return lax.div(row, 4), lax.rem(row, 4), lax.div(col, 2), lax.rem(col, 2)


def device(at):
    return (at[0] * 4 + at[1], at[2] * 2 + at[3])


def peer_along(axis, step):
    at = list(place())
    at[axis] = lax.rem(at[axis] + step, 4)
    return device(at)


def sibling():
    x, y, z, core = place()
    return (x * 4 + y, z * 2 + 1 - core)


def unfold(field, taps, view_row):
    @pl.loop(0, S)
    def _(s):
        def low(k):
            block = field[view_row, s + k // 3, pl.ds(k % 3, T)]
            return block.reshape(T * V, LANES)

        out = pl.ds(pl.multiple_of(s * T * V, T * V), T * V)
        for pair in range(4):
            first = low(2 * pair)
            second = pltpu.roll(low(2 * pair + 1), 64, 1)
            at = 384 * pair
            taps[out, at : at + 128] = first[:, :128]
            taps[out, at + 128 : at + 256] = first[:, 128:] + second[:, :128]
            taps[out, at + 256 : at + 384] = second[:, 128:]
        taps[out, 1536:1792] = low(8)


def shifted(values, by):
    rows = values.shape[0]
    view = lax.broadcasted_iota(jnp.int32, values.shape, 0) % V
    keep = (view >= by) if by > 0 else (view < V + by)
    return jnp.where(keep, pltpu.roll(values, by % rows, 0), jnp.zeros_like(values))


def correlate(taps, weights, acc, view_row, first):
    @pl.loop(0, 3)
    def _(b):
        at = pl.multiple_of((view_row * 3 + b) * GROUP, 64)
        term = jnp.dot(taps[...], weights[pl.ds(at, WIDE), :], preferred_element_type=F32)
        if first:
            acc[b] = term
        else:
            acc[b] += term


UNITS = 243
TILE = (16, 128)
LENGTHS = (64, 72, 80)


def window(chips, index, count):
    start = (index * (chips * 243)) // 64
    if isinstance(index, int):
        return min(start, UNITS - count)
    return jnp.minimum(start, UNITS - count)


def kernel_terms(taps, grads, dw, a):
    for part in range(5):
        at, size = 384 * part, (384 if part < 4 else 192)
        term = lax.dot_general(
            taps[a, :, at : at + (size if part < 4 else 256)],
            grads[...],
            (((0,), (0,)), ((), ())),
            preferred_element_type=F32,
        )
        for b in range(3):
            count = size // 64
            block = term[0:size, 256 * b : 256 * b + 256].reshape(count, 2, 2, 16, 256)
            dst = pl.ds((3 * a + b) * 27 + 6 * part, count)
            for core in range(2):
                low, high = block[:, core, 0], block[:, core, 1]
                dw[core, 0, dst] = low[:, :, :128].astype(BF16)
                dw[core, 1, dst] = high[:, :, :128].astype(BF16)
                tail = pltpu.roll(high[:, :, 128:].reshape(count * 16, 128), 64, 1)
                dw[core, 2, dst] = (low[:, :, 128:] + tail.reshape(count, 16, 128)).astype(BF16)


def send_to(peer, src, dst, sems, index):
    copy = pltpu.make_async_remote_copy(
        src_ref=src,
        dst_ref=dst,
        send_sem=sems.at[0, index],
        recv_sem=sems.at[1, index],
        device_id=peer,
        device_id_type=MESH,
    )
    copy.start()
    return copy


def pieces(plane):
    if plane == 0:
        found = []
        for x in range(4):
            start = window(16, x, 64)
            for a in range(3):
                low, high = max(start, 81 * a), min(start + 64, 81 * a + 81)
                if low < high:
                    found.append((x, low - start, low, high - low))
        return found
    if plane == 1:
        return [(p % 4, 18 * (p // 4), window(4, p, 18), 18) for p in range(16)]
    return [(q % 4, 5 * (q // 4), window(1, q, 5), 5) for q in range(64)]


def ready(start, count):
    return (start + count - 1) // 81


def spans(plane):
    found = {}
    for target, at, start, count in pieces(plane):
        key = (target, ready(start, count))
        low, size = found.get(key, (at, 0))
        found[key] = (low, size + count)
    return found


class Scatter:
    def __init__(self, plane, terms, got, send, recv):
        self.axis, self.terms, self.got, self.send, self.recv = plane, terms, got, send, recv
        self.me = place()[plane]
        self.spans = spans(plane)

    def copy(self, target, a, slot):
        low, size = self.spans[target, a]
        at = list(place())
        at[self.axis] = target
        return pltpu.make_async_remote_copy(
            src_ref=self.terms.at[target, pl.ds(low, size)],
            dst_ref=self.got.at[slot, pl.ds(low, size)],
            send_sem=self.send.at[target, a],
            recv_sem=self.recv.at[slot, a],
            device_id=device(at),
            device_id_type=MESH,
        )

    def start(self, now):
        for target, a in self.spans:
            if a == now:
                slot = lax.rem(self.me + 3 - target, 4)

                @pl.when(self.me != target)
                def _():
                    self.copy(target, a, slot).start()

    def wait(self):
        for target, a in self.spans:

            @pl.when(self.me == target)
            def _():
                for slot in range(3):
                    self.copy(target, a, slot).wait_recv()

        for target, a in self.spans:

            @pl.when(self.me != target)
            def _():
                self.copy(target, a, 0).wait_send()

    def total(self, units):
        value = self.terms[self.me, units].astype(F32)
        for slot in range(3):
            value += self.got[slot, units].astype(F32)
        return value.astype(BF16)


def step_kernel(
    x_ref, cot_ref, w_ref, gi_ref, gk_ref,
    xp, gp, xc, wv, wt, acc, gall, dw, pair,
    first_a, first_b, first_c, got_a, got_b, got_c, sum_a, sum_b, sum_c, ends, both,
    halo_send, halo_recv, wsem, pair_sems, first_send, first_recv, last_sems, core_sems,
):
    chip_x, chip_y, chip_z, core = place()
    wcopy = pltpu.make_async_copy(w_ref, wv.at[pl.ds(0, ROWS)], wsem)
    wcopy.start()
    xp[...] = jnp.zeros_like(xp)
    peers = greet()
    for s in range(S):
        block = jnp.swapaxes(x_ref[0, :, s].astype(F32), 0, 1).astype(BF16)
        xp[1, 1 + s, 1 : 1 + T, :, 0:C] = block
    gp[...] = jnp.zeros_like(gp)
    rest = pl.ds(ROWS, WIDE - GROUP)
    wv[rest, :] = jnp.zeros((WIDE - GROUP, C), BF16)
    wt[rest, :] = jnp.zeros((WIDE - GROUP, C), BF16)
    pl.semaphore_wait(pltpu.get_barrier_semaphore(), peers)
    jobs = start_halo(xp, halo_send.at[0], halo_recv.at[0])

    wcopy.wait()

    @pl.loop(0, 81)
    def _(tap):
        src = pl.ds(pl.multiple_of((80 - tap) * C, 64), C)
        dst = pl.ds(pl.multiple_of(tap * C, 64), C)
        wt[dst, :] = wv[src, :].T

    for copy, _, got in jobs[:2]:
        pl.when(got)(copy.wait_recv)
    unfold(xp, xc.at[1], 1)
    correlate(xc.at[1], wv, acc, 1, True)
    for copy, _, got in jobs[2:]:
        pl.when(got)(copy.wait_recv)
    for view_row in (0, 2):
        unfold(xp, xc.at[view_row], view_row)
        correlate(xc.at[view_row], wv, acc, view_row, False)
    for copy, sent, _ in jobs:
        pl.when(sent)(copy.wait_send)

    preact = shifted(acc[0], 1) + acc[1] + shifted(acc[2], -1)
    for s in range(S):
        upstream = jnp.swapaxes(cot_ref[0, :, s].astype(F32), 0, 1).reshape(T * V, C)
        pre = preact[s * T * V : (s + 1) * T * V]
        sigmoid = jax.nn.sigmoid(pre)
        grad = upstream * sigmoid * (1.0 + pre * (1.0 - sigmoid))
        gp[1, 1 + s, 1 : 1 + T, :, 0:C] = grad.astype(BF16).reshape(T, V, C)
    jobs = start_halo(gp, halo_send.at[1], halo_recv.at[1])
    grad = gp[1, 1 : 1 + S, 1 : 1 + T].reshape(CELLS, LANES)
    wide = grad.astype(F32)
    gall[:, 0:256] = shifted(wide, -1).astype(BF16)
    gall[:, 256:512] = grad
    gall[:, 512:768] = shifted(wide, 1).astype(BF16)

    firsts = (first_a, first_b, first_c)
    scatters = [
        Scatter(k, firsts[k], (got_a, got_b, got_c)[k], first_send.at[k], first_recv.at[k])
        for k in range(3)
    ]

    def exchange(a):
        units = pl.ds(81 * a, 81)
        return send_to(sibling(), dw.at[1 - core, :, units], pair.at[:, units], pair_sems, a)

    def both_cores(plane, start, count):
        units = pl.ds(start, count)
        return dw[core, plane, units] + pair[plane, units]

    def scatter(copy, a):
        copy.wait_recv()
        for plane in range(2):
            for target, at, start, count in pieces(plane):
                if ready(start, count) == a:
                    firsts[plane][target, at : at + count] = both_cores(plane, start, count)
            scatters[plane].start(a)
        chips = [q for q, (_, _, start, count) in enumerate(pieces(2)) if ready(start, count) == a]

        @pl.loop(chips[0], chips[-1] + 1)
        def _(q):
            at = pl.ds((q // 4) * 5, 5)
            first_c[q % 4, at] = both_cores(2, window(1, q, 5), 5)

        scatters[2].start(a)

    kernel_terms(xc, gall, dw, 0)
    pairs = [exchange(0)]
    for a in (1, 2):
        kernel_terms(xc, gall, dw, a)
        pairs.append(exchange(a))
        scatter(pairs[a - 1], a - 1)
    scatter(pairs[2], 2)

    for copy, sent, got in jobs:
        pl.when(got)(copy.wait_recv)
    for view_row in (1, 0, 2):
        unfold(gp, xc.at[view_row], view_row)
        correlate(xc.at[view_row], wt, acc, view_row, view_row == 1)

    for ring in scatters:
        ring.wait()
    sum_a[...] = scatters[0].total(pl.ds(0, 64))
    for x in range(4):
        sum_b[x] = scatters[1].total(pl.ds(18 * x, 18))

    @pl.loop(0, 16)
    def _(p):
        sum_c[p] = scatters[2].total(pl.ds(5 * p, 5))

    def chip_at(plane, step):
        at = [chip_x, chip_y, chip_z, core]
        for axis, ahead in zip(((1, 2), (0, 2), (0, 1))[plane], (step // 4, step % 4)):
            at[axis] = lax.rem(at[axis] + ahead, 4)
        return at

    def part(plane, at):
        column = at[0] * 4 + at[1]
        start = window(1, column * 4 + at[2], 5)
        if plane == 0:
            return sum_a.at[pl.ds(start - window(16, at[0], 64), 5)]
        if plane == 1:
            return sum_b.at[at[0], pl.ds(start - window(4, column, 18), 5)]
        return sum_c.at[column]

    def last(plane, step):
        at = chip_at(plane, step)
        return pltpu.make_async_remote_copy(
            src_ref=part(plane, at),
            dst_ref=ends.at[plane, step],
            send_sem=last_sems.at[0, plane, step],
            recv_sem=last_sems.at[1, plane, step],
            device_id=device(at),
            device_id_type=MESH,
        )

    @pl.loop(1, 16)
    def _(step):
        for plane in range(3):
            last(plane, step).start()

    total = shifted(acc[0], 1) + acc[1] + shifted(acc[2], -1)
    for s in range(S):
        block = total[s * T * V : (s + 1) * T * V].reshape(T, V, C)
        gi_ref[0, :, s] = jnp.swapaxes(block, 0, 1).astype(BF16)
    for copy, sent, got in jobs:
        pl.when(sent)(copy.wait_send)
    for copy in pairs:
        copy.wait_send()

    for plane in range(3):
        both[core, plane] = part(plane, chip_at(plane, 0))[...].astype(F32)

    @pl.loop(1, 16)
    def _(step):
        for plane in range(3):
            last(plane, step).wait()
            both[core, plane] += ends[plane, step].astype(F32)

    send_to(sibling(), both.at[core], both.at[core], core_sems, 0).wait()
    for k in range(2):
        gk_ref[:, k, 0, :, 0:128] = both[k, 0]
        gk_ref[:, k, 1, :, 0:128] = both[k, 1]
        tail = both[k, 2]
        gk_ref[:, k, 0, :, 128:192] = tail[:, :, 0:64]
        turned = pltpu.roll(tail.reshape(80, 128), 64, 1).reshape(5, 16, 128)
        gk_ref[:, k, 1, :, 128:192] = turned[:, :, 0:64]


def local(inputs, cotangent, kernel, moment_one, moment_two):
    vmem = pl.BlockSpec(memory_space=pltpu.VMEM)
    anywhere = pl.BlockSpec(memory_space=pl.ANY)
    padded = (3, S + 2, T + 2, V, LANES)
    tiles = lambda *lead: pltpu.VMEM((*lead, *TILE), BF16)
    dma = lambda *shape: pltpu.SemaphoreType.DMA(shape)
    long_kernel = pltpu.VMEM((ROWS + WIDE - GROUP, C), BF16)
    grad_input, window_grad = pl.pallas_call(
        step_kernel,
        out_shape=(
            jax.ShapeDtypeStruct(inputs.shape, BF16),
            jax.ShapeDtypeStruct((5, 2, 2, 16, C), F32),
        ),
        in_specs=[vmem, vmem, anywhere],
        out_specs=(vmem, vmem),
        scratch_shapes=[
            pltpu.VMEM(padded, BF16),
            pltpu.VMEM(padded, BF16),
            pltpu.VMEM((3, CELLS, WIDE), BF16),
            long_kernel,
            long_kernel,
            pltpu.VMEM((3, CELLS, C), F32),
            pltpu.VMEM((CELLS, 768), BF16),
            tiles(2, 3, UNITS),
            tiles(3, UNITS),
            *(tiles(4, n) for n in LENGTHS),
            *(tiles(3, n) for n in LENGTHS),
            tiles(64),
            tiles(4, 18),
            tiles(16, 5),
            tiles(3, 16, 5),
            pltpu.VMEM((2, 3, 5, *TILE), F32),
            dma(2, 8),
            dma(2, 8),
            pltpu.SemaphoreType.DMA,
            dma(2, 3),
            dma(3, 4, 3),
            dma(3, 3, 3),
            dma(2, 3, 16),
            dma(2, 1),
        ],
        compiler_params=pltpu.CompilerParams(
            vmem_limit_bytes=56 * 1024 * 1024, collective_id=0, has_side_effects=True
        ),
        cost_estimate=pl.CostEstimate(flops=9 * 10**9, bytes_accessed=10**7, transcendentals=10**5),
    )(inputs, cotangent, kernel.reshape(ROWS, C))
    share_len = moment_one.shape[0]
    chip = lax.axis_index("ang") * 4 + lax.axis_index("sp") // 2
    begin = lax.axis_index(("ang", "sp")) * share_len - window(1, chip, 5) * (64 * C)
    share = lax.dynamic_slice_in_dim(window_grad.reshape(-1), begin, share_len, 0)
    pixels = CELLS * lax.axis_size("ang") * lax.axis_size("sp")
    grad_share = share * F32(1.0 / math.sqrt(pixels))
    moment_next = beta_one * moment_one + (1.0 - beta_one) * grad_share
    square_next = beta_two * moment_two + (1.0 - beta_two) * grad_share * grad_share
    first_fix = 1.0 - beta_one**adam_step
    second_fix = 1.0 - beta_two**adam_step
    direction = moment_next / first_fix / (jnp.sqrt(square_next / second_fix) + epsilon)
    return (grad_input, moment_next, square_next, direction)


def solution(mesh):
    field = P("ang", None, None, "sp", None)
    share = P(("ang", "sp"))
    return jax.shard_map(
        local,
        mesh=mesh,
        in_specs=(field, field, P(), share, share),
        out_specs=(field, share, share, share),
        check_vma=False,
    )
```

```python
import functools
import math

import jax
import jax.numpy as jnp
from jax import lax
from jax.experimental import pallas as pl
from jax.experimental.pallas import tpu as pltpu
from jax.sharding import PartitionSpec as P

beta_one = 0.9
beta_two = 0.999
adam_step = 100
epsilon = 1e-08

MESH = pl.DeviceIdType.MESH
F32 = jnp.float32
BF16 = jnp.bfloat16

V, S, T, C = 16, 4, 8, 192
CELLS = V * S * T
GROUP = 9 * C
WIDE = GROUP + 64
ROWS = 9 * GROUP
LANES = 256
SIDES = ((0, 1), (0, -1), (1, 0), (-1, 0), (1, 1), (1, -1), (-1, 1), (-1, -1))


def start_halo(field, send, recv):
    rows, cols = lax.axis_size("ang"), lax.axis_size("sp")
    row, col = lax.axis_index("ang"), lax.axis_index("sp")
    jobs = []
    for side, (da, ds) in enumerate(SIDES):
        if ds == 0:
            src, dst = pl.ds(1, T), pl.ds(1, T)
        elif ds == 1:
            src, dst = pl.ds(T, 1), pl.ds(0, 1)
        else:
            src, dst = pl.ds(1, 1), pl.ds(T + 1, 1)
        sent = (row + da >= 0) & (row + da < rows) & (col + ds >= 0) & (col + ds < cols)
        got = (row - da >= 0) & (row - da < rows) & (col - ds >= 0) & (col - ds < cols)
        copy = pltpu.make_async_remote_copy(
            src_ref=field.at[1, pl.ds(1, S), src],
            dst_ref=field.at[1 - da, pl.ds(1, S), dst],
            send_sem=send.at[side],
            recv_sem=recv.at[side],
            device_id=(row + da, col + ds),
            device_id_type=MESH,
        )
        pl.when(sent)(copy.start)
        jobs.append((copy, sent, got))
    return jobs


def greet():
    rows, cols = lax.axis_size("ang"), lax.axis_size("sp")
    row, col = lax.axis_index("ang"), lax.axis_index("sp")
    barrier = pltpu.get_barrier_semaphore()

    def signal(peer):
        pl.semaphore_signal(barrier, inc=1, device_id=peer, device_id_type=MESH)

    for da, ds in SIDES:
        there = (row + da >= 0) & (row + da < rows) & (col + ds >= 0) & (col + ds < cols)
        pl.when(there)(functools.partial(signal, (row + da, col + ds)))
    for axis in range(3):
        for step in range(1, 4):
            signal(peer_along(axis, step))
    signal(sibling())
    tall = 1 + (row > 0).astype(jnp.int32) + (row < rows - 1).astype(jnp.int32)
    broad = 1 + (col > 0).astype(jnp.int32) + (col < cols - 1).astype(jnp.int32)
    return tall * broad + 9


def place():
    row, col = lax.axis_index("ang"), lax.axis_index("sp")
    return lax.div(row, 4), lax.rem(row, 4), lax.div(col, 2), lax.rem(col, 2)


def device(at):
    return (at[0] * 4 + at[1], at[2] * 2 + at[3])


def peer_along(axis, step):
    at = list(place())
    at[axis] = lax.rem(at[axis] + step, 4)
    return device(at)


def sibling():
    x, y, z, core = place()
    return (x * 4 + y, z * 2 + 1 - core)


def unfold(field, taps, view_row):
    @pl.loop(0, S)
    def _(s):
        def low(k):
            block = field[view_row, s + k // 3, pl.ds(k % 3, T)]
            return block.reshape(T * V, LANES)

        out = pl.ds(pl.multiple_of(s * T * V, T * V), T * V)
        for pair in range(4):
            first = low(2 * pair)
            second = pltpu.roll(low(2 * pair + 1), 64, 1)
            at = 384 * pair
            taps[out, at : at + 128] = first[:, :128]
            taps[out, at + 128 : at + 256] = first[:, 128:] + second[:, :128]
            taps[out, at + 256 : at + 384] = second[:, 128:]
        taps[out, 1536:1792] = low(8)


def shifted(values, by):
    rows = values.shape[0]
    view = lax.broadcasted_iota(jnp.int32, values.shape, 0) % V
    keep = (view >= by) if by > 0 else (view < V + by)
    return jnp.where(keep, pltpu.roll(values, by % rows, 0), jnp.zeros_like(values))


def correlate(taps, weights, acc, view_row, first):
    @pl.loop(0, 3)
    def _(b):
        at = pl.multiple_of((view_row * 3 + b) * GROUP, 64)
        term = jnp.dot(taps[...], weights[pl.ds(at, WIDE), :], preferred_element_type=F32)
        if first:
            acc[b] = term
        else:
            acc[b] += term


UNITS = 243
TILE = (16, 128)
LENGTHS = (64, 72, 80)


def window(chips, index, count):
    start = (index * (chips * 243)) // 64
    if isinstance(index, int):
        return min(start, UNITS - count)
    return jnp.minimum(start, UNITS - count)


def kernel_terms(taps, grads, dw, a):
    for part in range(5):
        at, size = 384 * part, (384 if part < 4 else 192)
        term = lax.dot_general(
            taps[a, :, at : at + (size if part < 4 else 256)],
            grads[...],
            (((0,), (0,)), ((), ())),
            preferred_element_type=F32,
        )
        for b in range(3):
            count = size // 64
            block = term[0:size, 256 * b : 256 * b + 256].reshape(count, 2, 2, 16, 256)
            dst = pl.ds((3 * a + b) * 27 + 6 * part, count)
            for core in range(2):
                low, high = block[:, core, 0], block[:, core, 1]
                dw[core, 0, dst] = low[:, :, :128].astype(BF16)
                dw[core, 1, dst] = high[:, :, :128].astype(BF16)
                tail = pltpu.roll(high[:, :, 128:].reshape(count * 16, 128), 64, 1)
                dw[core, 2, dst] = (low[:, :, 128:] + tail.reshape(count, 16, 128)).astype(BF16)


def send_to(peer, src, dst, sems, index):
    copy = pltpu.make_async_remote_copy(
        src_ref=src,
        dst_ref=dst,
        send_sem=sems.at[0, index],
        recv_sem=sems.at[1, index],
        device_id=peer,
        device_id_type=MESH,
    )
    copy.start()
    return copy


def pieces(plane):
    if plane == 0:
        found = []
        for x in range(4):
            start = window(16, x, 64)
            for a in range(3):
                low, high = max(start, 81 * a), min(start + 64, 81 * a + 81)
                if low < high:
                    found.append((x, low - start, low, high - low))
        return found
    if plane == 1:
        return [(p % 4, 18 * (p // 4), window(4, p, 18), 18) for p in range(16)]
    return [(q % 4, 5 * (q // 4), window(1, q, 5), 5) for q in range(64)]


def ready(start, count):
    return (start + count - 1) // 81


def spans(plane):
    found = {}
    for target, at, start, count in pieces(plane):
        key = (target, ready(start, count))
        low, size = found.get(key, (at, 0))
        found[key] = (low, size + count)
    return found


class Scatter:
    def __init__(self, plane, terms, got, send, recv):
        self.axis, self.terms, self.got, self.send, self.recv = plane, terms, got, send, recv
        self.me = place()[plane]
        self.spans = spans(plane)

    def copy(self, target, a, slot):
        low, size = self.spans[target, a]
        at = list(place())
        at[self.axis] = target
        return pltpu.make_async_remote_copy(
            src_ref=self.terms.at[target, pl.ds(low, size)],
            dst_ref=self.got.at[slot, pl.ds(low, size)],
            send_sem=self.send.at[target, a],
            recv_sem=self.recv.at[slot, a],
            device_id=device(at),
            device_id_type=MESH,
        )

    def start(self, now):
        for target, a in self.spans:
            if a == now:
                slot = lax.rem(self.me + 3 - target, 4)

                @pl.when(self.me != target)
                def _():
                    self.copy(target, a, slot).start()

    def wait(self):
        for target, a in self.spans:

            @pl.when(self.me == target)
            def _():
                for slot in range(3):
                    self.copy(target, a, slot).wait_recv()

        for target, a in self.spans:

            @pl.when(self.me != target)
            def _():
                self.copy(target, a, 0).wait_send()

    def total(self, units):
        value = self.terms[self.me, units].astype(F32)
        for slot in range(3):
            value += self.got[slot, units].astype(F32)
        return value.astype(BF16)


def step_kernel(
    x_ref, cot_ref, w_ref, gi_ref, gk_ref,
    xp, gp, xc, wv, wt, acc, gall, dw, pair,
    first_a, first_b, first_c, got_a, got_b, got_c, sum_a, sum_b, sum_c,
    next_b, near_a, near_b, near_c, last_a, last_b, last_c, ends, both, left, right,
    halo_send, halo_recv, wsem, pair_sems, first_send, first_recv, next_sems, last_sems, core_sems,
):
    chip_x, chip_y, chip_z, core = place()
    wcopy = pltpu.make_async_copy(w_ref, wv.at[pl.ds(0, ROWS)], wsem)
    wcopy.start()
    xp[...] = jnp.zeros_like(xp)
    peers = greet()
    for s in range(S):
        block = jnp.swapaxes(x_ref[0, :, s].astype(F32), 0, 1).astype(BF16)
        xp[1, 1 + s, 1 : 1 + T, :, 0:C] = block
    gp[...] = jnp.zeros_like(gp)
    rest = pl.ds(ROWS, WIDE - GROUP)
    wv[rest, :] = jnp.zeros((WIDE - GROUP, C), BF16)
    wt[rest, :] = jnp.zeros((WIDE - GROUP, C), BF16)
    pl.semaphore_wait(pltpu.get_barrier_semaphore(), peers)
    jobs = start_halo(xp, halo_send.at[0], halo_recv.at[0])

    wcopy.wait()

    @pl.loop(0, 81)
    def _(tap):
        src = pl.ds(pl.multiple_of((80 - tap) * C, 64), C)
        dst = pl.ds(pl.multiple_of(tap * C, 64), C)
        wt[dst, :] = wv[src, :].T

    for copy, _, got in jobs[:2]:
        pl.when(got)(copy.wait_recv)
    unfold(xp, xc.at[1], 1)
    correlate(xc.at[1], wv, acc, 1, True)
    for copy, _, got in jobs[2:]:
        pl.when(got)(copy.wait_recv)
    for view_row in (0, 2):
        unfold(xp, xc.at[view_row], view_row)
        correlate(xc.at[view_row], wv, acc, view_row, False)
    for copy, sent, _ in jobs:
        pl.when(sent)(copy.wait_send)

    preact = shifted(acc[0], 1) + acc[1] + shifted(acc[2], -1)
    for s in range(S):
        upstream = jnp.swapaxes(cot_ref[0, :, s].astype(F32), 0, 1).reshape(T * V, C)
        pre = preact[s * T * V : (s + 1) * T * V]
        sigmoid = jax.nn.sigmoid(pre)
        grad = upstream * sigmoid * (1.0 + pre * (1.0 - sigmoid))
        gp[1, 1 + s, 1 : 1 + T, :, 0:C] = grad.astype(BF16).reshape(T, V, C)
    jobs = start_halo(gp, halo_send.at[1], halo_recv.at[1])
    grad = gp[1, 1 : 1 + S, 1 : 1 + T].reshape(CELLS, LANES)
    wide = grad.astype(F32)
    gall[:, 0:256] = shifted(wide, -1).astype(BF16)
    gall[:, 256:512] = grad
    gall[:, 512:768] = shifted(wide, 1).astype(BF16)

    firsts = (first_a, first_b, first_c)
    scatters = [
        Scatter(k, firsts[k], (got_a, got_b, got_c)[k], first_send.at[k], first_recv.at[k])
        for k in range(3)
    ]

    def exchange(a):
        units = pl.ds(81 * a, 81)
        return send_to(sibling(), dw.at[1 - core, :, units], pair.at[:, units], pair_sems, a)

    def both_cores(plane, start, count):
        units = pl.ds(start, count)
        return dw[core, plane, units] + pair[plane, units]

    def scatter(copy, a):
        copy.wait_recv()
        for plane in range(2):
            for target, at, start, count in pieces(plane):
                if ready(start, count) == a:
                    firsts[plane][target, at : at + count] = both_cores(plane, start, count)
            scatters[plane].start(a)
        chips = [q for q, (_, _, start, count) in enumerate(pieces(2)) if ready(start, count) == a]

        @pl.loop(chips[0], chips[-1] + 1)
        def _(q):
            at = pl.ds((q // 4) * 5, 5)
            first_c[q % 4, at] = both_cores(2, window(1, q, 5), 5)

        scatters[2].start(a)

    def input_terms(view_row, first):
        unfold(gp, xc.at[view_row], view_row)
        correlate(xc.at[view_row], wt, acc, view_row, first)

    kernel_terms(xc, gall, dw, 0)
    pairs = [exchange(0)]
    for a in (1, 2):
        kernel_terms(xc, gall, dw, a)
        pairs.append(exchange(a))
        scatter(pairs[a - 1], a - 1)
    for copy, _, got in jobs[:2]:
        pl.when(got)(copy.wait_recv)
    input_terms(1, True)
    scatter(pairs[2], 2)
    for copy, _, got in jobs[2:]:
        pl.when(got)(copy.wait_recv)
    input_terms(0, False)

    for ring in scatters:
        ring.wait()
    sum_a[...] = scatters[0].total(pl.ds(0, 64))
    for x in range(4):
        sum_b[x] = scatters[1].total(pl.ds(18 * x, 18))

    @pl.loop(0, 16)
    def _(p):
        sum_c[p // 4, p % 4] = scatters[2].total(pl.ds(5 * p, 5))

    chips = (chip_x, chip_y, chip_z)
    column = chip_x * 4 + chip_y

    def next_part(plane, to):
        if plane == 0:
            return sum_a.at[pl.ds(window(4, chip_x * 4 + to, 18) - window(16, chip_x, 64), 18)]
        return (next_b if plane == 1 else sum_c).at[to]

    for x in range(4):
        for z in range(4):
            start = window(1, x * 16 + chip_y * 4 + z, 5) - window(4, x * 4 + chip_y, 18)
            next_b[z, x] = sum_b[x, pl.ds(start, 5)]
    sends = []
    for step in (2, 1, 3):
        for plane, axis in enumerate((1, 2, 0)):
            src = next_part(plane, lax.rem(chips[axis] + step, 4))
            dst = (near_a, near_b, near_c)[plane].at[step - 1]
            sends.append(send_to(peer_along(axis, step), src, dst, next_sems.at[plane], step - 1))

    input_terms(2, False)
    total = shifted(acc[0], 1) + acc[1] + shifted(acc[2], -1)
    for s in range(S):
        block = total[s * T * V : (s + 1) * T * V].reshape(T, V, C)
        gi_ref[0, :, s] = jnp.swapaxes(block, 0, 1).astype(BF16)

    for copy in sends:
        copy.wait_recv()

    def near_total(plane, near):
        value = next_part(plane, chips[(1, 2, 0)[plane]])[...].astype(F32)
        for k in range(3):
            value += near[k].astype(F32)
        return value.astype(BF16)

    last_a[...] = near_total(0, near_a)
    last_b[...] = near_total(1, near_b)
    last_c[...] = near_total(2, near_c)

    def last_part(plane, to):
        if plane == 0:
            return last_a.at[pl.ds(window(1, column * 4 + to, 5) - window(4, column, 18), 5)]
        return (last_b if plane == 1 else last_c).at[to]

    lasts = []
    for step in (2, 1, 3):
        for plane, axis in enumerate((2, 0, 1)):
            src = last_part(plane, lax.rem(chips[axis] + step, 4))
            slot = 3 * plane + step - 1
            lasts.append(send_to(peer_along(axis, step), src, ends.at[slot], last_sems, slot))
    for copy, sent, _ in jobs:
        pl.when(sent)(copy.wait_send)
    for copy in (*pairs, *sends):
        copy.wait_send()
    for copy in lasts:
        copy.wait()
    for plane, axis in enumerate((2, 0, 1)):
        value = last_part(plane, chips[axis])[...].astype(F32)
        for k in range(3):
            value += ends[3 * plane + k].astype(F32)
        both[core, plane] = value
    send_to(sibling(), both.at[core], both.at[core], core_sems, 0).wait()

    for k in range(2):
        for unit in range(5):
            row = 64 * unit + 32 * k
            tail = both[k, 2, unit]
            left[row : row + 16] = both[k, 0, unit]
            left[row + 16 : row + 32] = both[k, 1, unit]
            right[row : row + 16] = tail
            right[row + 16 : row + 32] = pltpu.roll(tail, 64, 1)
    count = 160
    odd = pltpu.roll(left[pl.ds(1, count, stride=2), :], 64, 1)
    head = lax.broadcasted_iota(jnp.int32, (count, 128), 1) < 64
    gk_ref[pl.ds(0, count, stride=3), :] = left[pl.ds(0, count, stride=2), :]
    gk_ref[pl.ds(1, count, stride=3), :] = jnp.where(head, right[pl.ds(0, count, stride=2), :], odd)
    rest = pltpu.roll(right[pl.ds(1, count, stride=2), :], 64, 1)
    gk_ref[pl.ds(2, count, stride=3), :] = jnp.where(head, odd, rest)


def local(inputs, cotangent, kernel, moment_one, moment_two):
    vmem = pl.BlockSpec(memory_space=pltpu.VMEM)
    anywhere = pl.BlockSpec(memory_space=pl.ANY)
    padded = (3, S + 2, T + 2, V, LANES)
    tiles = lambda *lead: pltpu.VMEM((*lead, *TILE), BF16)
    dma = lambda *shape: pltpu.SemaphoreType.DMA(shape)
    long_kernel = pltpu.VMEM((ROWS + WIDE - GROUP, C), BF16)
    grad_input, window_grad = pl.pallas_call(
        step_kernel,
        out_shape=(
            jax.ShapeDtypeStruct(inputs.shape, BF16),
            jax.ShapeDtypeStruct((480, 128), F32),
        ),
        in_specs=[vmem, vmem, anywhere],
        out_specs=(vmem, vmem),
        scratch_shapes=[
            pltpu.VMEM(padded, BF16),
            pltpu.VMEM(padded, BF16),
            pltpu.VMEM((3, CELLS, WIDE), BF16),
            long_kernel,
            long_kernel,
            pltpu.VMEM((3, CELLS, C), F32),
            pltpu.VMEM((CELLS, 768), BF16),
            tiles(2, 3, UNITS),
            tiles(3, UNITS),
            *(tiles(4, n) for n in LENGTHS),
            *(tiles(3, n) for n in LENGTHS),
            tiles(64),
            tiles(4, 18),
            tiles(4, 4, 5),
            tiles(4, 4, 5),
            tiles(3, 18),
            tiles(3, 4, 5),
            tiles(3, 4, 5),
            tiles(18),
            tiles(4, 5),
            tiles(4, 5),
            tiles(9, 5),
            pltpu.VMEM((2, 3, 5, *TILE), F32),
            pltpu.VMEM((320, 128), F32),
            pltpu.VMEM((320, 128), F32),
            dma(2, 8),
            dma(2, 8),
            pltpu.SemaphoreType.DMA,
            dma(2, 3),
            dma(3, 4, 3),
            dma(3, 3, 3),
            dma(3, 2, 3),
            dma(2, 9),
            dma(2, 1),
        ],
        compiler_params=pltpu.CompilerParams(
            vmem_limit_bytes=56 * 1024 * 1024, collective_id=0, has_side_effects=True
        ),
        cost_estimate=pl.CostEstimate(flops=9 * 10**9, bytes_accessed=10**7, transcendentals=10**5),
    )(inputs, cotangent, kernel.reshape(ROWS, C))
    share_len = moment_one.shape[0]
    chip = lax.axis_index("ang") * 4 + lax.axis_index("sp") // 2
    begin = lax.axis_index(("ang", "sp")) * share_len - window(1, chip, 5) * (64 * C)
    share = lax.dynamic_slice_in_dim(window_grad.reshape(-1), begin, share_len, 0)
    pixels = CELLS * lax.axis_size("ang") * lax.axis_size("sp")
    grad_share = share * F32(1.0 / math.sqrt(pixels))
    moment_next = beta_one * moment_one + (1.0 - beta_one) * grad_share
    square_next = beta_two * moment_two + (1.0 - beta_two) * grad_share * grad_share
    first_fix = 1.0 - beta_one**adam_step
    second_fix = 1.0 - beta_two**adam_step
    direction = moment_next / first_fix / (jnp.sqrt(square_next / second_fix) + epsilon)
    return (grad_input, moment_next, square_next, direction)


def solution(mesh):
    field = P("ang", None, None, "sp", None)
    share = P(("ang", "sp"))
    return jax.shard_map(
        local,
        mesh=mesh,
        in_specs=(field, field, P(), share, share),
        out_specs=(field, share, share, share),
        check_vma=False,
    )
```

```python
import functools
import math

import jax
import jax.numpy as jnp
from jax import lax
from jax.experimental import pallas as pl
from jax.experimental.pallas import tpu as pltpu
from jax.sharding import PartitionSpec as P

beta_one = 0.9
beta_two = 0.999
adam_step = 100
epsilon = 1e-08

MESH = pl.DeviceIdType.MESH
F32 = jnp.float32
BF16 = jnp.bfloat16

V, S, T, C = 16, 4, 8, 192
CELLS = V * S * T
GROUP = 9 * C
WIDE = GROUP + 64
ROWS = 9 * GROUP
LANES = 256
SIDES = ((0, 1), (0, -1), (1, 0), (-1, 0), (1, 1), (1, -1), (-1, 1), (-1, -1))


def start_halo(field, packed, edges, rows_in, cols_in, send, recv):
    rows, cols = lax.axis_size("ang"), lax.axis_size("sp")
    row, col = lax.axis_index("ang"), lax.axis_index("sp")
    for j in range(2):
        first = field[1, 1 + 2 * j, 1 : 1 + T].reshape(T * V, LANES)
        second = pltpu.roll(field[1, 2 + 2 * j, 1 : 1 + T].reshape(T * V, LANES), 64, 1)
        packed[j, :, :, 0:128] = first[:, :128].reshape(T, V, 128)
        packed[j, :, :, 128:256] = (first[:, 128:] + second[:, :128]).reshape(T, V, 128)
        packed[j, :, :, 256:384] = second[:, 128:].reshape(T, V, 128)
        edges[0, j] = packed[j, 0]
        edges[1, j] = packed[j, T - 1]
    jobs = []
    for side, (da, ds) in enumerate(SIDES):
        if ds == 0:
            src, dst = packed, rows_in.at[(1 - da) // 2]
        elif ds == 1:
            src, dst = edges.at[1], cols_in.at[1 - da, 0]
        else:
            src, dst = edges.at[0], cols_in.at[1 - da, 1]
        sent = (row + da >= 0) & (row + da < rows) & (col + ds >= 0) & (col + ds < cols)
        got = (row - da >= 0) & (row - da < rows) & (col - ds >= 0) & (col - ds < cols)
        copy = pltpu.make_async_remote_copy(
            src_ref=src,
            dst_ref=dst,
            send_sem=send.at[side],
            recv_sem=recv.at[side],
            device_id=(row + da, col + ds),
            device_id_type=MESH,
        )
        jobs.append((copy, sent, got))
    for side in (4, 5, 6, 7, 2, 3, 0, 1):
        pl.when(jobs[side][1])(jobs[side][0].start)
    return jobs


def unpack(value):
    lane = lax.broadcasted_iota(jnp.int32, (value.shape[0], LANES), 1)
    keep = (lane < C).astype(F32).astype(BF16)
    return value[:, 0:LANES] * keep, pltpu.roll(value[:, 128:384], 192, 1) * keep


def place_rim(field, rows_in, cols_in, view_row):
    for j in range(2):
        if view_row != 1:
            pair = unpack(rows_in[view_row // 2, j].reshape(T * V, 384))
            for k in range(2):
                field[view_row, 1 + 2 * j + k, 1 : 1 + T] = pair[k].reshape(T, V, LANES)
        for side, at in ((0, 0), (1, T + 1)):
            pair = unpack(cols_in[view_row, side, j])
            for k in range(2):
                field[view_row, 1 + 2 * j + k, at] = pair[k]


def greet():
    rows, cols = lax.axis_size("ang"), lax.axis_size("sp")
    row, col = lax.axis_index("ang"), lax.axis_index("sp")
    barrier = pltpu.get_barrier_semaphore()

    def signal(peer):
        pl.semaphore_signal(barrier, inc=1, device_id=peer, device_id_type=MESH)

    for da, ds in SIDES:
        there = (row + da >= 0) & (row + da < rows) & (col + ds >= 0) & (col + ds < cols)
        pl.when(there)(functools.partial(signal, (row + da, col + ds)))
    for axis in range(3):
        for step in range(1, 4):
            signal(peer_along(axis, step))
    signal(sibling())
    tall = 1 + (row > 0).astype(jnp.int32) + (row < rows - 1).astype(jnp.int32)
    broad = 1 + (col > 0).astype(jnp.int32) + (col < cols - 1).astype(jnp.int32)
    return tall * broad + 9


def place():
    row, col = lax.axis_index("ang"), lax.axis_index("sp")
    return lax.div(row, 4), lax.rem(row, 4), lax.div(col, 2), lax.rem(col, 2)


def device(at):
    return (at[0] * 4 + at[1], at[2] * 2 + at[3])


def peer_along(axis, step):
    at = list(place())
    at[axis] = lax.rem(at[axis] + step, 4)
    return device(at)


def sibling():
    x, y, z, core = place()
    return (x * 4 + y, z * 2 + 1 - core)


def unfold(field, taps, view_row):
    @pl.loop(0, S)
    def _(s):
        def low(k):
            block = field[view_row, s + k // 3, pl.ds(k % 3, T)]
            return block.reshape(T * V, LANES)

        out = pl.ds(pl.multiple_of(s * T * V, T * V), T * V)
        for pair in range(4):
            first = low(2 * pair)
            second = pltpu.roll(low(2 * pair + 1), 64, 1)
            at = 384 * pair
            taps[out, at : at + 128] = first[:, :128]
            taps[out, at + 128 : at + 256] = first[:, 128:] + second[:, :128]
            taps[out, at + 256 : at + 384] = second[:, 128:]
        taps[out, 1536:1792] = low(8)


def shifted(values, by):
    rows = values.shape[0]
    view = lax.broadcasted_iota(jnp.int32, values.shape, 0) % V
    keep = (view >= by) if by > 0 else (view < V + by)
    return jnp.where(keep, pltpu.roll(values, by % rows, 0), jnp.zeros_like(values))


def correlate(taps, weights, acc, view_row, first):
    @pl.loop(0, 3)
    def _(b):
        at = pl.multiple_of((view_row * 3 + b) * GROUP, 64)
        term = jnp.dot(taps[...], weights[pl.ds(at, WIDE), :], preferred_element_type=F32)
        if first:
            acc[b] = term
        else:
            acc[b] += term


UNITS = 243
TILE = (16, 128)
LENGTHS = (64, 72, 80)


def window(chips, index, count):
    start = (index * (chips * 243)) // 64
    if isinstance(index, int):
        return min(start, UNITS - count)
    return jnp.minimum(start, UNITS - count)


def kernel_terms(taps, grads, dw, a):
    for part in range(5):
        at, size = 384 * part, (384 if part < 4 else 192)
        term = lax.dot_general(
            taps[a, :, at : at + (size if part < 4 else 256)],
            grads[...],
            (((0,), (0,)), ((), ())),
            preferred_element_type=F32,
        )
        for b in range(3):
            count = size // 64
            block = term[0:size, 256 * b : 256 * b + 256].reshape(count, 2, 2, 16, 256)
            dst = pl.ds((3 * a + b) * 27 + 6 * part, count)
            for core in range(2):
                low, high = block[:, core, 0], block[:, core, 1]
                dw[core, 0, dst] = low[:, :, :128].astype(BF16)
                dw[core, 1, dst] = high[:, :, :128].astype(BF16)
                tail = pltpu.roll(high[:, :, 128:].reshape(count * 16, 128), 64, 1)
                dw[core, 2, dst] = (low[:, :, 128:] + tail.reshape(count, 16, 128)).astype(BF16)


def send_to(peer, src, dst, sems, index):
    copy = pltpu.make_async_remote_copy(
        src_ref=src,
        dst_ref=dst,
        send_sem=sems.at[0, index],
        recv_sem=sems.at[1, index],
        device_id=peer,
        device_id_type=MESH,
    )
    copy.start()
    return copy


def pieces(plane):
    if plane == 0:
        found = []
        for x in range(4):
            start = window(16, x, 64)
            for a in range(3):
                low, high = max(start, 81 * a), min(start + 64, 81 * a + 81)
                if low < high:
                    found.append((x, low - start, low, high - low))
        return found
    if plane == 1:
        return [(p % 4, 18 * (p // 4), window(4, p, 18), 18) for p in range(16)]
    return [(q % 4, 5 * (q // 4), window(1, q, 5), 5) for q in range(64)]


def ready(start, count):
    return (start + count - 1) // 81


def spans(plane):
    found = {}
    for target, at, start, count in pieces(plane):
        key = (target, ready(start, count))
        low, size = found.get(key, (at, 0))
        found[key] = (low, size + count)
    return found


class Scatter:
    def __init__(self, plane, terms, got, send, recv):
        self.axis, self.terms, self.got, self.send, self.recv = plane, terms, got, send, recv
        self.me = place()[plane]
        self.spans = spans(plane)

    def copy(self, target, a, slot):
        low, size = self.spans[target, a]
        at = list(place())
        at[self.axis] = target
        return pltpu.make_async_remote_copy(
            src_ref=self.terms.at[target, pl.ds(low, size)],
            dst_ref=self.got.at[slot, pl.ds(low, size)],
            send_sem=self.send.at[target, a],
            recv_sem=self.recv.at[slot, a],
            device_id=device(at),
            device_id_type=MESH,
        )

    def start(self, now):
        for target, a in self.spans:
            if a == now:
                slot = lax.rem(self.me + 3 - target, 4)

                @pl.when(self.me != target)
                def _():
                    self.copy(target, a, slot).start()

    def wait(self):
        for target, a in self.spans:

            @pl.when(self.me == target)
            def _():
                for slot in range(3):
                    self.copy(target, a, slot).wait_recv()

        for target, a in self.spans:

            @pl.when(self.me != target)
            def _():
                self.copy(target, a, 0).wait_send()

    def total(self, units):
        value = self.terms[self.me, units].astype(F32)
        for slot in range(3):
            value += self.got[slot, units].astype(F32)
        return value.astype(BF16)


def step_kernel(
    x_hbm, cot_hbm, w_ref, gi_ref, gk_ref,
    x_ref, cot_ref, gi_out, packed, edges, rows_in, cols_in, xp, gp, xc, wv, wt, acc, gall, dw, pair,
    first_a, first_b, first_c, got_a, got_b, got_c, sum_a, sum_b, sum_c,
    next_b, near_a, near_b, near_c, last_a, last_b, last_c, ends, both, left, right,
    halo_send, halo_recv, in_sems, wsem, pair_sems, first_send, first_recv, next_sems, last_sems, core_sems,
):
    chip_x, chip_y, chip_z, core = place()
    xcopy = pltpu.make_async_copy(x_hbm, x_ref, in_sems.at[0])
    ccopy = pltpu.make_async_copy(cot_hbm, cot_ref, in_sems.at[1])
    wcopy = pltpu.make_async_copy(w_ref, wv.at[pl.ds(0, ROWS)], wsem)
    xcopy.start()
    wcopy.start()
    ccopy.start()
    rows_in[...] = jnp.zeros_like(rows_in)
    cols_in[...] = jnp.zeros_like(cols_in)
    peers = greet()
    xp[...] = jnp.zeros_like(xp)
    gp[...] = jnp.zeros_like(gp)
    rest = pl.ds(ROWS, WIDE - GROUP)
    wv[rest, :] = jnp.zeros((WIDE - GROUP, C), BF16)
    wt[rest, :] = jnp.zeros((WIDE - GROUP, C), BF16)
    xcopy.wait()
    for s in range(S):
        block = jnp.swapaxes(x_ref[0, :, s].astype(F32), 0, 1).astype(BF16)
        xp[1, 1 + s, 1 : 1 + T, :, 0:C] = block

    def halo(field, k):
        pads = (packed.at[k], edges.at[k], rows_in.at[k], cols_in.at[k])
        return start_halo(field, *pads, halo_send.at[k], halo_recv.at[k])

    def rim(field, k, view_row):
        place_rim(field, rows_in.at[k], cols_in.at[k], view_row)

    pl.semaphore_wait(pltpu.get_barrier_semaphore(), peers)
    jobs = halo(xp, 0)

    wcopy.wait()

    @pl.loop(0, 81)
    def _(tap):
        src = pl.ds(pl.multiple_of((80 - tap) * C, 64), C)
        dst = pl.ds(pl.multiple_of(tap * C, 64), C)
        wt[dst, :] = wv[src, :].T

    for copy, _, got in jobs[:2]:
        pl.when(got)(copy.wait_recv)
    rim(xp, 0, 1)
    unfold(xp, xc.at[1], 1)
    correlate(xc.at[1], wv, acc, 1, True)
    for copy, _, got in jobs[2:]:
        pl.when(got)(copy.wait_recv)
    for view_row in (0, 2):
        rim(xp, 0, view_row)
        unfold(xp, xc.at[view_row], view_row)
        correlate(xc.at[view_row], wv, acc, view_row, False)
    for copy, sent, _ in jobs:
        pl.when(sent)(copy.wait_send)

    ccopy.wait()
    preact = shifted(acc[0], 1) + acc[1] + shifted(acc[2], -1)
    for s in range(S):
        upstream = jnp.swapaxes(cot_ref[0, :, s].astype(F32), 0, 1).reshape(T * V, C)
        pre = preact[s * T * V : (s + 1) * T * V]
        sigmoid = jax.nn.sigmoid(pre)
        grad = upstream * sigmoid * (1.0 + pre * (1.0 - sigmoid))
        gp[1, 1 + s, 1 : 1 + T, :, 0:C] = grad.astype(BF16).reshape(T, V, C)
    jobs = halo(gp, 1)
    grad = gp[1, 1 : 1 + S, 1 : 1 + T].reshape(CELLS, LANES)
    wide = grad.astype(F32)
    gall[:, 0:256] = shifted(wide, -1).astype(BF16)
    gall[:, 256:512] = grad
    gall[:, 512:768] = shifted(wide, 1).astype(BF16)

    firsts = (first_a, first_b, first_c)
    scatters = [
        Scatter(k, firsts[k], (got_a, got_b, got_c)[k], first_send.at[k], first_recv.at[k])
        for k in range(3)
    ]

    def exchange(a):
        units = pl.ds(81 * a, 81)
        return send_to(sibling(), dw.at[1 - core, :, units], pair.at[:, units], pair_sems, a)

    def both_cores(plane, start, count):
        units = pl.ds(start, count)
        return dw[core, plane, units] + pair[plane, units]

    def scatter(copy, a):
        copy.wait_recv()
        for plane in range(2):
            for target, at, start, count in pieces(plane):
                if ready(start, count) == a:
                    firsts[plane][target, at : at + count] = both_cores(plane, start, count)
            scatters[plane].start(a)
        chips = [q for q, (_, _, start, count) in enumerate(pieces(2)) if ready(start, count) == a]

        @pl.loop(chips[0], chips[-1] + 1)
        def _(q):
            at = pl.ds((q // 4) * 5, 5)
            first_c[q % 4, at] = both_cores(2, window(1, q, 5), 5)

        scatters[2].start(a)

    def input_terms(view_row, first):
        rim(gp, 1, view_row)
        unfold(gp, xc.at[view_row], view_row)
        correlate(xc.at[view_row], wt, acc, view_row, first)

    kernel_terms(xc, gall, dw, 0)
    pairs = [exchange(0)]
    for a in (1, 2):
        kernel_terms(xc, gall, dw, a)
        pairs.append(exchange(a))
        scatter(pairs[a - 1], a - 1)
    for copy, _, got in jobs[:2]:
        pl.when(got)(copy.wait_recv)
    input_terms(1, True)
    scatter(pairs[2], 2)
    for copy, _, got in jobs[2:]:
        pl.when(got)(copy.wait_recv)
    input_terms(0, False)

    for ring in scatters:
        ring.wait()
    sum_a[...] = scatters[0].total(pl.ds(0, 64))
    for x in range(4):
        sum_b[x] = scatters[1].total(pl.ds(18 * x, 18))

    @pl.loop(0, 16)
    def _(p):
        sum_c[p // 4, p % 4] = scatters[2].total(pl.ds(5 * p, 5))

    chips = (chip_x, chip_y, chip_z)
    column = chip_x * 4 + chip_y

    def next_part(plane, to):
        if plane == 0:
            return sum_a.at[pl.ds(window(4, chip_x * 4 + to, 18) - window(16, chip_x, 64), 18)]
        return (next_b if plane == 1 else sum_c).at[to]

    for x in range(4):
        for z in range(4):
            start = window(1, x * 16 + chip_y * 4 + z, 5) - window(4, x * 4 + chip_y, 18)
            next_b[z, x] = sum_b[x, pl.ds(start, 5)]
    sends = []
    for step in (2, 1, 3):
        for plane, axis in enumerate((1, 2, 0)):
            src = next_part(plane, lax.rem(chips[axis] + step, 4))
            dst = (near_a, near_b, near_c)[plane].at[step - 1]
            sends.append(send_to(peer_along(axis, step), src, dst, next_sems.at[plane], step - 1))

    input_terms(2, False)
    total = shifted(acc[0], 1) + acc[1] + shifted(acc[2], -1)
    for s in range(S):
        block = total[s * T * V : (s + 1) * T * V].reshape(T, V, C)
        gi_out[0, :, s] = jnp.swapaxes(block, 0, 1).astype(BF16)
    gcopy = pltpu.make_async_copy(gi_out, gi_ref, in_sems.at[2])
    gcopy.start()

    for copy in sends:
        copy.wait_recv()

    def near_total(plane, near):
        value = next_part(plane, chips[(1, 2, 0)[plane]])[...].astype(F32)
        for k in range(3):
            value += near[k].astype(F32)
        return value.astype(BF16)

    last_a[...] = near_total(0, near_a)
    last_b[...] = near_total(1, near_b)
    last_c[...] = near_total(2, near_c)

    def last_part(plane, to):
        if plane == 0:
            return last_a.at[pl.ds(window(1, column * 4 + to, 5) - window(4, column, 18), 5)]
        return (last_b if plane == 1 else last_c).at[to]

    lasts = []
    for step in (2, 1, 3):
        for plane, axis in enumerate((2, 0, 1)):
            src = last_part(plane, lax.rem(chips[axis] + step, 4))
            slot = 3 * plane + step - 1
            lasts.append(send_to(peer_along(axis, step), src, ends.at[slot], last_sems, slot))
    for copy, sent, _ in jobs:
        pl.when(sent)(copy.wait_send)
    for copy in (*pairs, *sends):
        copy.wait_send()
    for copy in lasts:
        copy.wait()
    for plane, axis in enumerate((2, 0, 1)):
        value = last_part(plane, chips[axis])[...].astype(F32)
        for k in range(3):
            value += ends[3 * plane + k].astype(F32)
        both[core, plane] = value
    gcopy.wait()
    send_to(sibling(), both.at[core], both.at[core], core_sems, 0).wait()

    for k in range(2):
        for unit in range(5):
            row = 64 * unit + 32 * k
            tail = both[k, 2, unit]
            left[row : row + 16] = both[k, 0, unit]
            left[row + 16 : row + 32] = both[k, 1, unit]
            right[row : row + 16] = tail
            right[row + 16 : row + 32] = pltpu.roll(tail, 64, 1)
    count = 160
    odd = pltpu.roll(left[pl.ds(1, count, stride=2), :], 64, 1)
    head = lax.broadcasted_iota(jnp.int32, (count, 128), 1) < 64
    gk_ref[pl.ds(0, count, stride=3), :] = left[pl.ds(0, count, stride=2), :]
    gk_ref[pl.ds(1, count, stride=3), :] = jnp.where(head, right[pl.ds(0, count, stride=2), :], odd)
    rest = pltpu.roll(right[pl.ds(1, count, stride=2), :], 64, 1)
    gk_ref[pl.ds(2, count, stride=3), :] = jnp.where(head, odd, rest)


def local(inputs, cotangent, kernel, moment_one, moment_two):
    vmem = pl.BlockSpec(memory_space=pltpu.VMEM)
    anywhere = pl.BlockSpec(memory_space=pl.ANY)
    padded = (3, S + 2, T + 2, V, LANES)
    tiles = lambda *lead: pltpu.VMEM((*lead, *TILE), BF16)
    dma = lambda *shape: pltpu.SemaphoreType.DMA(shape)
    long_kernel = pltpu.VMEM((ROWS + WIDE - GROUP, C), BF16)
    grad_input, window_grad = pl.pallas_call(
        step_kernel,
        out_shape=(
            jax.ShapeDtypeStruct(inputs.shape, BF16),
            jax.ShapeDtypeStruct((480, 128), F32),
        ),
        in_specs=[anywhere, anywhere, anywhere],
        out_specs=(anywhere, vmem),
        scratch_shapes=[
            *(pltpu.VMEM(inputs.shape, BF16) for _ in range(3)),
            pltpu.VMEM((2, 2, T, V, 384), BF16),
            pltpu.VMEM((2, 2, 2, V, 384), BF16),
            pltpu.VMEM((2, 2, 2, T, V, 384), BF16),
            pltpu.VMEM((2, 3, 2, 2, V, 384), BF16),
            pltpu.VMEM(padded, BF16),
            pltpu.VMEM(padded, BF16),
            pltpu.VMEM((3, CELLS, WIDE), BF16),
            long_kernel,
            long_kernel,
            pltpu.VMEM((3, CELLS, C), F32),
            pltpu.VMEM((CELLS, 768), BF16),
            tiles(2, 3, UNITS),
            tiles(3, UNITS),
            *(tiles(4, n) for n in LENGTHS),
            *(tiles(3, n) for n in LENGTHS),
            tiles(64),
            tiles(4, 18),
            tiles(4, 4, 5),
            tiles(4, 4, 5),
            tiles(3, 18),
            tiles(3, 4, 5),
            tiles(3, 4, 5),
            tiles(18),
            tiles(4, 5),
            tiles(4, 5),
            tiles(9, 5),
            pltpu.VMEM((2, 3, 5, *TILE), F32),
            pltpu.VMEM((320, 128), F32),
            pltpu.VMEM((320, 128), F32),
            dma(2, 8),
            dma(2, 8),
            dma(3),
            pltpu.SemaphoreType.DMA,
            dma(2, 3),
            dma(3, 4, 3),
            dma(3, 3, 3),
            dma(3, 2, 3),
            dma(2, 9),
            dma(2, 1),
        ],
        compiler_params=pltpu.CompilerParams(
            vmem_limit_bytes=56 * 1024 * 1024, collective_id=0, has_side_effects=True
        ),
        cost_estimate=pl.CostEstimate(flops=9 * 10**9, bytes_accessed=10**7, transcendentals=10**5),
    )(inputs, cotangent, kernel.reshape(ROWS, C))
    share_len = moment_one.shape[0]
    chip = lax.axis_index("ang") * 4 + lax.axis_index("sp") // 2
    begin = lax.axis_index(("ang", "sp")) * share_len - window(1, chip, 5) * (64 * C)
    share = lax.dynamic_slice_in_dim(window_grad.reshape(-1), begin, share_len, 0)
    pixels = CELLS * lax.axis_size("ang") * lax.axis_size("sp")
    grad_share = share * F32(1.0 / math.sqrt(pixels))
    moment_next = beta_one * moment_one + (1.0 - beta_one) * grad_share
    square_next = beta_two * moment_two + (1.0 - beta_two) * grad_share * grad_share
    first_fix = 1.0 - beta_one**adam_step
    second_fix = 1.0 - beta_two**adam_step
    direction = moment_next / first_fix / (jnp.sqrt(square_next / second_fix) + epsilon)
    return (grad_input, moment_next, square_next, direction)


def solution(mesh):
    field = P("ang", None, None, "sp", None)
    share = P(("ang", "sp"))
    return jax.shard_map(
        local,
        mesh=mesh,
        in_specs=(field, field, P(), share, share),
        out_specs=(field, share, share, share),
        check_vma=False,
    )
```

```python
import functools
import math

import jax
import jax.numpy as jnp
from jax import lax
from jax.experimental import pallas as pl
from jax.experimental.pallas import tpu as pltpu
from jax.sharding import PartitionSpec as P

beta_one = 0.9
beta_two = 0.999
adam_step = 100
epsilon = 1e-08

MESH = pl.DeviceIdType.MESH
F32 = jnp.float32
BF16 = jnp.bfloat16

V, S, T, C = 16, 4, 8, 192
CELLS = V * S * T
GROUP = 9 * C
WIDE = GROUP + 64
ROWS = 9 * GROUP
LANES = 256
SIDES = ((0, 1), (0, -1), (1, 0), (-1, 0), (1, 1), (1, -1), (-1, 1), (-1, -1))


def start_halo(field, packed, edges, rows_in, cols_in, send, recv):
    rows, cols = lax.axis_size("ang"), lax.axis_size("sp")
    row, col = lax.axis_index("ang"), lax.axis_index("sp")
    for j in range(2):
        first = field[1, 1 + 2 * j, 1 : 1 + T].reshape(T * V, LANES)
        second = pltpu.roll(field[1, 2 + 2 * j, 1 : 1 + T].reshape(T * V, LANES), 64, 1)
        packed[j, :, :, 0:128] = first[:, :128].reshape(T, V, 128)
        packed[j, :, :, 128:256] = (first[:, 128:] + second[:, :128]).reshape(T, V, 128)
        packed[j, :, :, 256:384] = second[:, 128:].reshape(T, V, 128)
        edges[0, j] = packed[j, 0]
        edges[1, j] = packed[j, T - 1]
    jobs = []
    for side, (da, ds) in enumerate(SIDES):
        if ds == 0:
            src, dst = packed, rows_in.at[(1 - da) // 2]
        elif ds == 1:
            src, dst = edges.at[1], cols_in.at[1 - da, 0]
        else:
            src, dst = edges.at[0], cols_in.at[1 - da, 1]
        sent = (row + da >= 0) & (row + da < rows) & (col + ds >= 0) & (col + ds < cols)
        got = (row - da >= 0) & (row - da < rows) & (col - ds >= 0) & (col - ds < cols)
        copy = pltpu.make_async_remote_copy(
            src_ref=src,
            dst_ref=dst,
            send_sem=send.at[side],
            recv_sem=recv.at[side],
            device_id=(row + da, col + ds),
            device_id_type=MESH,
        )
        jobs.append((copy, sent, got))
    for side in (4, 5, 6, 7, 2, 3, 0, 1):
        pl.when(jobs[side][1])(jobs[side][0].start)
    return jobs


def unpack(value):
    lane = lax.broadcasted_iota(jnp.int32, (value.shape[0], LANES), 1)
    keep = (lane < C).astype(F32).astype(BF16)
    return value[:, 0:LANES] * keep, pltpu.roll(value[:, 128:384], 192, 1) * keep


def place_rim(field, rows_in, cols_in, view_row):
    for j in range(2):
        if view_row != 1:
            pair = unpack(rows_in[view_row // 2, j].reshape(T * V, 384))
            for k in range(2):
                field[view_row, 1 + 2 * j + k, 1 : 1 + T] = pair[k].reshape(T, V, LANES)
        for side, at in ((0, 0), (1, T + 1)):
            pair = unpack(cols_in[view_row, side, j])
            for k in range(2):
                field[view_row, 1 + 2 * j + k, at] = pair[k]


def greet():
    rows, cols = lax.axis_size("ang"), lax.axis_size("sp")
    row, col = lax.axis_index("ang"), lax.axis_index("sp")
    barrier = pltpu.get_barrier_semaphore()

    def signal(peer):
        pl.semaphore_signal(barrier, inc=1, device_id=peer, device_id_type=MESH)

    for da, ds in SIDES:
        there = (row + da >= 0) & (row + da < rows) & (col + ds >= 0) & (col + ds < cols)
        pl.when(there)(functools.partial(signal, (row + da, col + ds)))
    for axis in range(3):
        for step in range(1, 4):
            signal(peer_along(axis, step))
    signal(sibling())
    tall = 1 + (row > 0).astype(jnp.int32) + (row < rows - 1).astype(jnp.int32)
    broad = 1 + (col > 0).astype(jnp.int32) + (col < cols - 1).astype(jnp.int32)
    return tall * broad + 9


def place():
    row, col = lax.axis_index("ang"), lax.axis_index("sp")
    return lax.div(row, 4), lax.rem(row, 4), lax.div(col, 2), lax.rem(col, 2)


def device(at):
    return (at[0] * 4 + at[1], at[2] * 2 + at[3])


def peer_along(axis, step):
    at = list(place())
    at[axis] = lax.rem(at[axis] + step, 4)
    return device(at)


def sibling():
    x, y, z, core = place()
    return (x * 4 + y, z * 2 + 1 - core)


def unfold(field, taps, view_row):
    @pl.loop(0, S)
    def _(s):
        def low(k):
            block = field[view_row, s + k // 3, pl.ds(k % 3, T)]
            return block.reshape(T * V, LANES)

        out = pl.ds(pl.multiple_of(s * T * V, T * V), T * V)
        for pair in range(4):
            first = low(2 * pair)
            second = pltpu.roll(low(2 * pair + 1), 64, 1)
            at = 384 * pair
            taps[out, at : at + 128] = first[:, :128]
            taps[out, at + 128 : at + 256] = first[:, 128:] + second[:, :128]
            taps[out, at + 256 : at + 384] = second[:, 128:]
        taps[out, 1536:1792] = low(8)


def shifted(values, by):
    rows = values.shape[0]
    view = lax.broadcasted_iota(jnp.int32, values.shape, 0) % V
    keep = (view >= by) if by > 0 else (view < V + by)
    return jnp.where(keep, pltpu.roll(values, by % rows, 0), jnp.zeros_like(values))


def correlate(taps, weights, acc, view_row, first):
    @pl.loop(0, 3)
    def _(b):
        at = pl.multiple_of((view_row * 3 + b) * GROUP, 64)
        term = jnp.dot(taps[...], weights[pl.ds(at, WIDE), :], preferred_element_type=F32)
        if first:
            acc[b] = term
        else:
            acc[b] += term


UNITS = 243
TILE = (16, 128)
SHARE = 243 * C // 2
BAND = 17
LENGTHS = (64, 4 * BAND, 80)


def window(chips, index, count):
    start = (index * (chips * 243)) // 64
    if isinstance(index, int):
        return min(start, UNITS - count)
    return jnp.minimum(start, UNITS - count)


def kernel_terms(taps, grads, dw, a):
    for part in range(5):
        at, size = 384 * part, (384 if part < 4 else 192)
        term = lax.dot_general(
            taps[a, :, at : at + (size if part < 4 else 256)],
            grads[...],
            (((0,), (0,)), ((), ())),
            preferred_element_type=F32,
        )
        for b in range(3):
            count = size // 64
            block = term[0:size, 256 * b : 256 * b + 256].reshape(count, 2, 2, 16, 256)
            dst = pl.ds((3 * a + b) * 27 + 6 * part, count)
            for core in range(2):
                low, high = block[:, core, 0], block[:, core, 1]
                dw[core, 0, dst] = low[:, :, :128].astype(BF16)
                dw[core, 1, dst] = high[:, :, :128].astype(BF16)
                tail = pltpu.roll(high[:, :, 128:].reshape(count * 16, 128), 64, 1)
                dw[core, 2, dst] = (low[:, :, 128:] + tail.reshape(count, 16, 128)).astype(BF16)


def send_to(peer, src, dst, sems, index):
    copy = pltpu.make_async_remote_copy(
        src_ref=src,
        dst_ref=dst,
        send_sem=sems.at[0, index],
        recv_sem=sems.at[1, index],
        device_id=peer,
        device_id_type=MESH,
    )
    copy.start()
    return copy


def pieces(plane):
    if plane == 0:
        found = []
        for x in range(4):
            start = window(16, x, 64)
            for a in range(3):
                low, high = max(start, 81 * a), min(start + 64, 81 * a + 81)
                if low < high:
                    found.append((x, low - start, low, high - low))
        return found
    if plane == 1:
        return [(p % 4, BAND * (p // 4), window(4, p, BAND), BAND) for p in range(16)]
    return [(q % 4, 5 * (q // 4), window(1, q, 5), 5) for q in range(64)]


def ready(start, count):
    return (start + count - 1) // 81


def spans(plane):
    found = {}
    for target, at, start, count in pieces(plane):
        key = (target, ready(start, count))
        low, size = found.get(key, (at, 0))
        found[key] = (low, size + count)
    return found


class Scatter:
    def __init__(self, plane, terms, got, send, recv):
        self.axis, self.terms, self.got, self.send, self.recv = plane, terms, got, send, recv
        self.me = place()[plane]
        self.spans = spans(plane)

    def copy(self, target, a, slot):
        low, size = self.spans[target, a]
        at = list(place())
        at[self.axis] = target
        return pltpu.make_async_remote_copy(
            src_ref=self.terms.at[target, pl.ds(low, size)],
            dst_ref=self.got.at[slot, pl.ds(low, size)],
            send_sem=self.send.at[target, a],
            recv_sem=self.recv.at[slot, a],
            device_id=device(at),
            device_id_type=MESH,
        )

    def start(self, now):
        for target, a in self.spans:
            if a == now:
                slot = lax.rem(self.me + 3 - target, 4)

                @pl.when(self.me != target)
                def _():
                    self.copy(target, a, slot).start()

    def wait(self):
        for target, a in self.spans:

            @pl.when(self.me == target)
            def _():
                for slot in range(3):
                    self.copy(target, a, slot).wait_recv()

        for target, a in self.spans:

            @pl.when(self.me != target)
            def _():
                self.copy(target, a, 0).wait_send()

    def total(self, units):
        value = self.terms[self.me, units].astype(F32)
        for slot in range(3):
            value += self.got[slot, units].astype(F32)
        return value.astype(BF16)


def step_kernel(
    x_hbm, cot_hbm, w_ref, gi_ref, gk_ref,
    x_ref, cot_ref, gi_out, packed, edges, rows_in, cols_in, xp, gp, xc, wv, wt, acc, gall, dw, pair,
    first_a, first_b, first_c, got_a, got_b, got_c, sum_a, sum_b, sum_c,
    next_b, near_a, near_b, near_c, last_a, last_b, last_c, ends, both, left, right, flat,
    halo_send, halo_recv, in_sems, wsem, pair_sems, first_send, first_recv, next_sems, last_sems, core_sems,
):
    chip_x, chip_y, chip_z, core = place()
    xcopy = pltpu.make_async_copy(x_hbm, x_ref, in_sems.at[0])
    ccopy = pltpu.make_async_copy(cot_hbm, cot_ref, in_sems.at[1])
    wcopy = pltpu.make_async_copy(w_ref, wv.at[pl.ds(0, ROWS)], wsem)
    xcopy.start()
    wcopy.start()
    ccopy.start()
    rows_in[...] = jnp.zeros_like(rows_in)
    cols_in[...] = jnp.zeros_like(cols_in)
    peers = greet()
    xp[...] = jnp.zeros_like(xp)
    gp[...] = jnp.zeros_like(gp)
    rest = pl.ds(ROWS, WIDE - GROUP)
    wv[rest, :] = jnp.zeros((WIDE - GROUP, C), BF16)
    wt[rest, :] = jnp.zeros((WIDE - GROUP, C), BF16)
    xcopy.wait()
    for s in range(S):
        block = jnp.swapaxes(x_ref[0, :, s].astype(F32), 0, 1).astype(BF16)
        xp[1, 1 + s, 1 : 1 + T, :, 0:C] = block

    def halo(field, k):
        pads = (packed.at[k], edges.at[k], rows_in.at[k], cols_in.at[k])
        return start_halo(field, *pads, halo_send.at[k], halo_recv.at[k])

    def rim(field, k, view_row):
        place_rim(field, rows_in.at[k], cols_in.at[k], view_row)

    wcopy.wait()

    def turn(low, high):
        @pl.loop(low, high)
        def _(tap):
            src = pl.ds(pl.multiple_of((80 - tap) * C, 64), C)
            dst = pl.ds(pl.multiple_of(tap * C, 64), C)
            wt[dst, :] = wv[src, :].T

    turn(0, 45)
    pl.semaphore_wait(pltpu.get_barrier_semaphore(), peers)
    jobs = halo(xp, 0)
    turn(45, 81)
    for copy, _, got in jobs[:2]:
        pl.when(got)(copy.wait_recv)
    rim(xp, 0, 1)
    unfold(xp, xc.at[1], 1)
    correlate(xc.at[1], wv, acc, 1, True)
    for copy, _, got in jobs[2:]:
        pl.when(got)(copy.wait_recv)
    for view_row in (0, 2):
        rim(xp, 0, view_row)
        unfold(xp, xc.at[view_row], view_row)
        correlate(xc.at[view_row], wv, acc, view_row, False)
    for copy, sent, _ in jobs:
        pl.when(sent)(copy.wait_send)

    ccopy.wait()
    preact = shifted(acc[0], 1) + acc[1] + shifted(acc[2], -1)
    for s in range(S):
        upstream = jnp.swapaxes(cot_ref[0, :, s].astype(F32), 0, 1).reshape(T * V, C)
        pre = preact[s * T * V : (s + 1) * T * V]
        sigmoid = jax.nn.sigmoid(pre)
        grad = upstream * sigmoid * (1.0 + pre * (1.0 - sigmoid))
        gp[1, 1 + s, 1 : 1 + T, :, 0:C] = grad.astype(BF16).reshape(T, V, C)
    jobs = halo(gp, 1)
    grad = gp[1, 1 : 1 + S, 1 : 1 + T].reshape(CELLS, LANES)
    wide = grad.astype(F32)
    gall[:, 0:256] = shifted(wide, -1).astype(BF16)
    gall[:, 256:512] = grad
    gall[:, 512:768] = shifted(wide, 1).astype(BF16)

    firsts = (first_a, first_b, first_c)
    scatters = [
        Scatter(k, firsts[k], (got_a, got_b, got_c)[k], first_send.at[k], first_recv.at[k])
        for k in range(3)
    ]

    def exchange(a):
        units = pl.ds(81 * a, 81)
        return send_to(sibling(), dw.at[1 - core, :, units], pair.at[:, units], pair_sems, a)

    def both_cores(plane, start, count):
        units = pl.ds(start, count)
        return dw[core, plane, units] + pair[plane, units]

    def scatter(copy, a):
        copy.wait_recv()
        for plane in range(2):
            for target, at, start, count in pieces(plane):
                if ready(start, count) == a:
                    firsts[plane][target, at : at + count] = both_cores(plane, start, count)
            scatters[plane].start(a)
        chips = [q for q, (_, _, start, count) in enumerate(pieces(2)) if ready(start, count) == a]

        @pl.loop(chips[0], chips[-1] + 1)
        def _(q):
            at = pl.ds((q // 4) * 5, 5)
            first_c[q % 4, at] = both_cores(2, window(1, q, 5), 5)

        scatters[2].start(a)

    def input_terms(view_row, first):
        rim(gp, 1, view_row)
        unfold(gp, xc.at[view_row], view_row)
        correlate(xc.at[view_row], wt, acc, view_row, first)

    kernel_terms(xc, gall, dw, 0)
    pairs = [exchange(0)]
    for a in (1, 2):
        kernel_terms(xc, gall, dw, a)
        pairs.append(exchange(a))
        scatter(pairs[a - 1], a - 1)
    for copy, _, got in jobs[:2]:
        pl.when(got)(copy.wait_recv)
    input_terms(1, True)
    scatter(pairs[2], 2)
    for copy, _, got in jobs[2:]:
        pl.when(got)(copy.wait_recv)
    input_terms(0, False)

    for ring in scatters:
        ring.wait()
    sum_a[...] = scatters[0].total(pl.ds(0, 64))
    for x in range(4):
        sum_b[x] = scatters[1].total(pl.ds(BAND * x, BAND))

    @pl.loop(0, 16)
    def _(p):
        sum_c[p // 4, p % 4] = scatters[2].total(pl.ds(5 * p, 5))

    chips = (chip_x, chip_y, chip_z)
    column = chip_x * 4 + chip_y

    def next_part(plane, to):
        if plane == 0:
            return sum_a.at[pl.ds(window(4, chip_x * 4 + to, BAND) - window(16, chip_x, 64), BAND)]
        return (next_b if plane == 1 else sum_c).at[to]

    for x in range(4):
        for z in range(4):
            start = window(1, x * 16 + chip_y * 4 + z, 5) - window(4, x * 4 + chip_y, BAND)
            next_b[z, x] = sum_b[x, pl.ds(start, 5)]
    sends = []
    for step in (2, 1, 3):
        for plane, axis in enumerate((1, 2, 0)):
            src = next_part(plane, lax.rem(chips[axis] + step, 4))
            dst = (near_a, near_b, near_c)[plane].at[step - 1]
            sends.append(send_to(peer_along(axis, step), src, dst, next_sems.at[plane], step - 1))

    input_terms(2, False)
    total = shifted(acc[0], 1) + acc[1] + shifted(acc[2], -1)
    for s in range(S):
        block = total[s * T * V : (s + 1) * T * V].reshape(T, V, C)
        gi_out[0, :, s] = jnp.swapaxes(block, 0, 1).astype(BF16)
    gcopy = pltpu.make_async_copy(gi_out, gi_ref, in_sems.at[2])
    gcopy.start()

    for copy in sends:
        copy.wait_recv()

    def near_total(plane, near):
        value = next_part(plane, chips[(1, 2, 0)[plane]])[...].astype(F32)
        for k in range(3):
            value += near[k].astype(F32)
        return value.astype(BF16)

    last_a[...] = near_total(0, near_a)
    last_b[...] = near_total(1, near_b)
    last_c[...] = near_total(2, near_c)

    def last_part(plane, to):
        if plane == 0:
            return last_a.at[pl.ds(window(1, column * 4 + to, 5) - window(4, column, BAND), 5)]
        return (last_b if plane == 1 else last_c).at[to]

    lasts = []
    for step in (2, 1, 3):
        for plane, axis in enumerate((2, 0, 1)):
            src = last_part(plane, lax.rem(chips[axis] + step, 4))
            slot = 3 * plane + step - 1
            lasts.append(send_to(peer_along(axis, step), src, ends.at[slot], last_sems, slot))
    for copy, sent, _ in jobs:
        pl.when(sent)(copy.wait_send)
    for copy in (*pairs, *sends):
        copy.wait_send()
    for copy in lasts:
        copy.wait()
    for plane, axis in enumerate((2, 0, 1)):
        value = last_part(plane, chips[axis])[...].astype(F32)
        for k in range(3):
            value += ends[3 * plane + k].astype(F32)
        both[core, plane] = value
    gcopy.wait()
    send_to(sibling(), both.at[core], both.at[core], core_sems, 0).wait()

    for k in range(2):
        for unit in range(5):
            row = 64 * unit + 32 * k
            tail = both[k, 2, unit]
            left[row : row + 16] = both[k, 0, unit]
            left[row + 16 : row + 32] = both[k, 1, unit]
            right[row : row + 16] = tail
            right[row + 16 : row + 32] = pltpu.roll(tail, 64, 1)
    count = 160
    odd = pltpu.roll(left[pl.ds(1, count, stride=2), :], 64, 1)
    head = lax.broadcasted_iota(jnp.int32, (count, 128), 1) < 64
    flat[pl.ds(0, count, stride=3), :] = left[pl.ds(0, count, stride=2), :]
    flat[pl.ds(1, count, stride=3), :] = jnp.where(head, right[pl.ds(0, count, stride=2), :], odd)
    rest = pltpu.roll(right[pl.ds(1, count, stride=2), :], 64, 1)
    flat[pl.ds(2, count, stride=3), :] = jnp.where(head, odd, rest)
    flat[480:488] = jnp.zeros((8, 128), F32)
    begin = (column * 4 + chip_z) * (243 * C) + core * SHARE - window(1, column * 4 + chip_z, 5) * (64 * C)
    row, turn_by = begin // 128, begin % 128
    held = gk_ref.shape[0]
    before = lax.broadcasted_iota(jnp.int32, (held, 128), 1) < 128 - turn_by
    this = pltpu.roll(flat[pl.ds(row, held), :], (128 - turn_by) % 128, 1)
    after = pltpu.roll(flat[pl.ds(row + 1, held), :], (128 - turn_by) % 128, 1)
    gk_ref[...] = jnp.where(before, this, after)


def local(inputs, cotangent, kernel, moment_one, moment_two):
    vmem = pl.BlockSpec(memory_space=pltpu.VMEM)
    anywhere = pl.BlockSpec(memory_space=pl.ANY)
    padded = (3, S + 2, T + 2, V, LANES)
    tiles = lambda *lead: pltpu.VMEM((*lead, *TILE), BF16)
    dma = lambda *shape: pltpu.SemaphoreType.DMA(shape)
    long_kernel = pltpu.VMEM((ROWS + WIDE - GROUP, C), BF16)
    grad_input, share_grad = pl.pallas_call(
        step_kernel,
        out_shape=(
            jax.ShapeDtypeStruct(inputs.shape, BF16),
            jax.ShapeDtypeStruct((184, 128), F32),
        ),
        in_specs=[anywhere, anywhere, anywhere],
        out_specs=(anywhere, vmem),
        scratch_shapes=[
            *(pltpu.VMEM(inputs.shape, BF16) for _ in range(3)),
            pltpu.VMEM((2, 2, T, V, 384), BF16),
            pltpu.VMEM((2, 2, 2, V, 384), BF16),
            pltpu.VMEM((2, 2, 2, T, V, 384), BF16),
            pltpu.VMEM((2, 3, 2, 2, V, 384), BF16),
            pltpu.VMEM(padded, BF16),
            pltpu.VMEM(padded, BF16),
            pltpu.VMEM((3, CELLS, WIDE), BF16),
            long_kernel,
            long_kernel,
            pltpu.VMEM((3, CELLS, C), F32),
            pltpu.VMEM((CELLS, 768), BF16),
            tiles(2, 3, UNITS),
            tiles(3, UNITS),
            *(tiles(4, n) for n in LENGTHS),
            *(tiles(3, n) for n in LENGTHS),
            tiles(64),
            tiles(4, BAND),
            tiles(4, 4, 5),
            tiles(4, 4, 5),
            tiles(3, BAND),
            tiles(3, 4, 5),
            tiles(3, 4, 5),
            tiles(BAND),
            tiles(4, 5),
            tiles(4, 5),
            tiles(9, 5),
            pltpu.VMEM((2, 3, 5, *TILE), F32),
            pltpu.VMEM((320, 128), F32),
            pltpu.VMEM((320, 128), F32),
            pltpu.VMEM((488, 128), F32),
            dma(2, 8),
            dma(2, 8),
            dma(3),
            pltpu.SemaphoreType.DMA,
            dma(2, 3),
            dma(3, 4, 3),
            dma(3, 3, 3),
            dma(3, 2, 3),
            dma(2, 9),
            dma(2, 1),
        ],
        compiler_params=pltpu.CompilerParams(
            vmem_limit_bytes=56 * 1024 * 1024, collective_id=0, has_side_effects=True
        ),
        cost_estimate=pl.CostEstimate(flops=9 * 10**9, bytes_accessed=10**7, transcendentals=10**5),
    )(inputs, cotangent, kernel.reshape(ROWS, C))
    share_len = moment_one.shape[0]
    share = share_grad.reshape(-1)[:share_len]
    pixels = CELLS * lax.axis_size("ang") * lax.axis_size("sp")
    grad_share = share * F32(1.0 / math.sqrt(pixels))
    moment_next = beta_one * moment_one + (1.0 - beta_one) * grad_share
    square_next = beta_two * moment_two + (1.0 - beta_two) * grad_share * grad_share
    first_fix = 1.0 - beta_one**adam_step
    second_fix = 1.0 - beta_two**adam_step
    direction = moment_next / first_fix / (jnp.sqrt(square_next / second_fix) + epsilon)
    return (grad_input, moment_next, square_next, direction)


def solution(mesh):
    field = P("ang", None, None, "sp", None)
    share = P(("ang", "sp"))
    return jax.shard_map(
        local,
        mesh=mesh,
        in_specs=(field, field, P(), share, share),
        out_specs=(field, share, share, share),
        check_vma=False,
    )
```

```python
import functools
import math

import jax
import jax.numpy as jnp
from jax import lax
from jax.experimental import pallas as pl
from jax.experimental.pallas import tpu as pltpu
from jax.sharding import PartitionSpec as P

beta_one = 0.9
beta_two = 0.999
adam_step = 100
epsilon = 1e-08

MESH = pl.DeviceIdType.MESH
F32 = jnp.float32
BF16 = jnp.bfloat16

V, S, T, C = 16, 4, 8, 192
CELLS = V * S * T
GROUP = 9 * C
WIDE = GROUP + 64
ROWS = 9 * GROUP
LANES = 256
SIDES = ((0, 1), (0, -1), (1, 0), (-1, 0), (1, 1), (1, -1), (-1, 1), (-1, -1))


def start_halo(field, packed, edges, rows_in, cols_in, send, recv):
    rows, cols = lax.axis_size("ang"), lax.axis_size("sp")
    row, col = lax.axis_index("ang"), lax.axis_index("sp")
    for j in range(2):
        first = field[1, 1 + 2 * j, 1 : 1 + T].reshape(T * V, LANES)
        second = pltpu.roll(field[1, 2 + 2 * j, 1 : 1 + T].reshape(T * V, LANES), 64, 1)
        packed[j, :, :, 0:128] = first[:, :128].reshape(T, V, 128)
        packed[j, :, :, 128:256] = (first[:, 128:] + second[:, :128]).reshape(T, V, 128)
        packed[j, :, :, 256:384] = second[:, 128:].reshape(T, V, 128)
        edges[0, j] = packed[j, 0]
        edges[1, j] = packed[j, T - 1]
    jobs = []
    for side, (da, ds) in enumerate(SIDES):
        if ds == 0:
            src, dst = packed, rows_in.at[(1 - da) // 2]
        elif ds == 1:
            src, dst = edges.at[1], cols_in.at[1 - da, 0]
        else:
            src, dst = edges.at[0], cols_in.at[1 - da, 1]
        sent = (row + da >= 0) & (row + da < rows) & (col + ds >= 0) & (col + ds < cols)
        got = (row - da >= 0) & (row - da < rows) & (col - ds >= 0) & (col - ds < cols)
        copy = pltpu.make_async_remote_copy(
            src_ref=src,
            dst_ref=dst,
            send_sem=send.at[side],
            recv_sem=recv.at[side],
            device_id=(row + da, col + ds),
            device_id_type=MESH,
        )
        jobs.append((copy, sent, got))
    for side in (4, 5, 6, 7, 2, 3, 0, 1):
        pl.when(jobs[side][1])(jobs[side][0].start)
    return jobs


def unpack(value):
    lane = lax.broadcasted_iota(jnp.int32, (value.shape[0], LANES), 1)
    keep = (lane < C).astype(F32).astype(BF16)
    return value[:, 0:LANES] * keep, pltpu.roll(value[:, 128:384], 192, 1) * keep


def place_rim(field, rows_in, cols_in, view_row):
    for j in range(2):
        if view_row != 1:
            pair = unpack(rows_in[view_row // 2, j].reshape(T * V, 384))
            for k in range(2):
                field[view_row, 1 + 2 * j + k, 1 : 1 + T] = pair[k].reshape(T, V, LANES)
        for side, at in ((0, 0), (1, T + 1)):
            pair = unpack(cols_in[view_row, side, j])
            for k in range(2):
                field[view_row, 1 + 2 * j + k, at] = pair[k]


def greet():
    rows, cols = lax.axis_size("ang"), lax.axis_size("sp")
    row, col = lax.axis_index("ang"), lax.axis_index("sp")
    barrier = pltpu.get_barrier_semaphore()

    def signal(peer):
        pl.semaphore_signal(barrier, inc=1, device_id=peer, device_id_type=MESH)

    for da, ds in SIDES:
        there = (row + da >= 0) & (row + da < rows) & (col + ds >= 0) & (col + ds < cols)
        pl.when(there)(functools.partial(signal, (row + da, col + ds)))
    for axis in range(3):
        for step in range(1, 4):
            signal(peer_along(axis, step))
    signal(sibling())
    tall = 1 + (row > 0).astype(jnp.int32) + (row < rows - 1).astype(jnp.int32)
    broad = 1 + (col > 0).astype(jnp.int32) + (col < cols - 1).astype(jnp.int32)
    return tall * broad + 9


def place():
    row, col = lax.axis_index("ang"), lax.axis_index("sp")
    return lax.div(row, 4), lax.rem(row, 4), lax.div(col, 2), lax.rem(col, 2)


def device(at):
    return (at[0] * 4 + at[1], at[2] * 2 + at[3])


def peer_along(axis, step):
    at = list(place())
    at[axis] = lax.rem(at[axis] + step, 4)
    return device(at)


def sibling():
    x, y, z, core = place()
    return (x * 4 + y, z * 2 + 1 - core)


def unfold(field, taps, view_row):
    @pl.loop(0, S)
    def _(s):
        def low(k):
            block = field[view_row, s + k // 3, pl.ds(k % 3, T)]
            return block.reshape(T * V, LANES)

        out = pl.ds(pl.multiple_of(s * T * V, T * V), T * V)
        for pair in range(4):
            first = low(2 * pair)
            second = pltpu.roll(low(2 * pair + 1), 64, 1)
            at = 384 * pair
            taps[out, at : at + 128] = first[:, :128]
            taps[out, at + 128 : at + 256] = first[:, 128:] + second[:, :128]
            taps[out, at + 256 : at + 384] = second[:, 128:]
        taps[out, 1536:1792] = low(8)


def shifted(values, by):
    rows = values.shape[0]
    view = lax.broadcasted_iota(jnp.int32, values.shape, 0) % V
    keep = (view >= by) if by > 0 else (view < V + by)
    return jnp.where(keep, pltpu.roll(values, by % rows, 0), jnp.zeros_like(values))


def correlate(taps, weights, acc, view_row, first):
    @pl.loop(0, 3)
    def _(b):
        at = pl.multiple_of((view_row * 3 + b) * GROUP, 64)
        term = jnp.dot(taps[...], weights[pl.ds(at, WIDE), :], preferred_element_type=F32)
        if first:
            acc[b] = term
        else:
            acc[b] += term


UNITS = 243
TILE = (16, 128)
SHARE = 243 * C // 2
BAND = 17
LENGTHS = (64, 4 * BAND, 80)


def window(chips, index, count):
    start = (index * (chips * 243)) // 64
    if isinstance(index, int):
        return min(start, UNITS - count)
    return jnp.minimum(start, UNITS - count)


def kernel_terms(taps, grads, dw, a):
    for part in range(5):
        at, size = 384 * part, (384 if part < 4 else 192)
        term = lax.dot_general(
            taps[a, :, at : at + (size if part < 4 else 256)],
            grads[...],
            (((0,), (0,)), ((), ())),
            preferred_element_type=F32,
        )
        for b in range(3):
            count = size // 64
            block = term[0:size, 256 * b : 256 * b + 256].reshape(count, 2, 2, 16, 256)
            dst = pl.ds((3 * a + b) * 27 + 6 * part, count)
            for core in range(2):
                low, high = block[:, core, 0], block[:, core, 1]
                dw[core, 0, dst] = low[:, :, :128].astype(BF16)
                dw[core, 1, dst] = high[:, :, :128].astype(BF16)
                tail = pltpu.roll(high[:, :, 128:].reshape(count * 16, 128), 64, 1)
                dw[core, 2, dst] = (low[:, :, 128:] + tail.reshape(count, 16, 128)).astype(BF16)


def send_to(peer, src, dst, sems, index):
    copy = pltpu.make_async_remote_copy(
        src_ref=src,
        dst_ref=dst,
        send_sem=sems.at[0, index],
        recv_sem=sems.at[1, index],
        device_id=peer,
        device_id_type=MESH,
    )
    copy.start()
    return copy


def pieces(plane):
    if plane == 0:
        found = []
        for x in range(4):
            start = window(16, x, 64)
            for a in range(3):
                low, high = max(start, 81 * a), min(start + 64, 81 * a + 81)
                if low < high:
                    found.append((x, low - start, low, high - low))
        return found
    if plane == 1:
        return [(p % 4, BAND * (p // 4), window(4, p, BAND), BAND) for p in range(16)]
    return [(q % 4, 5 * (q // 4), window(1, q, 5), 5) for q in range(64)]


def ready(start, count):
    return (start + count - 1) // 81


def spans(plane):
    found = {}
    for target, at, start, count in pieces(plane):
        key = (target, ready(start, count))
        low, size = found.get(key, (at, 0))
        found[key] = (low, size + count)
    return found


class Scatter:
    def __init__(self, plane, terms, got, send, recv):
        self.axis, self.terms, self.got, self.send, self.recv = plane, terms, got, send, recv
        self.me = place()[plane]
        self.spans = spans(plane)

    def copy(self, target, a, slot):
        low, size = self.spans[target, a]
        at = list(place())
        at[self.axis] = target
        return pltpu.make_async_remote_copy(
            src_ref=self.terms.at[target, pl.ds(low, size)],
            dst_ref=self.got.at[slot, pl.ds(low, size)],
            send_sem=self.send.at[target, a],
            recv_sem=self.recv.at[slot, a],
            device_id=device(at),
            device_id_type=MESH,
        )

    def start(self, now):
        for target, a in self.spans:
            if a == now:
                slot = lax.rem(self.me + 3 - target, 4)

                @pl.when(self.me != target)
                def _():
                    self.copy(target, a, slot).start()

    def wait(self):
        for target, a in self.spans:

            @pl.when(self.me == target)
            def _():
                for slot in range(3):
                    self.copy(target, a, slot).wait_recv()

        for target, a in self.spans:

            @pl.when(self.me != target)
            def _():
                self.copy(target, a, 0).wait_send()

    def total(self, units):
        value = self.terms[self.me, units].astype(F32)
        for slot in range(3):
            value += self.got[slot, units].astype(F32)
        return value.astype(BF16)


def step_kernel(
    x_hbm, cot_hbm, w_ref, gi_ref, gk_ref,
    x_ref, cot_ref, gi_out, packed, edges, rows_in, cols_in, xp, gp, xc, wv, wt, acc, gall, dw, pair,
    first_a, first_b, first_c, got_a, got_b, got_c, sum_a, sum_b, sum_c,
    next_b, near_a, near_b, near_c, last_a, last_b, last_c, ends, both, left, right, flat,
    halo_send, halo_recv, in_sems, wsem, pair_sems, first_send, first_recv, next_sems, last_sems, core_sems,
):
    chip_x, chip_y, chip_z, core = place()
    xcopy = pltpu.make_async_copy(x_hbm, x_ref, in_sems.at[0])
    ccopy = pltpu.make_async_copy(cot_hbm, cot_ref, in_sems.at[1])
    wcopy = pltpu.make_async_copy(w_ref, wv.at[pl.ds(0, ROWS)], wsem)
    xcopy.start()
    wcopy.start()
    ccopy.start()
    rows_in[...] = jnp.zeros_like(rows_in)
    cols_in[...] = jnp.zeros_like(cols_in)
    peers = greet()
    xp[...] = jnp.zeros_like(xp)
    gp[...] = jnp.zeros_like(gp)
    rest = pl.ds(ROWS, WIDE - GROUP)
    wv[rest, :] = jnp.zeros((WIDE - GROUP, C), BF16)
    wt[rest, :] = jnp.zeros((WIDE - GROUP, C), BF16)
    xcopy.wait()
    for s in range(S):
        block = jnp.swapaxes(x_ref[0, :, s].astype(F32), 0, 1).astype(BF16)
        xp[1, 1 + s, 1 : 1 + T, :, 0:C] = block

    def halo(field, k):
        pads = (packed.at[k], edges.at[k], rows_in.at[k], cols_in.at[k])
        return start_halo(field, *pads, halo_send.at[k], halo_recv.at[k])

    def rim(field, k, view_row):
        place_rim(field, rows_in.at[k], cols_in.at[k], view_row)

    pl.semaphore_wait(pltpu.get_barrier_semaphore(), peers)
    jobs = halo(xp, 0)
    wcopy.wait()

    def turn(low, high):
        @pl.loop(low, high)
        def _(tap):
            src = pl.ds(pl.multiple_of((80 - tap) * C, 64), C)
            dst = pl.ds(pl.multiple_of(tap * C, 64), C)
            wt[dst, :] = wv[src, :].T

    turn(0, 40)
    for copy, _, got in jobs[:2]:
        pl.when(got)(copy.wait_recv)
    rim(xp, 0, 1)
    unfold(xp, xc.at[1], 1)
    correlate(xc.at[1], wv, acc, 1, True)
    turn(40, 60)
    for copy, _, got in jobs[2:]:
        pl.when(got)(copy.wait_recv)
    for view_row in (0, 2):
        rim(xp, 0, view_row)
        unfold(xp, xc.at[view_row], view_row)
        correlate(xc.at[view_row], wv, acc, view_row, False)
    for copy, sent, _ in jobs:
        pl.when(sent)(copy.wait_send)

    ccopy.wait()
    preact = shifted(acc[0], 1) + acc[1] + shifted(acc[2], -1)
    for s in range(S):
        upstream = jnp.swapaxes(cot_ref[0, :, s].astype(F32), 0, 1).reshape(T * V, C)
        pre = preact[s * T * V : (s + 1) * T * V]
        sigmoid = jax.nn.sigmoid(pre)
        grad = upstream * sigmoid * (1.0 + pre * (1.0 - sigmoid))
        gp[1, 1 + s, 1 : 1 + T, :, 0:C] = grad.astype(BF16).reshape(T, V, C)
    jobs = halo(gp, 1)
    grad = gp[1, 1 : 1 + S, 1 : 1 + T].reshape(CELLS, LANES)
    wide = grad.astype(F32)
    gall[:, 0:256] = shifted(wide, -1).astype(BF16)
    gall[:, 256:512] = grad
    gall[:, 512:768] = shifted(wide, 1).astype(BF16)

    firsts = (first_a, first_b, first_c)
    scatters = [
        Scatter(k, firsts[k], (got_a, got_b, got_c)[k], first_send.at[k], first_recv.at[k])
        for k in range(3)
    ]

    def exchange(a):
        units = pl.ds(81 * a, 81)
        return send_to(sibling(), dw.at[1 - core, :, units], pair.at[:, units], pair_sems, a)

    def both_cores(plane, start, count):
        units = pl.ds(start, count)
        return dw[core, plane, units] + pair[plane, units]

    def scatter(copy, a):
        copy.wait_recv()
        for plane in range(2):
            for target, at, start, count in pieces(plane):
                if ready(start, count) == a:
                    firsts[plane][target, at : at + count] = both_cores(plane, start, count)
            scatters[plane].start(a)
        chips = [q for q, (_, _, start, count) in enumerate(pieces(2)) if ready(start, count) == a]

        @pl.loop(chips[0], chips[-1] + 1)
        def _(q):
            at = pl.ds((q // 4) * 5, 5)
            first_c[q % 4, at] = both_cores(2, window(1, q, 5), 5)

        scatters[2].start(a)

    def input_terms(view_row, first):
        rim(gp, 1, view_row)
        unfold(gp, xc.at[view_row], view_row)
        correlate(xc.at[view_row], wt, acc, view_row, first)

    kernel_terms(xc, gall, dw, 0)
    pairs = [exchange(0)]
    for a in (1, 2):
        kernel_terms(xc, gall, dw, a)
        pairs.append(exchange(a))
        scatter(pairs[a - 1], a - 1)
    turn(60, 81)
    for copy, _, got in jobs[:2]:
        pl.when(got)(copy.wait_recv)
    input_terms(1, True)
    scatter(pairs[2], 2)
    for copy, _, got in jobs[2:]:
        pl.when(got)(copy.wait_recv)
    input_terms(0, False)

    for ring in scatters:
        ring.wait()
    sum_a[...] = scatters[0].total(pl.ds(0, 64))
    for x in range(4):
        sum_b[x] = scatters[1].total(pl.ds(BAND * x, BAND))

    @pl.loop(0, 16)
    def _(p):
        sum_c[p // 4, p % 4] = scatters[2].total(pl.ds(5 * p, 5))

    chips = (chip_x, chip_y, chip_z)
    column = chip_x * 4 + chip_y

    def next_part(plane, to):
        if plane == 0:
            return sum_a.at[pl.ds(window(4, chip_x * 4 + to, BAND) - window(16, chip_x, 64), BAND)]
        return (next_b if plane == 1 else sum_c).at[to]

    for x in range(4):
        for z in range(4):
            start = window(1, x * 16 + chip_y * 4 + z, 5) - window(4, x * 4 + chip_y, BAND)
            next_b[z, x] = sum_b[x, pl.ds(start, 5)]
    sends = []
    for step in (2, 1, 3):
        for plane, axis in enumerate((1, 2, 0)):
            src = next_part(plane, lax.rem(chips[axis] + step, 4))
            dst = (near_a, near_b, near_c)[plane].at[step - 1]
            sends.append(send_to(peer_along(axis, step), src, dst, next_sems.at[plane], step - 1))

    input_terms(2, False)
    total = shifted(acc[0], 1) + acc[1] + shifted(acc[2], -1)
    for s in range(S):
        block = total[s * T * V : (s + 1) * T * V].reshape(T, V, C)
        gi_out[0, :, s] = jnp.swapaxes(block, 0, 1).astype(BF16)
    gcopy = pltpu.make_async_copy(gi_out, gi_ref, in_sems.at[2])
    gcopy.start()

    for copy in sends:
        copy.wait_recv()

    def near_total(plane, near):
        value = next_part(plane, chips[(1, 2, 0)[plane]])[...].astype(F32)
        for k in range(3):
            value += near[k].astype(F32)
        return value.astype(BF16)

    last_a[...] = near_total(0, near_a)
    last_b[...] = near_total(1, near_b)
    last_c[...] = near_total(2, near_c)

    def last_part(plane, to):
        if plane == 0:
            return last_a.at[pl.ds(window(1, column * 4 + to, 5) - window(4, column, BAND), 5)]
        return (last_b if plane == 1 else last_c).at[to]

    lasts = []
    for step in (2, 1, 3):
        for plane, axis in enumerate((2, 0, 1)):
            src = last_part(plane, lax.rem(chips[axis] + step, 4))
            slot = 3 * plane + step - 1
            lasts.append(send_to(peer_along(axis, step), src, ends.at[slot], last_sems, slot))
    for copy, sent, _ in jobs:
        pl.when(sent)(copy.wait_send)
    for copy in (*pairs, *sends):
        copy.wait_send()
    for copy in lasts:
        copy.wait()
    for plane, axis in enumerate((2, 0, 1)):
        value = last_part(plane, chips[axis])[...].astype(F32)
        for k in range(3):
            value += ends[3 * plane + k].astype(F32)
        both[core, plane] = value
    gcopy.wait()
    send_to(sibling(), both.at[core], both.at[core], core_sems, 0).wait()

    for k in range(2):
        for unit in range(5):
            row = 64 * unit + 32 * k
            tail = both[k, 2, unit]
            left[row : row + 16] = both[k, 0, unit]
            left[row + 16 : row + 32] = both[k, 1, unit]
            right[row : row + 16] = tail
            right[row + 16 : row + 32] = pltpu.roll(tail, 64, 1)
    count = 160
    odd = pltpu.roll(left[pl.ds(1, count, stride=2), :], 64, 1)
    head = lax.broadcasted_iota(jnp.int32, (count, 128), 1) < 64
    flat[pl.ds(0, count, stride=3), :] = left[pl.ds(0, count, stride=2), :]
    flat[pl.ds(1, count, stride=3), :] = jnp.where(head, right[pl.ds(0, count, stride=2), :], odd)
    rest = pltpu.roll(right[pl.ds(1, count, stride=2), :], 64, 1)
    flat[pl.ds(2, count, stride=3), :] = jnp.where(head, odd, rest)
    flat[480:488] = jnp.zeros((8, 128), F32)
    begin = (column * 4 + chip_z) * (243 * C) + core * SHARE - window(1, column * 4 + chip_z, 5) * (64 * C)
    row, turn_by = begin // 128, begin % 128
    held = gk_ref.shape[0]
    before = lax.broadcasted_iota(jnp.int32, (held, 128), 1) < 128 - turn_by
    this = pltpu.roll(flat[pl.ds(row, held), :], (128 - turn_by) % 128, 1)
    after = pltpu.roll(flat[pl.ds(row + 1, held), :], (128 - turn_by) % 128, 1)
    gk_ref[...] = jnp.where(before, this, after)


def local(inputs, cotangent, kernel, moment_one, moment_two):
    vmem = pl.BlockSpec(memory_space=pltpu.VMEM)
    anywhere = pl.BlockSpec(memory_space=pl.ANY)
    padded = (3, S + 2, T + 2, V, LANES)
    tiles = lambda *lead: pltpu.VMEM((*lead, *TILE), BF16)
    dma = lambda *shape: pltpu.SemaphoreType.DMA(shape)
    long_kernel = pltpu.VMEM((ROWS + WIDE - GROUP, C), BF16)
    grad_input, share_grad = pl.pallas_call(
        step_kernel,
        out_shape=(
            jax.ShapeDtypeStruct(inputs.shape, BF16),
            jax.ShapeDtypeStruct((184, 128), F32),
        ),
        in_specs=[anywhere, anywhere, anywhere],
        out_specs=(anywhere, vmem),
        scratch_shapes=[
            *(pltpu.VMEM(inputs.shape, BF16) for _ in range(3)),
            pltpu.VMEM((2, 2, T, V, 384), BF16),
            pltpu.VMEM((2, 2, 2, V, 384), BF16),
            pltpu.VMEM((2, 2, 2, T, V, 384), BF16),
            pltpu.VMEM((2, 3, 2, 2, V, 384), BF16),
            pltpu.VMEM(padded, BF16),
            pltpu.VMEM(padded, BF16),
            pltpu.VMEM((3, CELLS, WIDE), BF16),
            long_kernel,
            long_kernel,
            pltpu.VMEM((3, CELLS, C), F32),
            pltpu.VMEM((CELLS, 768), BF16),
            tiles(2, 3, UNITS),
            tiles(3, UNITS),
            *(tiles(4, n) for n in LENGTHS),
            *(tiles(3, n) for n in LENGTHS),
            tiles(64),
            tiles(4, BAND),
            tiles(4, 4, 5),
            tiles(4, 4, 5),
            tiles(3, BAND),
            tiles(3, 4, 5),
            tiles(3, 4, 5),
            tiles(BAND),
            tiles(4, 5),
            tiles(4, 5),
            tiles(9, 5),
            pltpu.VMEM((2, 3, 5, *TILE), F32),
            pltpu.VMEM((320, 128), F32),
            pltpu.VMEM((320, 128), F32),
            pltpu.VMEM((488, 128), F32),
            dma(2, 8),
            dma(2, 8),
            dma(3),
            pltpu.SemaphoreType.DMA,
            dma(2, 3),
            dma(3, 4, 3),
            dma(3, 3, 3),
            dma(3, 2, 3),
            dma(2, 9),
            dma(2, 1),
        ],
        compiler_params=pltpu.CompilerParams(
            vmem_limit_bytes=56 * 1024 * 1024, collective_id=0, has_side_effects=True
        ),
        cost_estimate=pl.CostEstimate(flops=9 * 10**9, bytes_accessed=10**7, transcendentals=10**5),
    )(inputs, cotangent, kernel.reshape(ROWS, C))
    share_len = moment_one.shape[0]
    share = share_grad.reshape(-1)[:share_len]
    pixels = CELLS * lax.axis_size("ang") * lax.axis_size("sp")
    grad_share = share * F32(1.0 / math.sqrt(pixels))
    moment_next = beta_one * moment_one + (1.0 - beta_one) * grad_share
    square_next = beta_two * moment_two + (1.0 - beta_two) * grad_share * grad_share
    first_fix = 1.0 - beta_one**adam_step
    second_fix = 1.0 - beta_two**adam_step
    direction = moment_next / first_fix / (jnp.sqrt(square_next / second_fix) + epsilon)
    return (grad_input, moment_next, square_next, direction)


def solution(mesh):
    field = P("ang", None, None, "sp", None)
    share = P(("ang", "sp"))
    return jax.shard_map(
        local,
        mesh=mesh,
        in_specs=(field, field, P(), share, share),
        out_specs=(field, share, share, share),
        check_vma=False,
    )
```

```python
import functools
import math

import jax
import jax.numpy as jnp
from jax import lax
from jax.experimental import pallas as pl
from jax.experimental.pallas import tpu as pltpu
from jax.sharding import PartitionSpec as P

beta_one = 0.9
beta_two = 0.999
adam_step = 100
epsilon = 1e-08

MESH = pl.DeviceIdType.MESH
F32 = jnp.float32
BF16 = jnp.bfloat16

V, S, T, C = 16, 4, 8, 192
CELLS = V * S * T
GROUP = 9 * C
WIDE = GROUP + 64
ROWS = 9 * GROUP
LANES = 256
SIDES = ((0, 1), (0, -1), (1, 0), (-1, 0), (1, 1), (1, -1), (-1, 1), (-1, -1))


def start_halo(field, packed, edges, rows_in, cols_in, send, recv):
    rows, cols = lax.axis_size("ang"), lax.axis_size("sp")
    row, col = lax.axis_index("ang"), lax.axis_index("sp")
    for j in range(2):
        first = field[1, 1 + 2 * j, 1 : 1 + T].reshape(T * V, LANES)
        second = pltpu.roll(field[1, 2 + 2 * j, 1 : 1 + T].reshape(T * V, LANES), 64, 1)
        packed[j, :, :, 0:128] = first[:, :128].reshape(T, V, 128)
        packed[j, :, :, 128:256] = (first[:, 128:] + second[:, :128]).reshape(T, V, 128)
        packed[j, :, :, 256:384] = second[:, 128:].reshape(T, V, 128)
        edges[0, j] = packed[j, 0]
        edges[1, j] = packed[j, T - 1]
    jobs = []
    for side, (da, ds) in enumerate(SIDES):
        if ds == 0:
            src, dst = packed, rows_in.at[(1 - da) // 2]
        elif ds == 1:
            src, dst = edges.at[1], cols_in.at[1 - da, 0]
        else:
            src, dst = edges.at[0], cols_in.at[1 - da, 1]
        sent = (row + da >= 0) & (row + da < rows) & (col + ds >= 0) & (col + ds < cols)
        got = (row - da >= 0) & (row - da < rows) & (col - ds >= 0) & (col - ds < cols)
        copy = pltpu.make_async_remote_copy(
            src_ref=src,
            dst_ref=dst,
            send_sem=send.at[side],
            recv_sem=recv.at[side],
            device_id=(row + da, col + ds),
            device_id_type=MESH,
        )
        jobs.append((copy, sent, got))
    for side in (4, 5, 6, 7, 2, 3, 0, 1):
        pl.when(jobs[side][1])(jobs[side][0].start)
    return jobs


def unpack(value):
    lane = lax.broadcasted_iota(jnp.int32, (value.shape[0], LANES), 1)
    keep = (lane < C).astype(F32).astype(BF16)
    return value[:, 0:LANES] * keep, pltpu.roll(value[:, 128:384], 192, 1) * keep


def place_rim(field, rows_in, cols_in, view_row):
    for j in range(2):
        if view_row != 1:
            pair = unpack(rows_in[view_row // 2, j].reshape(T * V, 384))
            for k in range(2):
                field[view_row, 1 + 2 * j + k, 1 : 1 + T] = pair[k].reshape(T, V, LANES)
        for side, at in ((0, 0), (1, T + 1)):
            pair = unpack(cols_in[view_row, side, j])
            for k in range(2):
                field[view_row, 1 + 2 * j + k, at] = pair[k]


def greet():
    rows, cols = lax.axis_size("ang"), lax.axis_size("sp")
    row, col = lax.axis_index("ang"), lax.axis_index("sp")
    barrier = pltpu.get_barrier_semaphore()

    def signal(peer):
        pl.semaphore_signal(barrier, inc=1, device_id=peer, device_id_type=MESH)

    for da, ds in SIDES:
        there = (row + da >= 0) & (row + da < rows) & (col + ds >= 0) & (col + ds < cols)
        pl.when(there)(functools.partial(signal, (row + da, col + ds)))
    for axis in range(3):
        for step in range(1, 4):
            signal(peer_along(axis, step))
    signal(sibling())
    tall = 1 + (row > 0).astype(jnp.int32) + (row < rows - 1).astype(jnp.int32)
    broad = 1 + (col > 0).astype(jnp.int32) + (col < cols - 1).astype(jnp.int32)
    return tall * broad + 9


def place():
    row, col = lax.axis_index("ang"), lax.axis_index("sp")
    return lax.div(row, 4), lax.rem(row, 4), lax.div(col, 2), lax.rem(col, 2)


def device(at):
    return (at[0] * 4 + at[1], at[2] * 2 + at[3])


def peer_along(axis, step):
    at = list(place())
    at[axis] = lax.rem(at[axis] + step, 4)
    return device(at)


def sibling():
    x, y, z, core = place()
    return (x * 4 + y, z * 2 + 1 - core)


def unfold(field, taps, view_row):
    @pl.loop(0, S)
    def _(s):
        def low(k):
            block = field[view_row, s + k // 3, pl.ds(k % 3, T)]
            return block.reshape(T * V, LANES)

        out = pl.ds(pl.multiple_of(s * T * V, T * V), T * V)
        for pair in range(4):
            first = low(2 * pair)
            second = pltpu.roll(low(2 * pair + 1), 64, 1)
            at = 384 * pair
            taps[out, at : at + 128] = first[:, :128]
            taps[out, at + 128 : at + 256] = first[:, 128:] + second[:, :128]
            taps[out, at + 256 : at + 384] = second[:, 128:]
        taps[out, 1536:1792] = low(8)


def shifted(values, by):
    rows = values.shape[0]
    view = lax.broadcasted_iota(jnp.int32, values.shape, 0) % V
    keep = (view >= by) if by > 0 else (view < V + by)
    return jnp.where(keep, pltpu.roll(values, by % rows, 0), jnp.zeros_like(values))


def correlate(taps, weights, acc, view_row, first):
    @pl.loop(0, 3)
    def _(b):
        at = pl.multiple_of((view_row * 3 + b) * GROUP, 64)
        term = jnp.dot(taps[...], weights[pl.ds(at, WIDE), :], preferred_element_type=F32)
        if first:
            acc[b] = term
        else:
            acc[b] += term


UNITS = 243
TILE = (16, 128)
BAND = 17
LENGTHS = (64, 4 * BAND, 80)


def window(chips, index, count):
    start = (index * (chips * 243)) // 64
    if isinstance(index, int):
        return min(start, UNITS - count)
    return jnp.minimum(start, UNITS - count)


def kernel_terms(taps, grads, dw, a):
    for part in range(5):
        at, size = 384 * part, (384 if part < 4 else 192)
        term = lax.dot_general(
            taps[a, :, at : at + (size if part < 4 else 256)],
            grads[...],
            (((0,), (0,)), ((), ())),
            preferred_element_type=F32,
        )
        for b in range(3):
            count = size // 64
            block = term[0:size, 256 * b : 256 * b + 256].reshape(count, 2, 2, 16, 256)
            dst = pl.ds((3 * a + b) * 27 + 6 * part, count)
            for core in range(2):
                low, high = block[:, core, 0], block[:, core, 1]
                dw[core, 0, dst] = low[:, :, :128].astype(BF16)
                dw[core, 1, dst] = high[:, :, :128].astype(BF16)
                tail = pltpu.roll(high[:, :, 128:].reshape(count * 16, 128), 64, 1)
                dw[core, 2, dst] = (low[:, :, 128:] + tail.reshape(count, 16, 128)).astype(BF16)


def send_to(peer, src, dst, sems, index):
    copy = pltpu.make_async_remote_copy(
        src_ref=src,
        dst_ref=dst,
        send_sem=sems.at[0, index],
        recv_sem=sems.at[1, index],
        device_id=peer,
        device_id_type=MESH,
    )
    copy.start()
    return copy


def pieces(plane):
    if plane == 0:
        found = []
        for x in range(4):
            start = window(16, x, 64)
            for a in range(3):
                low, high = max(start, 81 * a), min(start + 64, 81 * a + 81)
                if low < high:
                    found.append((x, low - start, low, high - low))
        return found
    if plane == 1:
        return [(p % 4, BAND * (p // 4), window(4, p, BAND), BAND) for p in range(16)]
    return [(q % 4, 5 * (q // 4), window(1, q, 5), 5) for q in range(64)]


def ready(start, count):
    return (start + count - 1) // 81


def spans(plane):
    found = {}
    for target, at, start, count in pieces(plane):
        key = (target, ready(start, count))
        low, size = found.get(key, (at, 0))
        found[key] = (low, size + count)
    return found


class Scatter:
    def __init__(self, plane, terms, got, send, recv):
        self.axis, self.terms, self.got, self.send, self.recv = plane, terms, got, send, recv
        self.me = place()[plane]
        self.spans = spans(plane)

    def copy(self, target, a, slot):
        low, size = self.spans[target, a]
        at = list(place())
        at[self.axis] = target
        return pltpu.make_async_remote_copy(
            src_ref=self.terms.at[target, pl.ds(low, size)],
            dst_ref=self.got.at[slot, pl.ds(low, size)],
            send_sem=self.send.at[target, a],
            recv_sem=self.recv.at[slot, a],
            device_id=device(at),
            device_id_type=MESH,
        )

    def start(self, now):
        for target, a in self.spans:
            if a == now:
                slot = lax.rem(self.me + 3 - target, 4)

                @pl.when(self.me != target)
                def _():
                    self.copy(target, a, slot).start()

    def wait(self):
        for target, a in self.spans:

            @pl.when(self.me == target)
            def _():
                for slot in range(3):
                    self.copy(target, a, slot).wait_recv()

        for target, a in self.spans:

            @pl.when(self.me != target)
            def _():
                self.copy(target, a, 0).wait_send()

    def total(self, units):
        value = self.terms[self.me, units].astype(F32)
        for slot in range(3):
            value += self.got[slot, units].astype(F32)
        return value.astype(BF16)


def step_kernel(
    x_hbm, cot_hbm, w_ref, gi_ref, gk_ref,
    x_ref, cot_ref, gi_out, packed, edges, rows_in, cols_in, xp, gp, xc, wv, wt, acc, gall, dw, pair,
    first_a, first_b, first_c, got_a, got_b, got_c, sum_a, sum_b, sum_c,
    next_b, near_a, near_b, near_c, last_a, last_b, last_c, ends, both, left, right,
    halo_send, halo_recv, in_sems, wsem, pair_sems, first_send, first_recv, next_sems, last_sems, core_sems,
):
    chip_x, chip_y, chip_z, core = place()
    xcopy = pltpu.make_async_copy(x_hbm, x_ref, in_sems.at[0])
    ccopy = pltpu.make_async_copy(cot_hbm, cot_ref, in_sems.at[1])
    wcopy = pltpu.make_async_copy(w_ref, wv.at[pl.ds(0, ROWS)], wsem)
    xcopy.start()
    wcopy.start()
    ccopy.start()
    rows_in[...] = jnp.zeros_like(rows_in)
    cols_in[...] = jnp.zeros_like(cols_in)
    peers = greet()
    xp[...] = jnp.zeros_like(xp)
    gp[...] = jnp.zeros_like(gp)
    rest = pl.ds(ROWS, WIDE - GROUP)
    wv[rest, :] = jnp.zeros((WIDE - GROUP, C), BF16)
    wt[rest, :] = jnp.zeros((WIDE - GROUP, C), BF16)
    xcopy.wait()
    for s in range(S):
        block = jnp.swapaxes(x_ref[0, :, s].astype(F32), 0, 1).astype(BF16)
        xp[1, 1 + s, 1 : 1 + T, :, 0:C] = block

    def halo(field, k):
        pads = (packed.at[k], edges.at[k], rows_in.at[k], cols_in.at[k])
        return start_halo(field, *pads, halo_send.at[k], halo_recv.at[k])

    def rim(field, k, view_row):
        place_rim(field, rows_in.at[k], cols_in.at[k], view_row)

    pl.semaphore_wait(pltpu.get_barrier_semaphore(), peers)
    jobs = halo(xp, 0)
    wcopy.wait()

    def turn(low, high):
        @pl.loop(low, high)
        def _(tap):
            src = pl.ds(pl.multiple_of((80 - tap) * C, 64), C)
            dst = pl.ds(pl.multiple_of(tap * C, 64), C)
            wt[dst, :] = wv[src, :].T

    turn(0, 40)
    for copy, _, got in jobs[:2]:
        pl.when(got)(copy.wait_recv)
    rim(xp, 0, 1)
    unfold(xp, xc.at[1], 1)
    correlate(xc.at[1], wv, acc, 1, True)
    turn(40, 60)
    for copy, _, got in jobs[2:]:
        pl.when(got)(copy.wait_recv)
    for view_row in (0, 2):
        rim(xp, 0, view_row)
        unfold(xp, xc.at[view_row], view_row)
        correlate(xc.at[view_row], wv, acc, view_row, False)
    for copy, sent, _ in jobs:
        pl.when(sent)(copy.wait_send)

    ccopy.wait()
    preact = shifted(acc[0], 1) + acc[1] + shifted(acc[2], -1)
    for s in range(S):
        upstream = jnp.swapaxes(cot_ref[0, :, s].astype(F32), 0, 1).reshape(T * V, C)
        pre = preact[s * T * V : (s + 1) * T * V]
        sigmoid = jax.nn.sigmoid(pre)
        grad = upstream * sigmoid * (1.0 + pre * (1.0 - sigmoid))
        gp[1, 1 + s, 1 : 1 + T, :, 0:C] = grad.astype(BF16).reshape(T, V, C)
    jobs = halo(gp, 1)
    grad = gp[1, 1 : 1 + S, 1 : 1 + T].reshape(CELLS, LANES)
    wide = grad.astype(F32)
    gall[:, 0:256] = shifted(wide, -1).astype(BF16)
    gall[:, 256:512] = grad
    gall[:, 512:768] = shifted(wide, 1).astype(BF16)

    firsts = (first_a, first_b, first_c)
    scatters = [
        Scatter(k, firsts[k], (got_a, got_b, got_c)[k], first_send.at[k], first_recv.at[k])
        for k in range(3)
    ]

    def exchange(a):
        units = pl.ds(81 * a, 81)
        return send_to(sibling(), dw.at[1 - core, :, units], pair.at[:, units], pair_sems, a)

    def both_cores(plane, start, count):
        units = pl.ds(start, count)
        return dw[core, plane, units] + pair[plane, units]

    def scatter(copy, a):
        copy.wait_recv()
        chips = [q for q, (_, _, start, count) in enumerate(pieces(2)) if ready(start, count) == a]

        @pl.loop(chips[0], chips[-1] + 1)
        def _(q):
            at = pl.ds((q // 4) * 5, 5)
            first_c[q % 4, at] = both_cores(2, window(1, q, 5), 5)

        scatters[2].start(a)
        for plane in (1, 0):
            for target, at, start, count in pieces(plane):
                if ready(start, count) == a:
                    firsts[plane][target, at : at + count] = both_cores(plane, start, count)
            scatters[plane].start(a)

    def input_terms(view_row, first):
        rim(gp, 1, view_row)
        unfold(gp, xc.at[view_row], view_row)
        correlate(xc.at[view_row], wt, acc, view_row, first)

    kernel_terms(xc, gall, dw, 0)
    pairs = [exchange(0)]
    for a in (1, 2):
        kernel_terms(xc, gall, dw, a)
        pairs.append(exchange(a))
        scatter(pairs[a - 1], a - 1)
    turn(60, 81)
    for copy, _, got in jobs[:2]:
        pl.when(got)(copy.wait_recv)
    input_terms(1, True)
    scatter(pairs[2], 2)
    for copy, _, got in jobs[2:]:
        pl.when(got)(copy.wait_recv)
    input_terms(0, False)

    chips = (chip_x, chip_y, chip_z)
    column = chip_x * 4 + chip_y

    def next_part(plane, to):
        if plane == 0:
            return sum_a.at[pl.ds(window(4, chip_x * 4 + to, BAND) - window(16, chip_x, 64), BAND)]
        return (next_b if plane == 1 else sum_c).at[to]

    def last_part(plane, to):
        if plane == 0:
            return last_a.at[pl.ds(window(1, column * 4 + to, 5) - window(4, column, BAND), 5)]
        return (last_b if plane == 1 else last_c).at[to]

    nears = (near_a, near_b, near_c)
    second, third = (1, 2, 0), (2, 0, 1)
    sends = {}
    for plane in range(3):
        scatters[plane].wait()
        if plane == 0:
            sum_a[...] = scatters[0].total(pl.ds(0, 64))
        elif plane == 1:
            for x in range(4):
                sum_b[x] = scatters[1].total(pl.ds(BAND * x, BAND))
            for x in range(4):
                for z in range(4):
                    start = window(1, x * 16 + chip_y * 4 + z, 5) - window(4, x * 4 + chip_y, BAND)
                    next_b[z, x] = sum_b[x, pl.ds(start, 5)]
        else:

            @pl.loop(0, 16)
            def _(p):
                sum_c[p // 4, p % 4] = scatters[2].total(pl.ds(5 * p, 5))

        axis = second[plane]
        for step in (2, 1, 3):
            src = next_part(plane, lax.rem(chips[axis] + step, 4))
            dst = nears[plane].at[step - 1]
            sends[plane, step] = send_to(
                peer_along(axis, step), src, dst, next_sems.at[plane], step - 1
            )

    input_terms(2, False)
    total = shifted(acc[0], 1) + acc[1] + shifted(acc[2], -1)
    for s in range(S):
        block = total[s * T * V : (s + 1) * T * V].reshape(T, V, C)
        gi_out[0, :, s] = jnp.swapaxes(block, 0, 1).astype(BF16)
    gcopy = pltpu.make_async_copy(gi_out, gi_ref, in_sems.at[2])
    gcopy.start()

    lasts = {}
    for plane in range(3):
        for step in (1, 3, 2):
            sends[plane, step].wait_recv()
        value = next_part(plane, chips[second[plane]])[...].astype(F32)
        for k in range(3):
            value += nears[plane][k].astype(F32)
        (last_a, last_b, last_c)[plane][...] = value.astype(BF16)
        axis = third[plane]
        for step in (2, 1, 3):
            src = last_part(plane, lax.rem(chips[axis] + step, 4))
            slot = 3 * plane + step - 1
            lasts[plane, step] = send_to(
                peer_along(axis, step), src, ends.at[slot], last_sems, slot
            )
    for copy, sent, _ in jobs:
        pl.when(sent)(copy.wait_send)
    for copy in (*pairs, *sends.values()):
        copy.wait_send()
    gcopy.wait()
    for plane in range(3):
        for step in (1, 3, 2):
            lasts[plane, step].wait()
        value = last_part(plane, chips[third[plane]])[...].astype(F32)
        for k in range(3):
            value += ends[3 * plane + k].astype(F32)
        both[core, plane] = value
    send_to(sibling(), both.at[core], both.at[core], core_sems, 0).wait()

    for k in range(2):
        for unit in range(5):
            row = 64 * unit + 32 * k
            tail = both[k, 2, unit]
            left[row : row + 16] = both[k, 0, unit]
            left[row + 16 : row + 32] = both[k, 1, unit]
            right[row : row + 16] = tail
            right[row + 16 : row + 32] = pltpu.roll(tail, 64, 1)
    count = 160
    odd = pltpu.roll(left[pl.ds(1, count, stride=2), :], 64, 1)
    head = lax.broadcasted_iota(jnp.int32, (count, 128), 1) < 64
    gk_ref[pl.ds(0, count, stride=3), :] = left[pl.ds(0, count, stride=2), :]
    gk_ref[pl.ds(1, count, stride=3), :] = jnp.where(head, right[pl.ds(0, count, stride=2), :], odd)
    rest = pltpu.roll(right[pl.ds(1, count, stride=2), :], 64, 1)
    gk_ref[pl.ds(2, count, stride=3), :] = jnp.where(head, odd, rest)


def local(inputs, cotangent, kernel, moment_one, moment_two):
    vmem = pl.BlockSpec(memory_space=pltpu.VMEM)
    anywhere = pl.BlockSpec(memory_space=pl.ANY)
    padded = (3, S + 2, T + 2, V, LANES)
    tiles = lambda *lead: pltpu.VMEM((*lead, *TILE), BF16)
    dma = lambda *shape: pltpu.SemaphoreType.DMA(shape)
    long_kernel = pltpu.VMEM((ROWS + WIDE - GROUP, C), BF16)
    grad_input, window_grad = pl.pallas_call(
        step_kernel,
        out_shape=(
            jax.ShapeDtypeStruct(inputs.shape, BF16),
            jax.ShapeDtypeStruct((480, 128), F32),
        ),
        in_specs=[anywhere, anywhere, anywhere],
        out_specs=(anywhere, vmem),
        scratch_shapes=[
            *(pltpu.VMEM(inputs.shape, BF16) for _ in range(3)),
            pltpu.VMEM((2, 2, T, V, 384), BF16),
            pltpu.VMEM((2, 2, 2, V, 384), BF16),
            pltpu.VMEM((2, 2, 2, T, V, 384), BF16),
            pltpu.VMEM((2, 3, 2, 2, V, 384), BF16),
            pltpu.VMEM(padded, BF16),
            pltpu.VMEM(padded, BF16),
            pltpu.VMEM((3, CELLS, WIDE), BF16),
            long_kernel,
            long_kernel,
            pltpu.VMEM((3, CELLS, C), F32),
            pltpu.VMEM((CELLS, 768), BF16),
            tiles(2, 3, UNITS),
            tiles(3, UNITS),
            *(tiles(4, n) for n in LENGTHS),
            *(tiles(3, n) for n in LENGTHS),
            tiles(64),
            tiles(4, BAND),
            tiles(4, 4, 5),
            tiles(4, 4, 5),
            tiles(3, BAND),
            tiles(3, 4, 5),
            tiles(3, 4, 5),
            tiles(BAND),
            tiles(4, 5),
            tiles(4, 5),
            tiles(9, 5),
            pltpu.VMEM((2, 3, 5, *TILE), F32),
            pltpu.VMEM((320, 128), F32),
            pltpu.VMEM((320, 128), F32),
            dma(2, 8),
            dma(2, 8),
            dma(3),
            pltpu.SemaphoreType.DMA,
            dma(2, 3),
            dma(3, 4, 3),
            dma(3, 3, 3),
            dma(3, 2, 3),
            dma(2, 9),
            dma(2, 1),
        ],
        compiler_params=pltpu.CompilerParams(
            vmem_limit_bytes=56 * 1024 * 1024, collective_id=0, has_side_effects=True
        ),
        cost_estimate=pl.CostEstimate(flops=9 * 10**9, bytes_accessed=10**7, transcendentals=10**5),
    )(inputs, cotangent, kernel.reshape(ROWS, C))
    share_len = moment_one.shape[0]
    chip = lax.axis_index("ang") * 4 + lax.axis_index("sp") // 2
    begin = lax.axis_index(("ang", "sp")) * share_len - window(1, chip, 5) * (64 * C)
    share = lax.dynamic_slice_in_dim(window_grad.reshape(-1), begin, share_len, 0)
    pixels = CELLS * lax.axis_size("ang") * lax.axis_size("sp")
    grad_share = share * F32(1.0 / math.sqrt(pixels))
    moment_next = beta_one * moment_one + (1.0 - beta_one) * grad_share
    square_next = beta_two * moment_two + (1.0 - beta_two) * grad_share * grad_share
    first_fix = 1.0 - beta_one**adam_step
    second_fix = 1.0 - beta_two**adam_step
    direction = moment_next / first_fix / (jnp.sqrt(square_next / second_fix) + epsilon)
    return (grad_input, moment_next, square_next, direction)


def solution(mesh):
    field = P("ang", None, None, "sp", None)
    share = P(("ang", "sp"))
    return jax.shard_map(
        local,
        mesh=mesh,
        in_specs=(field, field, P(), share, share),
        out_specs=(field, share, share, share),
        check_vma=False,
    )
```

```python
import functools
import math

import jax
import jax.numpy as jnp
from jax import lax
from jax.experimental import pallas as pl
from jax.experimental.pallas import tpu as pltpu
from jax.sharding import PartitionSpec as P

beta_one = 0.9
beta_two = 0.999
adam_step = 100
epsilon = 1e-08

MESH = pl.DeviceIdType.MESH
F32 = jnp.float32
BF16 = jnp.bfloat16

V, S, T, C = 16, 4, 8, 192
CELLS = V * S * T
GROUP = 9 * C
WIDE = GROUP + 64
ROWS = 9 * GROUP
LANES = 256
SIDES = ((0, 1), (0, -1), (1, 0), (-1, 0), (1, 1), (1, -1), (-1, 1), (-1, -1))


def start_halo(field, packed, edges, rows_in, cols_in, send, recv):
    rows, cols = lax.axis_size("ang"), lax.axis_size("sp")
    row, col = lax.axis_index("ang"), lax.axis_index("sp")
    for j in range(2):
        first = field[1, 1 + 2 * j, 1 : 1 + T].reshape(T * V, LANES)
        second = pltpu.roll(field[1, 2 + 2 * j, 1 : 1 + T].reshape(T * V, LANES), 64, 1)
        packed[j, :, :, 0:128] = first[:, :128].reshape(T, V, 128)
        packed[j, :, :, 128:256] = (first[:, 128:] + second[:, :128]).reshape(T, V, 128)
        packed[j, :, :, 256:384] = second[:, 128:].reshape(T, V, 128)
        edges[0, j] = packed[j, 0]
        edges[1, j] = packed[j, T - 1]
    jobs = []
    for side, (da, ds) in enumerate(SIDES):
        if ds == 0:
            src, dst = packed, rows_in.at[(1 - da) // 2]
        elif ds == 1:
            src, dst = edges.at[1], cols_in.at[1 - da, 0]
        else:
            src, dst = edges.at[0], cols_in.at[1 - da, 1]
        sent = (row + da >= 0) & (row + da < rows) & (col + ds >= 0) & (col + ds < cols)
        got = (row - da >= 0) & (row - da < rows) & (col - ds >= 0) & (col - ds < cols)
        copy = pltpu.make_async_remote_copy(
            src_ref=src,
            dst_ref=dst,
            send_sem=send.at[side],
            recv_sem=recv.at[side],
            device_id=(row + da, col + ds),
            device_id_type=MESH,
        )
        jobs.append((copy, sent, got))
    for side in (4, 5, 6, 7, 2, 3, 0, 1):
        pl.when(jobs[side][1])(jobs[side][0].start)
    return jobs


def unpack(value):
    lane = lax.broadcasted_iota(jnp.int32, (value.shape[0], LANES), 1)
    keep = (lane < C).astype(F32).astype(BF16)
    return value[:, 0:LANES] * keep, pltpu.roll(value[:, 128:384], 192, 1) * keep


def place_rim(field, rows_in, cols_in, view_row):
    for j in range(2):
        if view_row != 1:
            pair = unpack(rows_in[view_row // 2, j].reshape(T * V, 384))
            for k in range(2):
                field[view_row, 1 + 2 * j + k, 1 : 1 + T] = pair[k].reshape(T, V, LANES)
        for side, at in ((0, 0), (1, T + 1)):
            pair = unpack(cols_in[view_row, side, j])
            for k in range(2):
                field[view_row, 1 + 2 * j + k, at] = pair[k]


def greet():
    rows, cols = lax.axis_size("ang"), lax.axis_size("sp")
    row, col = lax.axis_index("ang"), lax.axis_index("sp")
    barrier = pltpu.get_barrier_semaphore()

    def signal(peer):
        pl.semaphore_signal(barrier, inc=1, device_id=peer, device_id_type=MESH)

    for da, ds in SIDES:
        there = (row + da >= 0) & (row + da < rows) & (col + ds >= 0) & (col + ds < cols)
        pl.when(there)(functools.partial(signal, (row + da, col + ds)))
    for axis in range(3):
        for step in range(1, 4):
            signal(peer_along(axis, step))
    signal(sibling())
    tall = 1 + (row > 0).astype(jnp.int32) + (row < rows - 1).astype(jnp.int32)
    broad = 1 + (col > 0).astype(jnp.int32) + (col < cols - 1).astype(jnp.int32)
    return tall * broad + 9


def place():
    row, col = lax.axis_index("ang"), lax.axis_index("sp")
    return lax.div(row, 4), lax.rem(row, 4), lax.div(col, 2), lax.rem(col, 2)


def device(at):
    return (at[0] * 4 + at[1], at[2] * 2 + at[3])


def peer_along(axis, step):
    at = list(place())
    at[axis] = lax.rem(at[axis] + step, 4)
    return device(at)


def sibling():
    x, y, z, core = place()
    return (x * 4 + y, z * 2 + 1 - core)


def unfold(field, taps, view_row):
    @pl.loop(0, S)
    def _(s):
        def low(k):
            block = field[view_row, s + k // 3, pl.ds(k % 3, T)]
            return block.reshape(T * V, LANES)

        out = pl.ds(pl.multiple_of(s * T * V, T * V), T * V)
        for pair in range(4):
            first = low(2 * pair)
            second = pltpu.roll(low(2 * pair + 1), 64, 1)
            at = 384 * pair
            taps[out, at : at + 128] = first[:, :128]
            taps[out, at + 128 : at + 256] = first[:, 128:] + second[:, :128]
            taps[out, at + 256 : at + 384] = second[:, 128:]
        taps[out, 1536:1792] = low(8)


def shifted(values, by):
    rows = values.shape[0]
    view = lax.broadcasted_iota(jnp.int32, values.shape, 0) % V
    keep = (view >= by) if by > 0 else (view < V + by)
    return jnp.where(keep, pltpu.roll(values, by % rows, 0), jnp.zeros_like(values))


def correlate(taps, weights, acc, view_row, first):
    @pl.loop(0, 3)
    def _(b):
        at = pl.multiple_of((view_row * 3 + b) * GROUP, 64)
        term = jnp.dot(taps[...], weights[pl.ds(at, WIDE), :], preferred_element_type=F32)
        if first:
            acc[b] = term
        else:
            acc[b] += term


UNITS = 243
TILE = (16, 128)
BAND = 17
LENGTHS = (64, 4 * BAND, 80)


def window(chips, index, count):
    start = (index * (chips * 243)) // 64
    if isinstance(index, int):
        return min(start, UNITS - count)
    return jnp.minimum(start, UNITS - count)


def kernel_terms(taps, grads, dw, a):
    for part in range(5):
        at, size = 384 * part, (384 if part < 4 else 192)
        term = lax.dot_general(
            taps[a, :, at : at + (size if part < 4 else 256)],
            grads[...],
            (((0,), (0,)), ((), ())),
            preferred_element_type=F32,
        )
        for b in range(3):
            count = size // 64
            block = term[0:size, 256 * b : 256 * b + 256].reshape(count, 2, 2, 16, 256)
            dst = pl.ds((3 * a + b) * 27 + 6 * part, count)
            for core in range(2):
                low, high = block[:, core, 0], block[:, core, 1]
                dw[core, 0, dst] = low[:, :, :128].astype(BF16)
                dw[core, 1, dst] = high[:, :, :128].astype(BF16)
                tail = pltpu.roll(high[:, :, 128:].reshape(count * 16, 128), 64, 1)
                dw[core, 2, dst] = (low[:, :, 128:] + tail.reshape(count, 16, 128)).astype(BF16)


def send_to(peer, src, dst, sems, index):
    copy = pltpu.make_async_remote_copy(
        src_ref=src,
        dst_ref=dst,
        send_sem=sems.at[0, index],
        recv_sem=sems.at[1, index],
        device_id=peer,
        device_id_type=MESH,
    )
    copy.start()
    return copy


def pieces(plane):
    if plane == 0:
        found = []
        for x in range(4):
            start = window(16, x, 64)
            for a in range(3):
                low, high = max(start, 81 * a), min(start + 64, 81 * a + 81)
                if low < high:
                    found.append((x, low - start, low, high - low))
        return found
    if plane == 1:
        return [(p % 4, BAND * (p // 4), window(4, p, BAND), BAND) for p in range(16)]
    return [(q % 4, 5 * (q // 4), window(1, q, 5), 5) for q in range(64)]


def ready(start, count):
    return (start + count - 1) // 81


def spans(plane):
    found = {}
    for target, at, start, count in pieces(plane):
        key = (target, ready(start, count))
        low, size = found.get(key, (at, 0))
        found[key] = (low, size + count)
    return found


class Scatter:
    def __init__(self, plane, terms, got, send, recv):
        self.axis, self.terms, self.got, self.send, self.recv = plane, terms, got, send, recv
        self.me = place()[plane]
        self.spans = spans(plane)

    def copy(self, target, a, slot):
        low, size = self.spans[target, a]
        at = list(place())
        at[self.axis] = target
        return pltpu.make_async_remote_copy(
            src_ref=self.terms.at[target, pl.ds(low, size)],
            dst_ref=self.got.at[slot, pl.ds(low, size)],
            send_sem=self.send.at[target, a],
            recv_sem=self.recv.at[slot, a],
            device_id=device(at),
            device_id_type=MESH,
        )

    def start(self, now, far):
        for target, a in self.spans:
            if a == now:
                slot = lax.rem(self.me + 3 - target, 4)
                chosen = slot == 1 if far else (slot == 0) | (slot == 2)

                @pl.when(chosen)
                def _():
                    self.copy(target, a, slot).start()

    def wait(self):
        for target, a in self.spans:

            @pl.when(self.me == target)
            def _():
                for slot in range(3):
                    self.copy(target, a, slot).wait_recv()

        for target, a in self.spans:

            @pl.when(self.me != target)
            def _():
                self.copy(target, a, 0).wait_send()

    def total(self, units):
        value = self.terms[self.me, units].astype(F32)
        for slot in range(3):
            value += self.got[slot, units].astype(F32)
        return value.astype(BF16)


def step_kernel(
    x_hbm, cot_hbm, w_ref, gi_ref, gk_ref,
    x_ref, cot_ref, gi_out, packed, edges, rows_in, cols_in, xp, gp, xc, wv, wt, acc, gall, dw, pair,
    first_a, first_b, first_c, got_a, got_b, got_c, sum_a, sum_b, sum_c,
    next_b, near_a, near_b, near_c, last_a, last_b, last_c, ends, both, left, right,
    halo_send, halo_recv, in_sems, wsem, pair_sems, first_send, first_recv, next_sems, last_sems, core_sems,
):
    chip_x, chip_y, chip_z, core = place()
    xcopy = pltpu.make_async_copy(x_hbm, x_ref, in_sems.at[0])
    ccopy = pltpu.make_async_copy(cot_hbm, cot_ref, in_sems.at[1])
    wcopy = pltpu.make_async_copy(w_ref, wv.at[pl.ds(0, ROWS)], wsem)
    xcopy.start()
    wcopy.start()
    ccopy.start()
    rows_in[...] = jnp.zeros_like(rows_in)
    cols_in[...] = jnp.zeros_like(cols_in)
    peers = greet()
    xp[...] = jnp.zeros_like(xp)
    gp[...] = jnp.zeros_like(gp)
    rest = pl.ds(ROWS, WIDE - GROUP)
    wv[rest, :] = jnp.zeros((WIDE - GROUP, C), BF16)
    wt[rest, :] = jnp.zeros((WIDE - GROUP, C), BF16)
    xcopy.wait()
    for s in range(S):
        block = jnp.swapaxes(x_ref[0, :, s].astype(F32), 0, 1).astype(BF16)
        xp[1, 1 + s, 1 : 1 + T, :, 0:C] = block

    def halo(field, k):
        pads = (packed.at[k], edges.at[k], rows_in.at[k], cols_in.at[k])
        return start_halo(field, *pads, halo_send.at[k], halo_recv.at[k])

    def rim(field, k, view_row):
        place_rim(field, rows_in.at[k], cols_in.at[k], view_row)

    pl.semaphore_wait(pltpu.get_barrier_semaphore(), peers)
    jobs = halo(xp, 0)
    wcopy.wait()

    def turn(low, high):
        @pl.loop(low, high)
        def _(tap):
            src = pl.ds(pl.multiple_of((80 - tap) * C, 64), C)
            dst = pl.ds(pl.multiple_of(tap * C, 64), C)
            wt[dst, :] = wv[src, :].T

    turn(0, 40)
    for copy, _, got in jobs[:2]:
        pl.when(got)(copy.wait_recv)
    rim(xp, 0, 1)
    unfold(xp, xc.at[1], 1)
    correlate(xc.at[1], wv, acc, 1, True)
    turn(40, 60)
    for copy, _, got in jobs[2:]:
        pl.when(got)(copy.wait_recv)
    for view_row in (0, 2):
        rim(xp, 0, view_row)
        unfold(xp, xc.at[view_row], view_row)
        correlate(xc.at[view_row], wv, acc, view_row, False)
    for copy, sent, _ in jobs:
        pl.when(sent)(copy.wait_send)

    ccopy.wait()
    preact = shifted(acc[0], 1) + acc[1] + shifted(acc[2], -1)
    for s in range(S):
        upstream = jnp.swapaxes(cot_ref[0, :, s].astype(F32), 0, 1).reshape(T * V, C)
        pre = preact[s * T * V : (s + 1) * T * V]
        sigmoid = jax.nn.sigmoid(pre)
        grad = upstream * sigmoid * (1.0 + pre * (1.0 - sigmoid))
        gp[1, 1 + s, 1 : 1 + T, :, 0:C] = grad.astype(BF16).reshape(T, V, C)
    jobs = halo(gp, 1)
    grad = gp[1, 1 : 1 + S, 1 : 1 + T].reshape(CELLS, LANES)
    wide = grad.astype(F32)
    gall[:, 0:256] = shifted(wide, -1).astype(BF16)
    gall[:, 256:512] = grad
    gall[:, 512:768] = shifted(wide, 1).astype(BF16)

    firsts = (first_a, first_b, first_c)
    scatters = [
        Scatter(k, firsts[k], (got_a, got_b, got_c)[k], first_send.at[k], first_recv.at[k])
        for k in range(3)
    ]

    def exchange(a):
        units = pl.ds(81 * a, 81)
        return send_to(sibling(), dw.at[1 - core, :, units], pair.at[:, units], pair_sems, a)

    def both_cores(plane, start, count):
        units = pl.ds(start, count)
        return dw[core, plane, units] + pair[plane, units]

    def scatter(copy, a):
        copy.wait_recv()
        chips = [q for q, (_, _, start, count) in enumerate(pieces(2)) if ready(start, count) == a]

        @pl.loop(chips[0], chips[-1] + 1)
        def _(q):
            at = pl.ds((q // 4) * 5, 5)
            first_c[q % 4, at] = both_cores(2, window(1, q, 5), 5)

        scatters[2].start(a, False)
        for plane in (1, 0):
            for target, at, start, count in pieces(plane):
                if ready(start, count) == a:
                    firsts[plane][target, at : at + count] = both_cores(plane, start, count)
            scatters[plane].start(a, False)
        for plane in (2, 1, 0):
            scatters[plane].start(a, True)

    def input_terms(view_row, first):
        rim(gp, 1, view_row)
        unfold(gp, xc.at[view_row], view_row)
        correlate(xc.at[view_row], wt, acc, view_row, first)

    kernel_terms(xc, gall, dw, 0)
    pairs = [exchange(0)]
    for a in (1, 2):
        kernel_terms(xc, gall, dw, a)
        pairs.append(exchange(a))
        scatter(pairs[a - 1], a - 1)
    turn(60, 81)
    for copy, _, got in jobs[:2]:
        pl.when(got)(copy.wait_recv)
    input_terms(1, True)
    scatter(pairs[2], 2)
    for copy, _, got in jobs[2:]:
        pl.when(got)(copy.wait_recv)
    input_terms(0, False)

    chips = (chip_x, chip_y, chip_z)
    column = chip_x * 4 + chip_y

    def next_part(plane, to):
        if plane == 0:
            return sum_a.at[pl.ds(window(4, chip_x * 4 + to, BAND) - window(16, chip_x, 64), BAND)]
        return (next_b if plane == 1 else sum_c).at[to]

    def last_part(plane, to):
        if plane == 0:
            return last_a.at[pl.ds(window(1, column * 4 + to, 5) - window(4, column, BAND), 5)]
        return (last_b if plane == 1 else last_c).at[to]

    nears = (near_a, near_b, near_c)
    second, third = (1, 2, 0), (2, 0, 1)
    sends = {}
    for plane in range(3):
        scatters[plane].wait()
        if plane == 0:
            sum_a[...] = scatters[0].total(pl.ds(0, 64))
        elif plane == 1:
            for x in range(4):
                sum_b[x] = scatters[1].total(pl.ds(BAND * x, BAND))
            for x in range(4):
                for z in range(4):
                    start = window(1, x * 16 + chip_y * 4 + z, 5) - window(4, x * 4 + chip_y, BAND)
                    next_b[z, x] = sum_b[x, pl.ds(start, 5)]
        else:

            @pl.loop(0, 16)
            def _(p):
                sum_c[p // 4, p % 4] = scatters[2].total(pl.ds(5 * p, 5))

        axis = second[plane]
        for step in (2, 1, 3):
            src = next_part(plane, lax.rem(chips[axis] + step, 4))
            dst = nears[plane].at[step - 1]
            sends[plane, step] = send_to(
                peer_along(axis, step), src, dst, next_sems.at[plane], step - 1
            )

    input_terms(2, False)
    total = shifted(acc[0], 1) + acc[1] + shifted(acc[2], -1)
    for s in range(S):
        block = total[s * T * V : (s + 1) * T * V].reshape(T, V, C)
        gi_out[0, :, s] = jnp.swapaxes(block, 0, 1).astype(BF16)
    gcopy = pltpu.make_async_copy(gi_out, gi_ref, in_sems.at[2])
    gcopy.start()

    lasts = {}
    for plane in range(3):
        for step in (1, 3, 2):
            sends[plane, step].wait_recv()
        value = next_part(plane, chips[second[plane]])[...].astype(F32)
        for k in range(3):
            value += nears[plane][k].astype(F32)
        (last_a, last_b, last_c)[plane][...] = value.astype(BF16)
        axis = third[plane]
        for step in (2, 1, 3):
            src = last_part(plane, lax.rem(chips[axis] + step, 4))
            slot = 3 * plane + step - 1
            lasts[plane, step] = send_to(
                peer_along(axis, step), src, ends.at[slot], last_sems, slot
            )
    for copy, sent, _ in jobs:
        pl.when(sent)(copy.wait_send)
    for copy in (*pairs, *sends.values()):
        copy.wait_send()
    gcopy.wait()
    for plane in range(3):
        for step in (1, 3, 2):
            lasts[plane, step].wait()
        value = last_part(plane, chips[third[plane]])[...].astype(F32)
        for k in range(3):
            value += ends[3 * plane + k].astype(F32)
        both[core, plane] = value
    send_to(sibling(), both.at[core], both.at[core], core_sems, 0).wait()

    for k in range(2):
        for unit in range(5):
            row = 64 * unit + 32 * k
            tail = both[k, 2, unit]
            left[row : row + 16] = both[k, 0, unit]
            left[row + 16 : row + 32] = both[k, 1, unit]
            right[row : row + 16] = tail
            right[row + 16 : row + 32] = pltpu.roll(tail, 64, 1)
    count = 160
    odd = pltpu.roll(left[pl.ds(1, count, stride=2), :], 64, 1)
    head = lax.broadcasted_iota(jnp.int32, (count, 128), 1) < 64
    gk_ref[pl.ds(0, count, stride=3), :] = left[pl.ds(0, count, stride=2), :]
    gk_ref[pl.ds(1, count, stride=3), :] = jnp.where(head, right[pl.ds(0, count, stride=2), :], odd)
    rest = pltpu.roll(right[pl.ds(1, count, stride=2), :], 64, 1)
    gk_ref[pl.ds(2, count, stride=3), :] = jnp.where(head, odd, rest)


def local(inputs, cotangent, kernel, moment_one, moment_two):
    vmem = pl.BlockSpec(memory_space=pltpu.VMEM)
    anywhere = pl.BlockSpec(memory_space=pl.ANY)
    padded = (3, S + 2, T + 2, V, LANES)
    tiles = lambda *lead: pltpu.VMEM((*lead, *TILE), BF16)
    dma = lambda *shape: pltpu.SemaphoreType.DMA(shape)
    long_kernel = pltpu.VMEM((ROWS + WIDE - GROUP, C), BF16)
    grad_input, window_grad = pl.pallas_call(
        step_kernel,
        out_shape=(
            jax.ShapeDtypeStruct(inputs.shape, BF16),
            jax.ShapeDtypeStruct((480, 128), F32),
        ),
        in_specs=[anywhere, anywhere, anywhere],
        out_specs=(anywhere, vmem),
        scratch_shapes=[
            *(pltpu.VMEM(inputs.shape, BF16) for _ in range(3)),
            pltpu.VMEM((2, 2, T, V, 384), BF16),
            pltpu.VMEM((2, 2, 2, V, 384), BF16),
            pltpu.VMEM((2, 2, 2, T, V, 384), BF16),
            pltpu.VMEM((2, 3, 2, 2, V, 384), BF16),
            pltpu.VMEM(padded, BF16),
            pltpu.VMEM(padded, BF16),
            pltpu.VMEM((3, CELLS, WIDE), BF16),
            long_kernel,
            long_kernel,
            pltpu.VMEM((3, CELLS, C), F32),
            pltpu.VMEM((CELLS, 768), BF16),
            tiles(2, 3, UNITS),
            tiles(3, UNITS),
            *(tiles(4, n) for n in LENGTHS),
            *(tiles(3, n) for n in LENGTHS),
            tiles(64),
            tiles(4, BAND),
            tiles(4, 4, 5),
            tiles(4, 4, 5),
            tiles(3, BAND),
            tiles(3, 4, 5),
            tiles(3, 4, 5),
            tiles(BAND),
            tiles(4, 5),
            tiles(4, 5),
            tiles(9, 5),
            pltpu.VMEM((2, 3, 5, *TILE), F32),
            pltpu.VMEM((320, 128), F32),
            pltpu.VMEM((320, 128), F32),
            dma(2, 8),
            dma(2, 8),
            dma(3),
            pltpu.SemaphoreType.DMA,
            dma(2, 3),
            dma(3, 4, 3),
            dma(3, 3, 3),
            dma(3, 2, 3),
            dma(2, 9),
            dma(2, 1),
        ],
        compiler_params=pltpu.CompilerParams(
            vmem_limit_bytes=56 * 1024 * 1024, collective_id=0, has_side_effects=True
        ),
        cost_estimate=pl.CostEstimate(flops=9 * 10**9, bytes_accessed=10**7, transcendentals=10**5),
    )(inputs, cotangent, kernel.reshape(ROWS, C))
    share_len = moment_one.shape[0]
    chip = lax.axis_index("ang") * 4 + lax.axis_index("sp") // 2
    begin = lax.axis_index(("ang", "sp")) * share_len - window(1, chip, 5) * (64 * C)
    share = lax.dynamic_slice_in_dim(window_grad.reshape(-1), begin, share_len, 0)
    pixels = CELLS * lax.axis_size("ang") * lax.axis_size("sp")
    grad_share = share * F32(1.0 / math.sqrt(pixels))
    moment_next = beta_one * moment_one + (1.0 - beta_one) * grad_share
    square_next = beta_two * moment_two + (1.0 - beta_two) * grad_share * grad_share
    first_fix = 1.0 - beta_one**adam_step
    second_fix = 1.0 - beta_two**adam_step
    direction = moment_next / first_fix / (jnp.sqrt(square_next / second_fix) + epsilon)
    return (grad_input, moment_next, square_next, direction)


def solution(mesh):
    field = P("ang", None, None, "sp", None)
    share = P(("ang", "sp"))
    return jax.shard_map(
        local,
        mesh=mesh,
        in_specs=(field, field, P(), share, share),
        out_specs=(field, share, share, share),
        check_vma=False,
    )
```

```python
import functools
import math

import jax
import jax.numpy as jnp
from jax import lax
from jax.experimental import pallas as pl
from jax.experimental.pallas import tpu as pltpu
from jax.sharding import PartitionSpec as P

beta_one = 0.9
beta_two = 0.999
adam_step = 100
epsilon = 1e-08

MESH = pl.DeviceIdType.MESH
F32 = jnp.float32
BF16 = jnp.bfloat16

V, S, T, C = 16, 4, 8, 192
CELLS = V * S * T
GROUP = 9 * C
WIDE = GROUP + 64
ROWS = 9 * GROUP
LANES = 256
SIDES = ((0, 1), (0, -1), (1, 0), (-1, 0), (1, 1), (1, -1), (-1, 1), (-1, -1))


def start_halo(field, packed, edges, rows_in, cols_in, send, recv):
    rows, cols = lax.axis_size("ang"), lax.axis_size("sp")
    row, col = lax.axis_index("ang"), lax.axis_index("sp")
    for j in range(2):
        first = field[1, 1 + 2 * j, 1 : 1 + T].reshape(T * V, LANES)
        second = pltpu.roll(field[1, 2 + 2 * j, 1 : 1 + T].reshape(T * V, LANES), 64, 1)
        packed[j, :, :, 0:128] = first[:, :128].reshape(T, V, 128)
        packed[j, :, :, 128:256] = (first[:, 128:] + second[:, :128]).reshape(T, V, 128)
        packed[j, :, :, 256:384] = second[:, 128:].reshape(T, V, 128)
        edges[0, j] = packed[j, 0]
        edges[1, j] = packed[j, T - 1]
    jobs = []
    for side, (da, ds) in enumerate(SIDES):
        if ds == 0:
            src, dst = packed, rows_in.at[(1 - da) // 2]
        elif ds == 1:
            src, dst = edges.at[1], cols_in.at[1 - da, 0]
        else:
            src, dst = edges.at[0], cols_in.at[1 - da, 1]
        sent = (row + da >= 0) & (row + da < rows) & (col + ds >= 0) & (col + ds < cols)
        got = (row - da >= 0) & (row - da < rows) & (col - ds >= 0) & (col - ds < cols)
        copy = pltpu.make_async_remote_copy(
            src_ref=src,
            dst_ref=dst,
            send_sem=send.at[side],
            recv_sem=recv.at[side],
            device_id=(row + da, col + ds),
            device_id_type=MESH,
        )
        jobs.append((copy, sent, got))
    for side in (4, 5, 6, 7, 2, 3, 0, 1):
        pl.when(jobs[side][1])(jobs[side][0].start)
    return jobs


def unpack(value):
    lane = lax.broadcasted_iota(jnp.int32, (value.shape[0], LANES), 1)
    keep = (lane < C).astype(F32).astype(BF16)
    return value[:, 0:LANES] * keep, pltpu.roll(value[:, 128:384], 192, 1) * keep


def place_rim(field, rows_in, cols_in, view_row):
    for j in range(2):
        if view_row != 1:
            pair = unpack(rows_in[view_row // 2, j].reshape(T * V, 384))
            for k in range(2):
                field[view_row, 1 + 2 * j + k, 1 : 1 + T] = pair[k].reshape(T, V, LANES)
        for side, at in ((0, 0), (1, T + 1)):
            pair = unpack(cols_in[view_row, side, j])
            for k in range(2):
                field[view_row, 1 + 2 * j + k, at] = pair[k]


def greet():
    rows, cols = lax.axis_size("ang"), lax.axis_size("sp")
    row, col = lax.axis_index("ang"), lax.axis_index("sp")
    barrier = pltpu.get_barrier_semaphore()

    def signal(peer):
        pl.semaphore_signal(barrier, inc=1, device_id=peer, device_id_type=MESH)

    for da, ds in SIDES:
        there = (row + da >= 0) & (row + da < rows) & (col + ds >= 0) & (col + ds < cols)
        pl.when(there)(functools.partial(signal, (row + da, col + ds)))
    for axis in range(3):
        for step in range(1, 4):
            signal(peer_along(axis, step))
    signal(sibling())
    tall = 1 + (row > 0).astype(jnp.int32) + (row < rows - 1).astype(jnp.int32)
    broad = 1 + (col > 0).astype(jnp.int32) + (col < cols - 1).astype(jnp.int32)
    return tall * broad + 9


def place():
    row, col = lax.axis_index("ang"), lax.axis_index("sp")
    return lax.div(row, 4), lax.rem(row, 4), lax.div(col, 2), lax.rem(col, 2)


def device(at):
    return (at[0] * 4 + at[1], at[2] * 2 + at[3])


def peer_along(axis, step):
    at = list(place())
    at[axis] = lax.rem(at[axis] + step, 4)
    return device(at)


def sibling():
    x, y, z, core = place()
    return (x * 4 + y, z * 2 + 1 - core)


def unfold(field, taps, view_row):
    @pl.loop(0, S)
    def _(s):
        def low(k):
            block = field[view_row, s + k // 3, pl.ds(k % 3, T)]
            return block.reshape(T * V, LANES)

        out = pl.ds(pl.multiple_of(s * T * V, T * V), T * V)
        for pair in range(4):
            first = low(2 * pair)
            second = pltpu.roll(low(2 * pair + 1), 64, 1)
            at = 384 * pair
            taps[out, at : at + 128] = first[:, :128]
            taps[out, at + 128 : at + 256] = first[:, 128:] + second[:, :128]
            taps[out, at + 256 : at + 384] = second[:, 128:]
        taps[out, 1536:1792] = low(8)


def shifted(values, by):
    rows = values.shape[0]
    view = lax.broadcasted_iota(jnp.int32, values.shape, 0) % V
    keep = (view >= by) if by > 0 else (view < V + by)
    return jnp.where(keep, pltpu.roll(values, by % rows, 0), jnp.zeros_like(values))


def correlate(taps, weights, acc, view_row, first):
    @pl.loop(0, 3)
    def _(b):
        at = pl.multiple_of((view_row * 3 + b) * GROUP, 64)
        term = jnp.dot(taps[...], weights[pl.ds(at, WIDE), :], preferred_element_type=F32)
        if first:
            acc[b] = term
        else:
            acc[b] += term


UNITS = 243
TILE = (16, 128)
LENGTHS = (64, 72, 80)


def window(chips, index, count):
    start = (index * (chips * 243)) // 64
    if isinstance(index, int):
        return min(start, UNITS - count)
    return jnp.minimum(start, UNITS - count)


def kernel_terms(taps, grads, dw, a):
    for part in range(5):
        at, size = 384 * part, (384 if part < 4 else 192)
        term = lax.dot_general(
            taps[a, :, at : at + (size if part < 4 else 256)],
            grads[...],
            (((0,), (0,)), ((), ())),
            preferred_element_type=F32,
        )
        for b in range(3):
            count = size // 64
            block = term[0:size, 256 * b : 256 * b + 256].reshape(count, 2, 2, 16, 256)
            dst = pl.ds((3 * a + b) * 27 + 6 * part, count)
            for core in range(2):
                low, high = block[:, core, 0], block[:, core, 1]
                dw[core, 0, dst] = low[:, :, :128].astype(BF16)
                dw[core, 1, dst] = high[:, :, :128].astype(BF16)
                tail = pltpu.roll(high[:, :, 128:].reshape(count * 16, 128), 64, 1)
                dw[core, 2, dst] = (low[:, :, 128:] + tail.reshape(count, 16, 128)).astype(BF16)


def send_to(peer, src, dst, sems, index):
    copy = pltpu.make_async_remote_copy(
        src_ref=src,
        dst_ref=dst,
        send_sem=sems.at[0, index],
        recv_sem=sems.at[1, index],
        device_id=peer,
        device_id_type=MESH,
    )
    copy.start()
    return copy


def pieces(plane):
    if plane == 0:
        found = []
        for x in range(4):
            start = window(16, x, 64)
            for a in range(3):
                low, high = max(start, 81 * a), min(start + 64, 81 * a + 81)
                if low < high:
                    found.append((x, low - start, low, high - low))
        return found
    if plane == 1:
        return [(p % 4, 18 * (p // 4), window(4, p, 18), 18) for p in range(16)]
    return [(q % 4, 5 * (q // 4), window(1, q, 5), 5) for q in range(64)]


def ready(start, count):
    return (start + count - 1) // 81


def spans(plane):
    found = {}
    for target, at, start, count in pieces(plane):
        key = (target, ready(start, count))
        low, size = found.get(key, (at, 0))
        found[key] = (low, size + count)
    return found


class Scatter:
    def __init__(self, plane, terms, got, send, recv):
        self.axis, self.terms, self.got, self.send, self.recv = plane, terms, got, send, recv
        self.me = place()[plane]
        self.spans = spans(plane)

    def copy(self, target, a, slot):
        low, size = self.spans[target, a]
        at = list(place())
        at[self.axis] = target
        return pltpu.make_async_remote_copy(
            src_ref=self.terms.at[target, pl.ds(low, size)],
            dst_ref=self.got.at[slot, pl.ds(low, size)],
            send_sem=self.send.at[target, a],
            recv_sem=self.recv.at[slot, a],
            device_id=device(at),
            device_id_type=MESH,
        )

    def start(self, now):
        for target, a in self.spans:
            if a == now:
                slot = lax.rem(self.me + 3 - target, 4)

                @pl.when(self.me != target)
                def _():
                    self.copy(target, a, slot).start()

    def wait(self):
        for target, a in self.spans:

            @pl.when(self.me == target)
            def _():
                for slot in range(3):
                    self.copy(target, a, slot).wait_recv()

        for target, a in self.spans:

            @pl.when(self.me != target)
            def _():
                self.copy(target, a, 0).wait_send()

    def total(self, units):
        value = self.terms[self.me, units].astype(F32)
        for slot in range(3):
            value += self.got[slot, units].astype(F32)
        return value.astype(BF16)


def step_kernel(
    x_hbm, cot_hbm, w_ref, gi_ref, gk_ref,
    x_ref, cot_ref, gi_out, packed, edges, rows_in, cols_in, xp, gp, xc, wv, wt, acc, gall, dw, pair,
    first_a, first_b, first_c, got_a, got_b, got_c, sum_a, sum_b, sum_c,
    next_b, near_a, near_b, near_c, last_a, last_b, last_c, ends, both, left, right,
    halo_send, halo_recv, in_sems, wsem, pair_sems, first_send, first_recv, next_sems, last_sems, core_sems,
):
    chip_x, chip_y, chip_z, core = place()
    xcopy = pltpu.make_async_copy(x_hbm, x_ref, in_sems.at[0])
    ccopy = pltpu.make_async_copy(cot_hbm, cot_ref, in_sems.at[1])
    wcopy = pltpu.make_async_copy(w_ref, wv.at[pl.ds(0, ROWS)], wsem)
    xcopy.start()
    wcopy.start()
    ccopy.start()
    rows_in[...] = jnp.zeros_like(rows_in)
    cols_in[...] = jnp.zeros_like(cols_in)
    peers = greet()
    xp[...] = jnp.zeros_like(xp)
    gp[...] = jnp.zeros_like(gp)
    rest = pl.ds(ROWS, WIDE - GROUP)
    wv[rest, :] = jnp.zeros((WIDE - GROUP, C), BF16)
    wt[rest, :] = jnp.zeros((WIDE - GROUP, C), BF16)
    xcopy.wait()
    for s in range(S):
        block = jnp.swapaxes(x_ref[0, :, s].astype(F32), 0, 1).astype(BF16)
        xp[1, 1 + s, 1 : 1 + T, :, 0:C] = block

    def halo(field, k):
        pads = (packed.at[k], edges.at[k], rows_in.at[k], cols_in.at[k])
        return start_halo(field, *pads, halo_send.at[k], halo_recv.at[k])

    def rim(field, k, view_row):
        place_rim(field, rows_in.at[k], cols_in.at[k], view_row)

    pl.semaphore_wait(pltpu.get_barrier_semaphore(), peers)
    jobs = halo(xp, 0)

    wcopy.wait()

    def turn(low, high):
        @pl.loop(low, high)
        def _(tap):
            src = pl.ds(pl.multiple_of((80 - tap) * C, 64), C)
            dst = pl.ds(pl.multiple_of(tap * C, 64), C)
            wt[dst, :] = wv[src, :].T

    turn(0, 54)
    for copy, _, got in jobs[:2]:
        pl.when(got)(copy.wait_recv)
    rim(xp, 0, 1)
    unfold(xp, xc.at[1], 1)
    correlate(xc.at[1], wv, acc, 1, True)
    for copy, _, got in jobs[2:]:
        pl.when(got)(copy.wait_recv)
    for view_row in (0, 2):
        rim(xp, 0, view_row)
        unfold(xp, xc.at[view_row], view_row)
        correlate(xc.at[view_row], wv, acc, view_row, False)
    for copy, sent, _ in jobs:
        pl.when(sent)(copy.wait_send)

    ccopy.wait()
    preact = shifted(acc[0], 1) + acc[1] + shifted(acc[2], -1)
    for s in range(S):
        upstream = jnp.swapaxes(cot_ref[0, :, s].astype(F32), 0, 1).reshape(T * V, C)
        pre = preact[s * T * V : (s + 1) * T * V]
        sigmoid = jax.nn.sigmoid(pre)
        grad = upstream * sigmoid * (1.0 + pre * (1.0 - sigmoid))
        gp[1, 1 + s, 1 : 1 + T, :, 0:C] = grad.astype(BF16).reshape(T, V, C)
    jobs = halo(gp, 1)
    grad = gp[1, 1 : 1 + S, 1 : 1 + T].reshape(CELLS, LANES)
    wide = grad.astype(F32)
    gall[:, 0:256] = shifted(wide, -1).astype(BF16)
    gall[:, 256:512] = grad
    gall[:, 512:768] = shifted(wide, 1).astype(BF16)

    firsts = (first_a, first_b, first_c)
    scatters = [
        Scatter(k, firsts[k], (got_a, got_b, got_c)[k], first_send.at[k], first_recv.at[k])
        for k in range(3)
    ]

    def exchange(a):
        units = pl.ds(81 * a, 81)
        return send_to(sibling(), dw.at[1 - core, :, units], pair.at[:, units], pair_sems, a)

    def both_cores(plane, start, count):
        units = pl.ds(start, count)
        return dw[core, plane, units] + pair[plane, units]

    def scatter(copy, a):
        copy.wait_recv()
        for plane in range(2):
            for target, at, start, count in pieces(plane):
                if ready(start, count) == a:
                    firsts[plane][target, at : at + count] = both_cores(plane, start, count)
            scatters[plane].start(a)
        chips = [q for q, (_, _, start, count) in enumerate(pieces(2)) if ready(start, count) == a]

        @pl.loop(chips[0], chips[-1] + 1)
        def _(q):
            at = pl.ds((q // 4) * 5, 5)
            first_c[q % 4, at] = both_cores(2, window(1, q, 5), 5)

        scatters[2].start(a)

    def input_terms(view_row, first):
        rim(gp, 1, view_row)
        unfold(gp, xc.at[view_row], view_row)
        correlate(xc.at[view_row], wt, acc, view_row, first)

    kernel_terms(xc, gall, dw, 0)
    pairs = [exchange(0)]
    for a in (1, 2):
        kernel_terms(xc, gall, dw, a)
        pairs.append(exchange(a))
        scatter(pairs[a - 1], a - 1)
    turn(54, 81)
    for copy, _, got in jobs[:2]:
        pl.when(got)(copy.wait_recv)
    input_terms(1, True)
    scatter(pairs[2], 2)
    for copy, _, got in jobs[2:]:
        pl.when(got)(copy.wait_recv)
    input_terms(0, False)

    for ring in scatters:
        ring.wait()
    sum_a[...] = scatters[0].total(pl.ds(0, 64))
    for x in range(4):
        sum_b[x] = scatters[1].total(pl.ds(18 * x, 18))

    @pl.loop(0, 16)
    def _(p):
        sum_c[p // 4, p % 4] = scatters[2].total(pl.ds(5 * p, 5))

    chips = (chip_x, chip_y, chip_z)
    column = chip_x * 4 + chip_y

    def next_part(plane, to):
        if plane == 0:
            return sum_a.at[pl.ds(window(4, chip_x * 4 + to, 18) - window(16, chip_x, 64), 18)]
        return (next_b if plane == 1 else sum_c).at[to]

    for x in range(4):
        for z in range(4):
            start = window(1, x * 16 + chip_y * 4 + z, 5) - window(4, x * 4 + chip_y, 18)
            next_b[z, x] = sum_b[x, pl.ds(start, 5)]
    sends = []
    for step in (2, 1, 3):
        for plane, axis in enumerate((1, 2, 0)):
            src = next_part(plane, lax.rem(chips[axis] + step, 4))
            dst = (near_a, near_b, near_c)[plane].at[step - 1]
            sends.append(send_to(peer_along(axis, step), src, dst, next_sems.at[plane], step - 1))

    input_terms(2, False)
    total = shifted(acc[0], 1) + acc[1] + shifted(acc[2], -1)
    for s in range(S):
        block = total[s * T * V : (s + 1) * T * V].reshape(T, V, C)
        gi_out[0, :, s] = jnp.swapaxes(block, 0, 1).astype(BF16)
    gcopy = pltpu.make_async_copy(gi_out, gi_ref, in_sems.at[2])
    gcopy.start()

    for copy in sends:
        copy.wait_recv()

    def near_total(plane, near):
        value = next_part(plane, chips[(1, 2, 0)[plane]])[...].astype(F32)
        for k in range(3):
            value += near[k].astype(F32)
        return value.astype(BF16)

    last_a[...] = near_total(0, near_a)
    last_b[...] = near_total(1, near_b)
    last_c[...] = near_total(2, near_c)

    def last_part(plane, to):
        if plane == 0:
            return last_a.at[pl.ds(window(1, column * 4 + to, 5) - window(4, column, 18), 5)]
        return (last_b if plane == 1 else last_c).at[to]

    lasts = []
    for step in (2, 1, 3):
        for plane, axis in enumerate((2, 0, 1)):
            src = last_part(plane, lax.rem(chips[axis] + step, 4))
            slot = 3 * plane + step - 1
            lasts.append(send_to(peer_along(axis, step), src, ends.at[slot], last_sems, slot))
    for copy, sent, _ in jobs:
        pl.when(sent)(copy.wait_send)
    for copy in (*pairs, *sends):
        copy.wait_send()
    for copy in lasts:
        copy.wait()
    for plane, axis in enumerate((2, 0, 1)):
        value = last_part(plane, chips[axis])[...].astype(F32)
        for k in range(3):
            value += ends[3 * plane + k].astype(F32)
        both[core, plane] = value
    gcopy.wait()
    send_to(sibling(), both.at[core], both.at[core], core_sems, 0).wait()

    for k in range(2):
        for unit in range(5):
            row = 64 * unit + 32 * k
            tail = both[k, 2, unit]
            left[row : row + 16] = both[k, 0, unit]
            left[row + 16 : row + 32] = both[k, 1, unit]
            right[row : row + 16] = tail
            right[row + 16 : row + 32] = pltpu.roll(tail, 64, 1)
    count = 160
    odd = pltpu.roll(left[pl.ds(1, count, stride=2), :], 64, 1)
    head = lax.broadcasted_iota(jnp.int32, (count, 128), 1) < 64
    gk_ref[pl.ds(0, count, stride=3), :] = left[pl.ds(0, count, stride=2), :]
    gk_ref[pl.ds(1, count, stride=3), :] = jnp.where(head, right[pl.ds(0, count, stride=2), :], odd)
    rest = pltpu.roll(right[pl.ds(1, count, stride=2), :], 64, 1)
    gk_ref[pl.ds(2, count, stride=3), :] = jnp.where(head, odd, rest)


def local(inputs, cotangent, kernel, moment_one, moment_two):
    vmem = pl.BlockSpec(memory_space=pltpu.VMEM)
    anywhere = pl.BlockSpec(memory_space=pl.ANY)
    padded = (3, S + 2, T + 2, V, LANES)
    tiles = lambda *lead: pltpu.VMEM((*lead, *TILE), BF16)
    dma = lambda *shape: pltpu.SemaphoreType.DMA(shape)
    long_kernel = pltpu.VMEM((ROWS + WIDE - GROUP, C), BF16)
    grad_input, window_grad = pl.pallas_call(
        step_kernel,
        out_shape=(
            jax.ShapeDtypeStruct(inputs.shape, BF16),
            jax.ShapeDtypeStruct((480, 128), F32),
        ),
        in_specs=[anywhere, anywhere, anywhere],
        out_specs=(anywhere, vmem),
        scratch_shapes=[
            *(pltpu.VMEM(inputs.shape, BF16) for _ in range(3)),
            pltpu.VMEM((2, 2, T, V, 384), BF16),
            pltpu.VMEM((2, 2, 2, V, 384), BF16),
            pltpu.VMEM((2, 2, 2, T, V, 384), BF16),
            pltpu.VMEM((2, 3, 2, 2, V, 384), BF16),
            pltpu.VMEM(padded, BF16),
            pltpu.VMEM(padded, BF16),
            pltpu.VMEM((3, CELLS, WIDE), BF16),
            long_kernel,
            long_kernel,
            pltpu.VMEM((3, CELLS, C), F32),
            pltpu.VMEM((CELLS, 768), BF16),
            tiles(2, 3, UNITS),
            tiles(3, UNITS),
            *(tiles(4, n) for n in LENGTHS),
            *(tiles(3, n) for n in LENGTHS),
            tiles(64),
            tiles(4, 18),
            tiles(4, 4, 5),
            tiles(4, 4, 5),
            tiles(3, 18),
            tiles(3, 4, 5),
            tiles(3, 4, 5),
            tiles(18),
            tiles(4, 5),
            tiles(4, 5),
            tiles(9, 5),
            pltpu.VMEM((2, 3, 5, *TILE), F32),
            pltpu.VMEM((320, 128), F32),
            pltpu.VMEM((320, 128), F32),
            dma(2, 8),
            dma(2, 8),
            dma(3),
            pltpu.SemaphoreType.DMA,
            dma(2, 3),
            dma(3, 4, 3),
            dma(3, 3, 3),
            dma(3, 2, 3),
            dma(2, 9),
            dma(2, 1),
        ],
        compiler_params=pltpu.CompilerParams(
            vmem_limit_bytes=56 * 1024 * 1024, collective_id=0, has_side_effects=True
        ),
        cost_estimate=pl.CostEstimate(flops=9 * 10**9, bytes_accessed=10**7, transcendentals=10**5),
    )(inputs, cotangent, kernel.reshape(ROWS, C))
    share_len = moment_one.shape[0]
    chip = lax.axis_index("ang") * 4 + lax.axis_index("sp") // 2
    begin = lax.axis_index(("ang", "sp")) * share_len - window(1, chip, 5) * (64 * C)
    share = lax.dynamic_slice_in_dim(window_grad.reshape(-1), begin, share_len, 0)
    pixels = CELLS * lax.axis_size("ang") * lax.axis_size("sp")
    grad_share = share * F32(1.0 / math.sqrt(pixels))
    moment_next = beta_one * moment_one + (1.0 - beta_one) * grad_share
    square_next = beta_two * moment_two + (1.0 - beta_two) * grad_share * grad_share
    first_fix = 1.0 - beta_one**adam_step
    second_fix = 1.0 - beta_two**adam_step
    direction = moment_next / first_fix / (jnp.sqrt(square_next / second_fix) + epsilon)
    return (grad_input, moment_next, square_next, direction)


def solution(mesh):
    field = P("ang", None, None, "sp", None)
    share = P(("ang", "sp"))
    return jax.shard_map(
        local,
        mesh=mesh,
        in_specs=(field, field, P(), share, share),
        out_specs=(field, share, share, share),
        check_vma=False,
    )
```
